32 devices in a mesh: cuts: 2 (over y), row: 4 (over z), vec: 4 (over x, core).
Axes of the slice: x: 2, y: 2, z: 4, core: 2. Of those that a mesh axis runs over, the one named last changes fastest.
Arguments:
- vectors: float32 [16384, 512], P(('cuts', 'row'), 'vec'), parts along dimension 0, may hold values from -6 to 6
- intersection: float32 [8192, 1536], P('row'), may hold values from -0.15625 to 0.15625
- factor: float32 [16384, 2048], P(('cuts', 'row')), parts along dimension 0, may hold values from -0.1875 to 0.1875
- pivot_rows: int32 [16384], P(('cuts', 'row')), parts along dimension 0, may hold values from 0 to 2047, as said below
- pivot_sizes: int32 [2048], P('cuts'), parts along dimension 0, may hold values from 1 to 2
- pivot_diag: float32 [4096], P('cuts'), parts along dimension 0, may hold values from 0.5 to 2
- pivot_off: float32 [2048], P('cuts'), parts along dimension 0, may hold values from 2.5 to 4
Outputs:
- partial_solve: float32 [16384, 512], P(('cuts', 'row'), 'vec'), parts along dimension 0
The draws below stay inside these ranges and needn't reach their ends.
There are 2 independent parts, one for each index of `cuts`. The reference program is written for one: setup_inputs(seed, part) draws one part's arguments, and reference() takes and returns one part's arrays. A program takes and returns all parts, laid end to end along the dimension named above; an argument that names none is the same for every part. Nothing has to cross between parts.
Inputs may be any that keep to these rules, and one draw needn't show every extreme that they name: `pivot_rows`: each aligned run of 2048 entries is a permutation of 0 to 2047. `pivot_sizes`: 2 marks a 2x2 pivot block on the pair of rows, 1 two 1x1 blocks.
All inputs are finite; a program needn't handle non-finite values.
Results may differ from the reference program's by a relative error of at most 0.00011.
Values sent between devices are 32-bit elements; how exact they have to be, the bound alone decides.
No kernel may reach another device: no remote copies, remote signals or barrier semaphores. Data moves between devices by JAX's collectives and lax.ppermute only.
A program may use at most 128 MiB of HBM per device.

```python
import math
import jax
import jax.numpy as jnp
from jax import lax

VECS = 512
BS = 512
PANEL = 1024
PANELS = 2
CYC = 16
ROWS_DEV = 2048
OWNERS = 4
ORDER = 8192
SOLVED = 2048


def one_device(subkey):
    return jax.random.permutation(subkey, ROWS_DEV)


def draw_pivot_rows(key, part):
    subkeys = jax.random.split(jax.random.fold_in(key, 7), ORDER // ROWS_DEV)
    orders = jax.vmap(one_device)(subkeys)
    return orders.reshape(ORDER).astype(jnp.int32)


def plant(values, stream_key, smallest, largest):
    place = [jax.random.randint(jax.random.fold_in(stream_key, axis), (), 0, length) for axis, length in enumerate(values.shape)]
    longest = values.shape.index(max(values.shape))
    next_to = place[:longest] + [(place[longest] + 1) % values.shape[longest]] + place[longest + 1:]
    return values.at[tuple(place)].set(smallest).at[tuple(next_to)].set(largest)


def block_scale(rng, extent, cuts, low, largest):
    loudness, own = 1.0, jax.random.fold_in(rng, 6)
    for position, blocks in cuts:
        draws = jnp.exp(jax.random.uniform(jax.random.fold_in(own, position), (blocks,), jnp.float32, low / len(cuts), largest / len(cuts)))
        loudness = loudness * jnp.repeat(draws, extent[position] // blocks).reshape([-1 if axis == position else 1 for axis in range(len(extent))])
    return loudness


def centred(stream_key, shape, spread, most, pieces=(), kind=jnp.bfloat16):
    values = jax.random.normal(stream_key, shape, jnp.float32) * spread
    if len(pieces) > 0:
        values = block_scale(stream_key, shape, pieces, -0.22, 0.18) * values
    return jnp.clip(values, min=-most, max=most).astype(kind)


def setup_inputs(seed: int = 0, part: int = 0) -> dict:
    seeds = jax.random.split(jax.random.key(seed), 8)
    part_splits = jax.random.split(jax.random.fold_in(seeds[7], part), 8)
    vectors = centred(part_splits[0], (ORDER, VECS), 1.0, 6.0, ((0, 4), (1, 4)), jnp.float32)
    intersection = centred(seeds[1], (ORDER, 3 * BS), (3 * BS) ** -0.5, 0.15625, ((0, 4),), jnp.float32)
    factor = centred(part_splits[2], (ORDER, SOLVED), (SOLVED // 2) ** -0.5, 0.1875, ((0, 4),), jnp.float32)
    pivot_rows = draw_pivot_rows(jax.random.fold_in(jax.random.fold_in(seeds[7], part), 71), part)
    pivot_sizes = plant(jax.random.randint(part_splits[4], (SOLVED // 2,), 1, 3), jax.random.fold_in(part_splits[4], 1), 1, 2).astype(jnp.int32)
    pivot_diag = jnp.clip(jnp.exp(jax.random.uniform(part_splits[5], (SOLVED,), jnp.float32, math.log(0.5), math.log(2.0))), 0.5, 2.0)
    pivot_off = jnp.clip(jax.random.uniform(part_splits[6], (SOLVED // 2,), jnp.float32, 2.5, 4.0), 2.5, 4.0)
    return {"vectors": vectors, "intersection": intersection, "factor": factor, "pivot_rows": pivot_rows, "pivot_sizes": pivot_sizes, "pivot_diag": pivot_diag, "pivot_off": pivot_off}


def layout_rows(positions):
    device = positions // ROWS_DEV
    within = positions % ROWS_DEV
    return ((within // CYC * OWNERS + device) * CYC + within % CYC).astype(jnp.int32)

def band_product(intersection, padded, blocks_here):
    band_width = intersection.shape[1] // 3
    band_rows = intersection.reshape(blocks_here, band_width, 3 * band_width)
    result = jnp.zeros((blocks_here, band_width, padded.shape[1]), jnp.float32)
    for offset in range(3):
        window = padded[offset * band_width:offset * band_width + blocks_here * band_width]
        window = window.reshape(blocks_here, band_width, padded.shape[1])
        result = result + jnp.einsum('kij,kjv->kiv', band_rows[:, :, offset * band_width:(offset + 1) * band_width], window, precision=lax.Precision.HIGHEST)
    return result.reshape(blocks_here * band_width, padded.shape[1])

def scale_pivots(values, sizes_here, diag_here, off_here):
    paired = values.reshape(-1, 2, values.shape[1])
    leading = paired[:, 0]
    trailing = paired[:, 1]
    diag_lead = diag_here[0::2][:, None]
    diag_next = diag_here[1::2][:, None]
    coupling = off_here[:, None]
    determ = diag_lead * diag_next - coupling * coupling
    is_pair = (sizes_here == 2)[:, None]
    new_lead = jnp.where(is_pair, (diag_next * leading - coupling * trailing) / determ, leading / diag_lead)
    new_next = jnp.where(is_pair, (diag_lead * trailing - coupling * leading) / determ, trailing / diag_next)
    return jnp.stack([new_lead, new_next], axis=1).reshape(values.shape)

def reference(vectors, intersection, factor, pivot_rows, pivot_sizes, pivot_diag, pivot_off):
    padded = jnp.pad(vectors, ((BS, BS), (0, 0)))
    product = band_product(intersection, padded, ORDER // BS)
    positions = jnp.arange(ORDER, dtype=jnp.int32)
    mapped = layout_rows(positions)
    source = layout_rows(positions // ROWS_DEV * ROWS_DEV + pivot_rows.astype(jnp.int32))
    rhs_fac = jnp.zeros_like(product).at[mapped].set(product[source])
    lower_fac = jnp.zeros((ORDER, SOLVED), jnp.float32).at[mapped].set(factor)
    solved = []
    for panel_num in range(PANELS):
        first_row = panel_num * PANEL
        last_row = first_row + PANEL
        block_sol = jax.scipy.linalg.solve_triangular(lower_fac[first_row:last_row, first_row:last_row], rhs_fac[first_row:last_row], lower=True, unit_diagonal=True)
        update = jnp.dot(lower_fac[last_row:, first_row:last_row], block_sol, precision=lax.Precision.HIGHEST)
        rhs_fac = jnp.concatenate([rhs_fac[:last_row], rhs_fac[last_row:] - update], axis=0)
        solved.append(scale_pivots(block_sol, pivot_sizes[first_row // 2:last_row // 2], pivot_diag[first_row:last_row], pivot_off[first_row // 2:last_row // 2]))
    combined = jnp.concatenate(solved + [rhs_fac[SOLVED:]], axis=0)
    return combined[mapped]
```

```python
import functools

import jax
import jax.numpy as jnp
from jax import lax
from jax.experimental import pallas as pl
from jax.experimental.pallas import tpu as pltpu
from jax.sharding import PartitionSpec as P

BS = 512
PANEL = 1024
PANELS = 2
CYC = 16
DIAG = 256
HALF = 128
VMEM_LIMIT = 40 * 1024 * 1024
F32 = jnp.float32
BF16 = jnp.bfloat16


def params():
    return pltpu.CompilerParams(vmem_limit_bytes=VMEM_LIMIT)


def cost(flops, moved):
    return pl.CostEstimate(flops=int(flops), bytes_accessed=int(moved), transcendentals=0)


def split(value):
    high = value.astype(BF16)
    low = (value - high.astype(F32)).astype(BF16)
    return high, low


def side_by_side(value):
    return jnp.concatenate(split(value), axis=1)


def dot(left, right):
    return jnp.dot(left, right, preferred_element_type=F32)


def fold(wide):
    width = wide.shape[1] // 2
    return wide[:, :width] + wide[:, width:]


def times(left, right_wide):
    high, low = split(left)
    return fold(dot(high, right_wide) + dot(low, right_wide))


def small_times(left_wide, right):
    wide = side_by_side(right)
    return fold(dot(left_wide, jnp.concatenate([wide, wide], axis=0)))


def band_kernel(inner, tiles, owners, me_ref, inter_ref, vec_ref, *rest):
    if inner:
        outs, (wide_ref, stage_ref) = rest[:owners], rest[owners:]
    else:
        before_ref, after_ref = rest[:2]
        outs, (wide_ref, stage_ref) = rest[2 : 2 + owners], rest[2 + owners :]
    block, tile = pl.program_id(0), pl.program_id(1)
    rows = vec_ref.shape[0]

    @pl.when((block == 0) & (tile == 0))
    def _():
        if inner:
            wide_ref[...] = side_by_side(vec_ref[...])
        else:
            wide_ref[:BS] = side_by_side(before_ref[...])
            wide_ref[BS : 3 * BS] = side_by_side(vec_ref[: 2 * BS])
            wide_ref[3 * BS : 5 * BS] = side_by_side(vec_ref[rows - 2 * BS :])
            wide_ref[5 * BS :] = side_by_side(after_ref[...])

    start = block * BS if inner else block * (3 * BS)
    window = wide_ref[pl.ds(pl.multiple_of(start, BS), 3 * BS)]
    product = times(inter_ref[...], window)
    groups = product.shape[0] // (owners * CYC)
    stage_ref[...] = product.reshape(groups, owners, CYC, product.shape[1])
    me = me_ref[0]
    for k in range(owners):
        outs[k][...] = stage_ref[:, me ^ k].reshape(groups * CYC, product.shape[1])


def band_part(inner, place, intersection, vectors, halo, owners):
    rows, columns = vectors.shape
    width = intersection.shape[1]
    blocks = rows // BS
    tile_rows = BS // 2
    tiles = BS // tile_rows
    count = blocks - 2 if inner else 2
    if inner:
        inter_map = lambda b, t, s: ((b + 1) * tiles + t, 0)
    else:
        inter_map = lambda b, t, s: (b * (blocks - 1) * tiles + t, 0)
    whole = lambda b, t, s: (0, 0)
    slot_rows = tile_rows // owners
    in_specs = [pl.BlockSpec((tile_rows, width), inter_map), pl.BlockSpec((rows, columns), whole)]
    in_specs += [pl.BlockSpec((BS, columns), whole)] * len(halo)
    out_map = lambda b, t, s: (b * tiles + t, 0)
    return pl.pallas_call(
        functools.partial(band_kernel, inner, tiles, owners),
        out_shape=[jax.ShapeDtypeStruct((count * BS // owners, columns), F32)] * owners,
        grid_spec=pltpu.PrefetchScalarGridSpec(
            num_scalar_prefetch=1,
            grid=(count, tiles),
            in_specs=in_specs,
            out_specs=[pl.BlockSpec((slot_rows, columns), out_map)] * owners,
            scratch_shapes=[
                pltpu.VMEM((rows if inner else 6 * BS, 2 * columns), BF16),
                pltpu.VMEM((slot_rows // CYC, owners, CYC, columns), F32),
            ],
        ),
        compiler_params=params(),
        cost_estimate=cost(8 * count * BS * width * columns, 4 * count * BS * width),
        name="band_inner" if inner else "band_outer",
    )(place, intersection, vectors, *halo)


def share_kernel(groups, parts, place_ref, *refs):
    ins, outs = refs[: PANELS * groups], refs[PANELS * groups :]
    for panel in range(PANELS):
        at = 0
        for k in range(groups):
            for j in range(k + 1):
                outs[panel][at] = ins[panel * groups + k][:, j * DIAG : (j + 1) * DIAG]
                at += 1


def own_shares(place, factor, slots, shares):
    groups = PANEL // DIAG
    blocks = groups * (groups + 1) // 2

    def spec(panel, k):
        return pl.BlockSpec((CYC, PANEL), lambda i, s: (panel * slots + k * shares + s[1], panel))

    return pl.pallas_call(
        functools.partial(share_kernel, groups, shares),
        out_shape=[jax.ShapeDtypeStruct((blocks, CYC, DIAG), F32)] * PANELS,
        grid_spec=pltpu.PrefetchScalarGridSpec(
            num_scalar_prefetch=1,
            grid=(1,),
            in_specs=[spec(panel, k) for panel in range(PANELS) for k in range(groups)],
            out_specs=[pl.BlockSpec((blocks, CYC, DIAG), lambda i, s: (0, 0, 0))] * PANELS,
        ),
        compiler_params=params(),
        name="own_shares",
    )(place, *([factor] * (PANELS * groups)))


def invert_kernel(owners, shares, place_ref, own_ref, *refs):
    direct = refs[: owners - 1]
    crossed = refs[owners - 1 : owners + 2]
    high_ref, low_ref, inv_high_ref, inv_low_ref, tri_ref = refs[owners + 2 :]
    groups = PANEL // DIAG
    me, part = place_ref[0], place_ref[1]
    for k in range(groups):
        reach = (k + 1) * DIAG
        for s in range(shares):
            row = (k * shares + s) * CYC
            tri_ref[(k * shares + s) * owners + me, :, :reach] = own_ref[row : row + CYC, :reach]
    for other in range(1, owners):
        owner = me ^ other
        for turn in range(shares):
            at = 0
            for k in range(groups):
                for j in range(k + 1):
                    if turn == 0:
                        piece = direct[other - 1][at]
                    else:
                        piece = crossed[turn - 1][other - 1, at]
                    to = (k * shares + (part ^ turn)) * owners + owner
                    tri_ref[to, :, j * DIAG : (j + 1) * DIAG] = piece
                    at += 1

    def block(row, column, size):
        part_rows = tri_ref[row // CYC : (row + size) // CYC, :, column : column + size]
        return part_rows.reshape(size, size)

    for k in range(1, groups):
        rows = slice(k * DIAG, (k + 1) * DIAG)
        left = tri_ref[rows.start // CYC : rows.stop // CYC, :, : k * DIAG].reshape(DIAG, k * DIAG)
        high_ref[rows, : k * DIAG], low_ref[rows, : k * DIAG] = split(left)

    down = lax.broadcasted_iota(jnp.int32, (HALF, HALF), 0)
    along = lax.broadcasted_iota(jnp.int32, (HALF, HALF), 1)
    eye = jnp.where(down == along, 1.0, 0.0).astype(F32)

    def below(size):
        return (down // size == along // size + 1) & ((down // size) % 2 == 1)

    count = PANEL // HALF
    diagonal = [block(i * HALF, i * HALF, HALF) for i in range(count)]
    wides = [side_by_side(d) for d in diagonal]
    inverse = [eye - jnp.where(below(1), d, 0.0) for d in diagonal]
    size = 2
    while size < HALF:
        keep = jnp.where(below(size), 1.0, 0.0).astype(BF16)
        keep = jnp.concatenate([keep, keep], axis=1)
        right = [small_times(wides[i] * keep, inverse[i]) for i in range(count)]
        inverse = [inverse[i] - small_times(side_by_side(inverse[i]), right[i]) for i in range(count)]
        size *= 2
    for k in range(groups):
        first, second = inverse[2 * k], inverse[2 * k + 1]
        corner = block(k * DIAG + HALF, k * DIAG, HALF)
        right = small_times(side_by_side(corner), first)
        corner = -small_times(side_by_side(second), right)
        empty = jnp.zeros((HALF, HALF), F32)
        whole = jnp.concatenate(
            [jnp.concatenate([first, empty], axis=1), jnp.concatenate([corner, second], axis=1)], axis=0
        )
        inv_high_ref[k], inv_low_ref[k] = split(whole)


def invert_panel(panel, place, factor, direct, crossed, owners, shares, panel_rows):
    groups = PANEL // DIAG
    full = lambda shape: pl.BlockSpec(shape, lambda i, s: (0,) * len(shape))
    out_shape = [
        jax.ShapeDtypeStruct((PANEL, PANEL), BF16),
        jax.ShapeDtypeStruct((PANEL, PANEL), BF16),
        jax.ShapeDtypeStruct((groups, DIAG, DIAG), BF16),
        jax.ShapeDtypeStruct((groups, DIAG, DIAG), BF16),
    ]
    return pl.pallas_call(
        functools.partial(invert_kernel, owners, shares),
        out_shape=out_shape,
        grid_spec=pltpu.PrefetchScalarGridSpec(
            num_scalar_prefetch=1,
            grid=(1,),
            in_specs=[pl.BlockSpec((panel_rows, PANEL), lambda i, s: (panel, panel))]
            + [full(a.shape) for a in (*direct, *crossed)],
            out_specs=[full(s.shape) for s in out_shape],
            scratch_shapes=[pltpu.VMEM((PANEL // CYC, CYC, PANEL), F32)],
        ),
        compiler_params=params(),
        cost_estimate=cost(2**30, 12 * 2**20),
        name="invert_panel",
    )(place, factor, *direct, *crossed)


def order_kernel(owners, panel_rows, place_ref, pivot_ref, *refs):
    inner, outer = refs[:owners], refs[owners : 2 * owners]
    grouped_ref, first_ref, second_ref = refs[2 * owners :]
    me = place_ref[0]
    edge = outer[0].shape[0] // 2
    middle = inner[0].shape[0]
    chunk = 2 * edge + middle
    for k in range(owners):
        start = (me ^ k) * chunk
        grouped_ref[pl.ds(pl.multiple_of(start, CYC), edge)] = outer[k][:edge]
        grouped_ref[pl.ds(pl.multiple_of(start + edge, CYC), middle)] = inner[k][...]
        grouped_ref[pl.ds(pl.multiple_of(start + edge + middle, CYC), edge)] = outer[k][edge:]
    pick_rows(pivot_ref, 0, grouped_ref, first_ref)
    pick_rows(pivot_ref, panel_rows, grouped_ref, second_ref)


def pick_rows(pivot_ref, first, source_ref, target_ref):
    step = 8

    def body(i, _):
        base = i * step
        rows = [source_ref[pl.ds(pivot_ref[first + base + j], 1)] for j in range(step)]
        target_ref[pl.ds(pl.multiple_of(base, step), step)] = jnp.concatenate(rows, axis=0)
        return 0

    lax.fori_loop(0, target_ref.shape[0] // step, body, 0, unroll=4)


def order_rows(place, pivot_rows, inner, outer, panel_rows):
    owners = len(inner)
    columns = inner[0].shape[1]
    rows = pivot_rows.shape[0]
    full = lambda shape: pl.BlockSpec(shape, lambda i, s, p: (0, 0))
    out_shape = [jax.ShapeDtypeStruct((n, columns), F32) for n in (rows, panel_rows, panel_rows)]
    return pl.pallas_call(
        functools.partial(order_kernel, owners, panel_rows),
        out_shape=out_shape,
        grid_spec=pltpu.PrefetchScalarGridSpec(
            num_scalar_prefetch=2,
            grid=(1,),
            in_specs=[full(a.shape) for a in (*inner, *outer)],
            out_specs=[full(s.shape) for s in out_shape],
        ),
        compiler_params=params(),
        name="order_rows",
    )(place, pivot_rows, *inner, *outer)


def solve_into(me, owners, pieces, high_ref, low_ref, inv_high_ref, inv_low_ref, rhs_ref, wide_ref, y_ref):
    slots = pieces[0].shape[0] // CYC
    columns = pieces[0].shape[1]
    for k in range(owners):
        for s in range(slots):
            rhs_ref[s * owners + (me ^ k)] = pieces[k][s * CYC : (s + 1) * CYC]
    for k in range(PANEL // DIAG):
        rows = slice(k * DIAG, (k + 1) * DIAG)
        rhs = rhs_ref[rows.start // CYC : rows.stop // CYC].reshape(DIAG, columns)
        if k:
            done = wide_ref[: k * DIAG]
            known = dot(high_ref[rows, : k * DIAG], done) + dot(low_ref[rows, : k * DIAG], done)
            rhs = rhs - fold(known)
        wide = side_by_side(rhs)
        block = fold(dot(inv_high_ref[k], wide) + dot(inv_low_ref[k], wide))
        wide_ref[rows] = side_by_side(block)
        y_ref[rows.start // CYC : rows.stop // CYC] = block.reshape(DIAG // CYC, CYC, columns)


def first_kernel(owners, place_ref, *refs):
    pieces = refs[:owners]
    high, low, inv_high, inv_low, factor_ref, current_ref = refs[owners : owners + 6]
    y_ref, next_ref, rhs_ref, wide_ref = refs[owners + 6 :]
    solve_into(place_ref[0], owners, pieces, high, low, inv_high, inv_low, rhs_ref, wide_ref, y_ref)
    next_ref[...] = current_ref[...] - times(factor_ref[...], wide_ref[...])


def first_solve(place, pieces, prepared, factor, current, panel_rows):
    owners = len(pieces)
    columns = current.shape[1]
    full = lambda shape: pl.BlockSpec(shape, lambda i, s: (0,) * len(shape))
    out_shape = [
        jax.ShapeDtypeStruct((PANEL // CYC, CYC, columns), F32),
        jax.ShapeDtypeStruct((panel_rows, columns), F32),
    ]
    return pl.pallas_call(
        functools.partial(first_kernel, owners),
        out_shape=out_shape,
        grid_spec=pltpu.PrefetchScalarGridSpec(
            num_scalar_prefetch=1,
            grid=(1,),
            in_specs=[full(a.shape) for a in (*pieces, *prepared)]
            + [pl.BlockSpec((panel_rows, PANEL), lambda i, s: (1, 0)), full(current.shape)],
            out_specs=[full(s.shape) for s in out_shape],
            scratch_shapes=[
                pltpu.VMEM((PANEL // CYC, CYC, columns), F32),
                pltpu.VMEM((PANEL, 2 * columns), BF16),
            ],
        ),
        compiler_params=params(),
        cost_estimate=cost(8 * PANEL * PANEL * columns, 6 * 2**20),
        name="first_solve",
    )(place, *pieces, *prepared, factor, current)


def middle_kernel(pivot_ref, grouped_ref, y_ref, factor_ref, out_ref, wide_ref, picked_ref):
    tile = pl.program_id(0)

    @pl.when(tile == 0)
    def _():
        wide_ref[...] = side_by_side(y_ref[...].reshape(PANEL, y_ref.shape[2]))

    pick_rows(pivot_ref, (tile + 1) * out_ref.shape[0], grouped_ref, picked_ref)
    out_ref[...] = picked_ref[...] - times(factor_ref[...], wide_ref[...])


def middle_update(pivot_rows, grouped, y, factor, tile_rows):
    rows, columns = grouped.shape
    full = lambda shape: pl.BlockSpec(shape, lambda i, p: (0,) * len(shape))
    tiles = rows // tile_rows - 1
    return pl.pallas_call(
        middle_kernel,
        out_shape=jax.ShapeDtypeStruct((tiles * tile_rows, columns), F32),
        grid_spec=pltpu.PrefetchScalarGridSpec(
            num_scalar_prefetch=1,
            grid=(tiles,),
            in_specs=[
                full(grouped.shape),
                full(y.shape),
                pl.BlockSpec((tile_rows, PANEL), lambda i, p: (i + 1, 0)),
            ],
            out_specs=pl.BlockSpec((tile_rows, columns), lambda i, p: (i, 0)),
            scratch_shapes=[
                pltpu.VMEM((PANEL, 2 * columns), BF16),
                pltpu.VMEM((tile_rows, columns), F32),
            ],
        ),
        compiler_params=params(),
        cost_estimate=cost(8 * tiles * tile_rows * PANEL * columns, 8 * 2**20),
        name="middle_update",
    )(pivot_rows, grouped, y, factor)


def last_kernel(owners, place_ref, *refs):
    pieces = refs[:owners]
    high, low, inv_high, inv_low, y_ref, keep_ref, swap_ref, rest_ref, factor_ref = refs[owners : owners + 9]
    out_ref, rhs_ref, wide_ref, second_ref = refs[owners + 9 :]
    tile = pl.program_id(0)
    columns = out_ref.shape[1]

    @pl.when(tile == 0)
    def _():
        me = place_ref[0]
        solve_into(me, owners, pieces, high, low, inv_high, inv_low, rhs_ref, wide_ref, second_ref)
        slots = pieces[0].shape[0] // CYC
        for panel, source in enumerate((y_ref, second_ref)):
            for s in range(slots):
                at = (panel * slots + s) * CYC
                rows = source[s * owners + me]
                odd = lax.broadcasted_iota(jnp.int32, rows.shape, 0) % 2 == 1
                other = jnp.where(odd, pltpu.roll(rows, 1, 0), pltpu.roll(rows, CYC - 1, 0))
                keep = keep_ref[at : at + CYC]
                swap = swap_ref[at : at + CYC]
                mixed = keep * rows + jnp.where(swap != 0, swap * other, 0.0)
                out_ref[at : at + CYC] = mixed

    @pl.when(tile > 0)
    def _():
        out_ref[...] = rest_ref[...] - times(factor_ref[...], wide_ref[...])


def last_solve(place, pieces, prepared, y, keep, swap, rest, factor, tile_rows):
    owners = len(pieces)
    columns = rest.shape[1]
    rows = rest.shape[0] + tile_rows
    full = lambda shape: pl.BlockSpec(shape, lambda i, s: (0,) * len(shape))
    return pl.pallas_call(
        functools.partial(last_kernel, owners),
        out_shape=jax.ShapeDtypeStruct((rows, columns), F32),
        grid_spec=pltpu.PrefetchScalarGridSpec(
            num_scalar_prefetch=1,
            grid=(rows // tile_rows,),
            in_specs=[full(a.shape) for a in (*pieces, *prepared, y, keep, swap)]
            + [
                pl.BlockSpec((tile_rows, columns), lambda i, s: (jnp.maximum(i, 1) - 1, 0)),
                pl.BlockSpec((tile_rows, PANEL), lambda i, s: (jnp.maximum(i, 1), 1)),
            ],
            out_specs=pl.BlockSpec((tile_rows, columns), lambda i, s: (i, 0)),
            scratch_shapes=[
                pltpu.VMEM((PANEL // CYC, CYC, columns), F32),
                pltpu.VMEM((PANEL, 2 * columns), BF16),
                pltpu.VMEM((PANEL // CYC, CYC, columns), F32),
            ],
        ),
        compiler_params=params(),
        cost_estimate=cost(8 * rows * PANEL * columns, 12 * 2**20),
        name="last_solve",
    )(place, *pieces, *prepared, y, keep, swap, rest, factor)


def swap_with(value, axis, distance):
    size = lax.axis_size(axis)
    return lax.ppermute(value, axis, [(i, i ^ distance) for i in range(size)])


def from_all(value, axis):
    return [value] + [swap_with(value, axis, k) for k in range(1, lax.axis_size(axis))]


def halo_rows(vectors):
    devices, rows = lax.axis_size("row"), vectors.shape[0]
    up = [(i, i + 1) for i in range(devices - 1)]
    down = [(j, i) for i, j in up]
    return lax.ppermute(vectors[rows - BS :], "row", up), lax.ppermute(vectors[:BS], "row", down)


def pivot_weights(sizes, diag, off, device, owners):
    pairs = diag.reshape(-1, 2)
    determ = pairs[:, 0] * pairs[:, 1] - off * off
    is_pair = (sizes == 2)[:, None]
    keep = jnp.where(is_pair, pairs[:, ::-1] / determ[:, None], 1.0 / pairs)
    swap = jnp.where(is_pair, jnp.broadcast_to((-off / determ)[:, None], pairs.shape), 0.0)

    def own(value):
        value = value.reshape(-1, owners, CYC)
        return lax.dynamic_slice_in_dim(value, device, 1, 1).reshape(-1, 1)

    return own(keep), own(swap)


def local(vectors, intersection, factor, pivot_rows, pivot_sizes, pivot_diag, pivot_off):
    owners, shares = lax.axis_size("row"), lax.axis_size("vec")
    device, part = lax.axis_index("row"), lax.axis_index("vec")
    slots = PANEL // owners // CYC
    panel_rows = slots * CYC
    place = jnp.stack([device, part]).astype(jnp.int32)

    halo = halo_rows(vectors)
    share = own_shares(place, factor, slots, shares)

    def prepare(panel):
        direct = from_all(share[panel], "row")[1:]
        stacked = jnp.stack(direct)
        crossed_x = swap_with(stacked, "vec", 2)
        crossed = (swap_with(stacked, "vec", 1), crossed_x, swap_with(crossed_x, "vec", 1))
        return invert_panel(panel, place, factor, direct, crossed, owners, shares, panel_rows)

    prepared = [prepare(panel) for panel in range(PANELS)]
    inner = band_part(True, place, intersection, vectors, (), owners)
    inner = [inner[0]] + [swap_with(inner[k], "row", k) for k in range(1, owners)]
    outer = band_part(False, place, intersection, vectors, halo, owners)
    outer = [outer[0]] + [swap_with(outer[k], "row", k) for k in range(1, owners)]
    grouped, first, second = order_rows(place, pivot_rows, inner, outer, panel_rows)
    y, second = first_solve(place, from_all(first, "row"), prepared[0], factor, second, panel_rows)
    pieces = from_all(second, "row")
    tile_rows = PANELS * panel_rows
    rest = middle_update(pivot_rows, grouped, y, factor, tile_rows)
    keep, swap = pivot_weights(pivot_sizes, pivot_diag, pivot_off, device, owners)
    return last_solve(place, pieces, prepared[1], y, keep, swap, rest, factor, tile_rows)


def padded_2(shard, sides, width):
    for axis, dim in sides:
        devices, length = (lax.axis_size(axis), shard.shape[dim])
        up = [(i, (i + 1) % devices) for i in range(devices - 1)]
        down = [(j, i) for i, j in up]
        last = lax.slice_in_dim(shard, length - width, length, axis=dim)
        leading = lax.slice_in_dim(shard, 0, width, axis=dim)
        before = lax.ppermute(last, axis, up)
        after = lax.ppermute(leading, axis, down)
        shard = jnp.concatenate([before, shard, after], axis=dim)
    return shard


def band_product(intersection, padded, blocks_here):
    band_width = intersection.shape[1] // 3
    band_rows = intersection.reshape(blocks_here, band_width, 3 * band_width)
    result = jnp.zeros((blocks_here, band_width, padded.shape[1]), jnp.float32)
    for offset in range(3):
        window = padded[offset * band_width : offset * band_width + blocks_here * band_width]
        window = window.reshape(blocks_here, band_width, padded.shape[1])
        result = result + jnp.einsum(
            "kij,kjv->kiv",
            band_rows[:, :, offset * band_width : (offset + 1) * band_width],
            window,
            precision=lax.Precision.HIGHEST,
        )
    return result.reshape(blocks_here * band_width, padded.shape[1])


def scale_pivots(values, sizes_here, diag_here, off_here):
    paired = values.reshape(-1, 2, values.shape[1])
    leading = paired[:, 0]
    trailing = paired[:, 1]
    diag_lead = diag_here[0::2][:, None]
    diag_next = diag_here[1::2][:, None]
    coupling = off_here[:, None]
    determ = diag_lead * diag_next - coupling * coupling
    is_pair = (sizes_here == 2)[:, None]
    new_lead = jnp.where(
        is_pair, (diag_next * leading - coupling * trailing) / determ, leading / diag_lead
    )
    new_next = jnp.where(
        is_pair, (diag_lead * trailing - coupling * leading) / determ, trailing / diag_next
    )
    return jnp.stack([new_lead, new_next], axis=1).reshape(values.shape)


def local_many(vectors, intersection, factor, pivot_rows, pivot_sizes, pivot_diag, pivot_off):
    owners = lax.axis_size("row")
    device = lax.axis_index("row")
    rows_here = vectors.shape[0]
    columns = vectors.shape[1]
    slot_count = PANEL // owners // CYC
    panel_rows = slot_count * CYC
    triangles = []
    quarter = PANEL // lax.axis_size("vec")
    column_idx = lax.axis_index("vec")
    for panel_num in range(PANELS):
        local_rows = factor[panel_num * panel_rows : (panel_num + 1) * panel_rows]
        column_part = lax.dynamic_slice_in_dim(
            local_rows, panel_num * PANEL + column_idx * quarter, quarter, 1
        )
        column_part = column_part.reshape(slot_count, 1, CYC, quarter)
        gathered = lax.all_gather(column_part, "row", axis=1, tiled=True)
        triangles.append(lax.all_gather(gathered, "vec", axis=3, tiled=True).reshape(PANEL, PANEL))
    padded = padded_2(vectors, (("row", 0),), BS)
    product = band_product(intersection, padded, rows_here // BS)
    grouped = product.reshape(rows_here // (CYC * owners), owners, CYC, columns)
    regrouped = lax.all_to_all(grouped, "row", split_axis=1, concat_axis=0, tiled=True).reshape(
        rows_here, columns
    )
    current = jnp.take(regrouped, pivot_rows, axis=0)
    outputs = []
    for panel_num in range(PANELS):
        row_first = panel_num * panel_rows
        row_end = row_first + panel_rows
        col_first = panel_num * PANEL
        col_end = col_first + PANEL
        rhs_local = current[row_first:row_end].reshape(slot_count, 1, CYC, columns)
        rhs_all = lax.all_gather(rhs_local, "row", axis=1, tiled=True)
        triangle = triangles[panel_num]
        block_sol = jax.scipy.linalg.solve_triangular(
            triangle, rhs_all.reshape(PANEL, columns), lower=True, unit_diagonal=True
        )
        update = jnp.dot(
            factor[row_end:, col_first:col_end], block_sol, precision=lax.Precision.HIGHEST
        )
        current = jnp.concatenate([current[:row_end], current[row_end:] - update], axis=0)
        scaled = scale_pivots(
            block_sol,
            pivot_sizes[col_first // 2 : col_end // 2],
            pivot_diag[col_first:col_end],
            pivot_off[col_first // 2 : col_end // 2],
        )
        own_rows = lax.dynamic_slice_in_dim(
            scaled.reshape(slot_count, owners, CYC, columns), device, 1, 1
        )
        outputs.append(own_rows.reshape(panel_rows, columns))
    outputs.append(current[PANELS * panel_rows :])
    return jnp.concatenate(outputs, axis=0)


def solution(mesh):
    in_specs = (
        P(("cuts", "row"), "vec"),
        P("row", None),
        P(("cuts", "row"), None),
        P(("cuts", "row")),
        P("cuts"),
        P("cuts"),
        P("cuts"),
    )
    out_specs = P(("cuts", "row"), "vec")
    owners, shares = mesh.shape["row"], mesh.shape["vec"]
    few = owners == 4 and shares == 4 and DIAG == owners * shares * CYC
    body = local if few else local_many
    return jax.shard_map(body, mesh=mesh, in_specs=in_specs, out_specs=out_specs, check_vma=False)
```

```python
import functools

import jax
import jax.numpy as jnp
from jax import lax
from jax.experimental import pallas as pl
from jax.experimental.pallas import tpu as pltpu
from jax.sharding import PartitionSpec as P

BS = 512
PANEL = 1024
PANELS = 2
CYC = 16
DIAG = 256
HALF = 128
MIB = 1024 * 1024
HEAVY = 2**37
LIGHT = 2**30
F32 = jnp.float32
BF16 = jnp.bfloat16


def params(mib):
    return pltpu.CompilerParams(vmem_limit_bytes=mib * MIB)


IN_VMEM = pl.BlockSpec(memory_space=pltpu.VMEM)
IN_SMEM = pl.BlockSpec(memory_space=pltpu.SMEM)
IN_HBM = pl.BlockSpec(memory_space=pltpu.HBM)


def shaped(*shape, dtype=F32):
    return jax.ShapeDtypeStruct(shape, dtype)


def cost(flops, moved):
    return pl.CostEstimate(flops=int(flops), bytes_accessed=int(moved), transcendentals=0)


def split(value):
    high = value.astype(BF16)
    low = (value - high.astype(F32)).astype(BF16)
    return high, low


def side_by_side(value):
    return jnp.concatenate(split(value), axis=1)


def dot(left, right):
    return jnp.dot(left, right, preferred_element_type=F32)


def fold(wide):
    width = wide.shape[1] // 2
    return wide[:, :width] + wide[:, width:]


def times(left, right_wide):
    high, low = split(left)
    return parts_times(high, low, right_wide)


def parts_times(high, low, right_wide):
    return fold(dot(high, right_wide)) + dot(low, right_wide[:, : right_wide.shape[1] // 2])


def small_times(left_wide, right):
    wide = side_by_side(right)
    return fold(dot(left_wide, jnp.concatenate([wide, wide], axis=0)))


def start_kernel(slots, shares, place_ref, factor_ref, vec_ref, *refs):
    share_ref, first_ref, last_ref, sems = refs
    groups = PANEL // DIAG
    part = place_ref[1]
    rows = vec_ref.shape[0]
    copies = [(vec_ref.at[pl.ds(rows - BS, BS)], last_ref), (vec_ref.at[pl.ds(0, BS)], first_ref)]
    for panel in range(PANELS):
        at = 0
        for k in range(groups):
            row = pl.multiple_of((panel * slots + k * shares + part) * CYC, CYC)
            for j in range(k + 1):
                source = factor_ref.at[pl.ds(row, CYC), pl.ds(panel * PANEL + j * DIAG, DIAG)]
                copies.append((source, share_ref.at[panel, at]))
                at += 1
    started = [pltpu.make_async_copy(a, b, sems.at[i]) for i, (a, b) in enumerate(copies)]
    for copy in started:
        copy.start()
    for copy in started:
        copy.wait()


def first_sends(place, factor, vectors, slots, shares):
    groups = PANEL // DIAG
    blocks = groups * (groups + 1) // 2
    edge = shaped(BS, vectors.shape[1])
    return pl.pallas_call(
        functools.partial(start_kernel, slots, shares),
        out_shape=[shaped(PANELS, blocks, CYC, DIAG), edge, edge],
        in_specs=[IN_SMEM, IN_HBM, IN_HBM],
        out_specs=[IN_VMEM] * 3,
        scratch_shapes=[pltpu.SemaphoreType.DMA((PANELS * blocks + 2,))],
        compiler_params=params(4),
        cost_estimate=cost(0, 4 * MIB),
        name="first_sends",
    )(place, factor, vectors)


def band_kernel(inter_ref, vec_ref, before_ref, after_ref, out_ref, wide_ref):
    tile = pl.program_id(0)
    rows = vec_ref.shape[0]
    tile_rows = inter_ref.shape[0]
    owners = out_ref.shape[0]

    @pl.when(tile == 0)
    def _():
        wide_ref[:BS] = side_by_side(before_ref[...])
        wide_ref[BS : BS + rows] = side_by_side(vec_ref[...])
        wide_ref[BS + rows :] = side_by_side(after_ref[...])

    window = wide_ref[pl.ds(pl.multiple_of(tile * BS, BS), 3 * BS)]
    product = times(inter_ref[...], window)
    groups = tile_rows // (owners * CYC)
    for g in range(groups):
        for owner in range(owners):
            first = (g * owners + owner) * CYC
            out_ref[owner, g * CYC : (g + 1) * CYC] = product[first : first + CYC]


def band_product_split(intersection, vectors, halo, owners):
    rows, columns = vectors.shape
    width = intersection.shape[1]
    tile_rows = BS
    slot_rows = tile_rows // owners
    whole = lambda t: (0, 0)
    return pl.pallas_call(
        band_kernel,
        out_shape=shaped(owners, rows // owners, columns),
        grid=(rows // tile_rows,),
        in_specs=[
            pl.BlockSpec((tile_rows, width), lambda t: (t, 0)),
            pl.BlockSpec((rows, columns), whole),
            pl.BlockSpec((BS, columns), whole),
            pl.BlockSpec((BS, columns), whole),
        ],
        out_specs=pl.BlockSpec((owners, slot_rows, columns), lambda t: (0, t, 0)),
        scratch_shapes=[pltpu.VMEM((rows + 2 * BS, 2 * columns), BF16)],
        compiler_params=params(16),
        cost_estimate=cost(8 * rows * width * columns, 4 * rows * width),
        name="band_product_split",
    )(intersection, vectors, *halo)


def stack_kernel(panel, count, *refs):
    for k in range(count):
        refs[-1][k] = refs[k][panel]


def stack(panel, pieces, after):
    count = len(pieces)
    return pl.pallas_call(
        functools.partial(stack_kernel, panel, count),
        out_shape=shaped(count, *pieces[0].shape[1:]),
        in_specs=[IN_VMEM] * count + [pl.BlockSpec(memory_space=pl.ANY)],
        out_specs=IN_VMEM,
        compiler_params=params(4),
        name="stack",
    )(*pieces, after)


def pair_kernel(first_ref, second_ref, *refs):
    out_ref = refs[-1]
    out_ref[0] = first_ref[...]
    out_ref[1] = second_ref[...]


def pair(first, second, after):
    return pl.pallas_call(
        pair_kernel,
        out_shape=shaped(2, *first.shape),
        in_specs=[IN_VMEM] * 2 + [pl.BlockSpec(memory_space=pl.ANY)] * len(after),
        out_specs=IN_VMEM,
        compiler_params=params(4),
        name="pair",
    )(first, second, *after)


def invert_kernel(panel, owners, shares, place_ref, after_ref, factor_ref, *refs):
    mine_ref, theirs_ref, high_ref, low_ref, inv_high_ref, inv_low_ref, own_ref, tri_ref, sem = refs
    groups = PANEL // DIAG
    me, part = place_ref[0], place_ref[1]
    rows = own_ref.shape[0]
    copy = pltpu.make_async_copy(
        factor_ref.at[pl.ds(panel * rows, rows), pl.ds(panel * PANEL, PANEL)], own_ref, sem
    )
    copy.start()
    for other in range(1, owners):
        owner = me ^ other
        for turn in range(shares):
            at = 0
            for k in range(groups):
                for j in range(k + 1):
                    source = theirs_ref if turn % 2 else mine_ref
                    piece = source[turn // 2, other - 1, at]
                    to = (k * shares + (part ^ turn)) * owners + owner
                    tri_ref[to, :, j * DIAG : (j + 1) * DIAG] = piece
                    at += 1
    copy.wait()
    for k in range(groups):
        reach = (k + 1) * DIAG
        for s in range(shares):
            row = (k * shares + s) * CYC
            tri_ref[(k * shares + s) * owners + me, :, :reach] = own_ref[row : row + CYC, :reach]

    def block(row, column, size):
        part_rows = tri_ref[row // CYC : (row + size) // CYC, :, column : column + size]
        return part_rows.reshape(size, size)

    for k in range(1, groups):
        rows = slice(k * DIAG, (k + 1) * DIAG)
        left = tri_ref[rows.start // CYC : rows.stop // CYC, :, : k * DIAG].reshape(DIAG, k * DIAG)
        high_ref[rows, : k * DIAG], low_ref[rows, : k * DIAG] = split(left)

    down = lax.broadcasted_iota(jnp.int32, (HALF, HALF), 0)
    along = lax.broadcasted_iota(jnp.int32, (HALF, HALF), 1)
    eye = jnp.where(down == along, 1.0, 0.0).astype(F32)

    def below(size):
        return (down // size == along // size + 1) & ((down // size) % 2 == 1)

    count = PANEL // HALF
    diagonal = [block(i * HALF, i * HALF, HALF) for i in range(count)]
    wides = [side_by_side(d) for d in diagonal]
    inverse = [eye - jnp.where(below(1), d, 0.0) for d in diagonal]
    size = 2
    while size < HALF:
        keep = jnp.where(below(size), 1.0, 0.0).astype(BF16)
        keep = jnp.concatenate([keep, keep], axis=1)
        right = [small_times(wides[i] * keep, inverse[i]) for i in range(count)]
        inverse = [inverse[i] - small_times(side_by_side(inverse[i]), right[i]) for i in range(count)]
        size *= 2
    for k in range(groups):
        first, second = inverse[2 * k], inverse[2 * k + 1]
        corner = block(k * DIAG + HALF, k * DIAG, HALF)
        right = small_times(side_by_side(corner), first)
        corner = -small_times(side_by_side(second), right)
        empty = jnp.zeros((HALF, HALF), F32)
        whole = jnp.concatenate(
            [jnp.concatenate([first, empty], axis=1), jnp.concatenate([corner, second], axis=1)], axis=0
        )
        inv_high_ref[k], inv_low_ref[k] = split(whole)


def invert_panel(panel, place, factor, pieces, owners, shares, panel_rows, after, flops):
    groups = PANEL // DIAG
    return pl.pallas_call(
        functools.partial(invert_kernel, panel, owners, shares),
        out_shape=[shaped(PANEL, PANEL, dtype=BF16)] * 2 + [shaped(groups, DIAG, DIAG, dtype=BF16)] * 2,
        in_specs=[IN_SMEM, pl.BlockSpec(memory_space=pl.ANY), IN_HBM] + [IN_VMEM] * len(pieces),
        out_specs=[IN_VMEM] * 4,
        scratch_shapes=[
            pltpu.VMEM((panel_rows, PANEL), F32),
            pltpu.VMEM((PANEL // CYC, CYC, PANEL), F32),
            pltpu.SemaphoreType.DMA,
        ],
        compiler_params=params(16),
        cost_estimate=cost(flops, 12 * MIB),
        name="invert_panel",
    )(place, after, factor, *pieces)


def order_kernel(first, pivot_ref, grouped_ref, after_ref, *out_refs):
    for out_ref in out_refs:
        pick_rows(pivot_ref, first, grouped_ref, out_ref)
        first += out_ref.shape[0]


def pick_rows(pivot_ref, first, source_ref, target_ref):
    step = 8

    def body(i, _):
        base = i * step
        rows = [source_ref[pl.ds(pivot_ref[first + base + j], 1)] for j in range(step)]
        target_ref[pl.ds(pl.multiple_of(base, step), step)] = jnp.concatenate(rows, axis=0)
        return 0

    lax.fori_loop(0, target_ref.shape[0] // step, body, 0, unroll=4)


def order_rows(first, counts, pivot_rows, grouped, after):
    return pl.pallas_call(
        functools.partial(order_kernel, first),
        out_shape=[shaped(count, grouped.shape[1]) for count in counts],
        in_specs=[IN_SMEM, IN_VMEM, pl.BlockSpec(memory_space=pl.ANY)],
        out_specs=[IN_VMEM] * len(counts),
        compiler_params=params(4),
        cost_estimate=cost(0, 2 * MIB),
        name="order_rows",
    )(pivot_rows, grouped, after)


def solve_into(me, owners, pieces, high_ref, low_ref, inv_high_ref, inv_low_ref, rhs_ref, wide_ref, y_ref):
    slots = pieces[0].shape[0] // CYC
    columns = pieces[0].shape[1]
    for k in range(owners):
        for s in range(slots):
            rhs_ref[s * owners + (me ^ k)] = pieces[k][s * CYC : (s + 1) * CYC]
    for k in range(PANEL // DIAG):
        rows = slice(k * DIAG, (k + 1) * DIAG)
        rhs = rhs_ref[rows.start // CYC : rows.stop // CYC].reshape(DIAG, columns)
        if k:
            done = wide_ref[: k * DIAG]
            rhs = rhs - parts_times(high_ref[rows, : k * DIAG], low_ref[rows, : k * DIAG], done)
        wide = side_by_side(rhs)
        block = parts_times(inv_high_ref[k], inv_low_ref[k], wide)
        wide_ref[rows] = side_by_side(block)
        y_ref[rows.start // CYC : rows.stop // CYC] = block.reshape(DIAG // CYC, CYC, columns)


def first_kernel(owners, place_ref, factor_ref, *refs):
    pieces = refs[:owners]
    high, low, inv_high, inv_low, current_ref = refs[owners : owners + 5]
    y_ref, next_ref, rhs_ref, wide_ref, left_ref, sem = refs[owners + 5 :]
    rows = left_ref.shape[0]
    copy = pltpu.make_async_copy(factor_ref.at[pl.ds(rows, rows), pl.ds(0, PANEL)], left_ref, sem)
    copy.start()
    solve_into(place_ref[0], owners, pieces, high, low, inv_high, inv_low, rhs_ref, wide_ref, y_ref)
    copy.wait()
    next_ref[...] = current_ref[...] - times(left_ref[...], wide_ref[...])


def first_solve(place, pieces, prepared, factor, current, panel_rows):
    owners = len(pieces)
    columns = current.shape[1]
    return pl.pallas_call(
        functools.partial(first_kernel, owners),
        out_shape=[shaped(PANEL // CYC, CYC, columns), shaped(panel_rows, columns)],
        in_specs=[IN_SMEM, IN_HBM] + [IN_VMEM] * (owners + 5),
        out_specs=[IN_VMEM] * 2,
        scratch_shapes=[
            pltpu.VMEM((PANEL // CYC, CYC, columns), F32),
            pltpu.VMEM((PANEL, 2 * columns), BF16),
            pltpu.VMEM((panel_rows, PANEL), F32),
            pltpu.SemaphoreType.DMA,
        ],
        compiler_params=params(8),
        cost_estimate=cost(HEAVY, 6 * MIB),
        name="first_solve",
    )(place, factor, *pieces, *prepared, current)


def pivot_weights(me, sizes, diag, off):
    pairs, lanes = off.shape[1], diag.shape[1]
    spread = lax.broadcasted_iota(jnp.int32, (pairs, lanes), 1) // 2 == lax.broadcasted_iota(
        jnp.int32, (pairs, lanes), 0
    )
    spread = jnp.where(spread, 1.0, 0.0).astype(F32)
    off = jnp.dot(off, spread, precision=lax.Precision.HIGHEST, preferred_element_type=F32)
    sizes = jnp.dot(sizes.astype(F32), spread, precision=lax.Precision.HIGHEST, preferred_element_type=F32)
    odd = lax.broadcasted_iota(jnp.int32, diag.shape, 1) % 2 == 1
    other = jnp.where(odd, pltpu.roll(diag, 1, 1), pltpu.roll(diag, lanes - 1, 1))
    determ = diag * other - off * off
    is_pair = sizes > 1.5
    keep = jnp.where(is_pair, other / determ, 1.0 / diag)
    swap = jnp.where(is_pair, -off / determ, 0.0)
    turned = []
    for weight in (keep, swap):
        weight = pltpu.roll(weight, lax.rem(lanes - CYC * me, lanes), 1)
        tall = jnp.concatenate([weight] * (HALF // weight.shape[0]), axis=0)
        turned.append(tall.T)
    return turned


def ready_kernel(
    tile_rows, place_ref, after_ref, factor_ref, sizes_ref, diag_ref, off_ref, keep_ref, swap_ref, high_ref, low_ref,
    left_ref, sems,
):
    tiles = left_ref.shape[0]
    loads = []
    for t in range(tiles):
        source = factor_ref.at[pl.ds((t + 1) * tile_rows, tile_rows), pl.ds((PANELS - 1) * PANEL, PANEL)]
        loads.append(pltpu.make_async_copy(source, left_ref.at[t], sems.at[t]))
        loads[t].start()
    keep_ref[...], swap_ref[...] = pivot_weights(place_ref[0], sizes_ref[...], diag_ref[...], off_ref[...])
    for t in range(tiles):
        loads[t].wait()
        rows = slice(t * tile_rows, (t + 1) * tile_rows)
        high_ref[rows], low_ref[rows] = split(left_ref[t])


def make_ready(place, factor, pivots, tile_rows, after):
    weight = shaped(pivots[1].shape[1], HALF)
    tiles = factor.shape[0] // tile_rows - 1
    return pl.pallas_call(
        functools.partial(ready_kernel, tile_rows),
        out_shape=[weight, weight] + [shaped(tiles * tile_rows, PANEL, dtype=BF16)] * 2,
        in_specs=[IN_SMEM, pl.BlockSpec(memory_space=pl.ANY), IN_HBM] + [IN_VMEM] * len(pivots),
        out_specs=[IN_VMEM] * 4,
        scratch_shapes=[pltpu.VMEM((tiles, tile_rows, PANEL), F32), pltpu.SemaphoreType.DMA((tiles,))],
        compiler_params=params(12),
        cost_estimate=cost(HEAVY, 0),
        name="make_ready",
    )(place, after, factor, *pivots)


def middle_kernel(tile_rows, factor_ref, rest_ref, y_ref, out_ref, wide_ref, left_ref, sems):
    tiles = left_ref.shape[0]
    loads = []
    for t in range(tiles):
        source = factor_ref.at[pl.ds((t + 1) * tile_rows, tile_rows), pl.ds(0, PANEL)]
        loads.append(pltpu.make_async_copy(source, left_ref.at[t], sems.at[t]))
        loads[t].start()
    wide_ref[...] = side_by_side(y_ref[...].reshape(PANEL, y_ref.shape[2]))
    for t in range(tiles):
        loads[t].wait()
        rows = slice(t * tile_rows, (t + 1) * tile_rows)
        out_ref[rows] = rest_ref[rows] - times(left_ref[t], wide_ref[...])


def middle_update(rest, y, factor, tile_rows):
    rows, columns = rest.shape
    tiles = rows // tile_rows
    return pl.pallas_call(
        functools.partial(middle_kernel, tile_rows),
        out_shape=shaped(rows, columns),
        in_specs=[IN_HBM] + [IN_VMEM] * 2,
        out_specs=IN_VMEM,
        scratch_shapes=[
            pltpu.VMEM((PANEL, 2 * columns), BF16),
            pltpu.VMEM((tiles, tile_rows, PANEL), F32),
            pltpu.SemaphoreType.DMA((tiles,)),
        ],
        compiler_params=params(12),
        cost_estimate=cost(8 * rows * PANEL * columns, 8 * MIB),
        name="middle_update",
    )(factor, rest, y)


def last_kernel(owners, tile_rows, place_ref, *refs):
    pieces = refs[:owners]
    high, low, inv_high, inv_low, y_ref, keep_ref, swap_ref = refs[owners : owners + 7]
    left_high, left_low, rest_ref, out_ref, rhs_ref, wide_ref, second_ref, stage_ref, sems = refs[owners + 7 :]
    me = place_ref[0]
    solve_into(me, owners, pieces, high, low, inv_high, inv_low, rhs_ref, wide_ref, second_ref)
    stores = []
    for t in range(stage_ref.shape[0]):
        if t:
            rows = slice((t - 1) * tile_rows, t * tile_rows)
            stage_ref[t] = rest_ref[rows] - parts_times(left_high[rows], left_low[rows], wide_ref[...])
        else:
            scale_own_rows(me, owners, y_ref, second_ref, keep_ref, swap_ref, stage_ref)
        target = out_ref.at[pl.ds(t * tile_rows, tile_rows)]
        stores.append(pltpu.make_async_copy(stage_ref.at[t], target, sems.at[t]))
        stores[t].start()
    for store in stores:
        store.wait()


def scale_own_rows(me, owners, first_ref, second_ref, keep_ref, swap_ref, stage_ref):
    slots = first_ref.shape[0] // owners
    runs = keep_ref.shape[0] // (owners * CYC)
    for panel, source in enumerate((first_ref, second_ref)):
        for s in range(slots):
            at = panel * slots + s
            rows = source[s * owners + me]
            odd = lax.broadcasted_iota(jnp.int32, rows.shape, 0) % 2 == 1
            other = jnp.where(odd, pltpu.roll(rows, 1, 0), pltpu.roll(rows, CYC - 1, 0))
            first = (at % runs) * owners * CYC
            keep = keep_ref[first : first + CYC, at // runs : at // runs + 1]
            swap = swap_ref[first : first + CYC, at // runs : at // runs + 1]
            mixed = keep * rows + jnp.where(swap != 0, swap * other, 0.0)
            stage_ref[0, at * CYC : (at + 1) * CYC] = mixed


def last_solve(place, pieces, prepared, y, weights, left, rest, tile_rows):
    owners = len(pieces)
    columns = rest.shape[1]
    rows = rest.shape[0] + tile_rows
    return pl.pallas_call(
        functools.partial(last_kernel, owners, tile_rows),
        out_shape=shaped(rows, columns),
        in_specs=[IN_SMEM] + [IN_VMEM] * (owners + 10),
        out_specs=IN_HBM,
        scratch_shapes=[
            pltpu.VMEM((PANEL // CYC, CYC, columns), F32),
            pltpu.VMEM((PANEL, 2 * columns), BF16),
            pltpu.VMEM((PANEL // CYC, CYC, columns), F32),
            pltpu.VMEM((rows // tile_rows, tile_rows, columns), F32),
            pltpu.SemaphoreType.DMA((rows // tile_rows,)),
        ],
        compiler_params=params(12),
        cost_estimate=cost(8 * rows * PANEL * columns, 12 * MIB),
        name="last_solve",
    )(place, *pieces, *prepared, y, *weights, *left, rest)


def swap_with(value, axis, distance):
    size = lax.axis_size(axis)
    return lax.ppermute(value, axis, [(i, i ^ distance) for i in range(size)])


def from_all(value, axis):
    return [value] + [swap_with(value, axis, k) for k in range(1, lax.axis_size(axis))]


def local(vectors, intersection, factor, pivot_rows, pivot_sizes, pivot_diag, pivot_off):
    owners, shares = lax.axis_size("row"), lax.axis_size("vec")
    slots = PANEL // owners // CYC
    panel_rows = slots * CYC
    place = jnp.stack([lax.axis_index("row"), lax.axis_index("vec")]).astype(jnp.int32)
    intersection, factor = (pltpu.with_memory_space_constraint(a, pltpu.HBM) for a in (intersection, factor))

    share, first, last = first_sends(
        place, factor, pltpu.with_memory_space_constraint(vectors, pltpu.HBM), slots, shares
    )
    up = [(i, i + 1) for i in range(owners - 1)]
    down = [(j, i) for i, j in up]
    halo = lax.ppermute(last, "row", up), lax.ppermute(first, "row", down)
    direct = from_all(share, "row")[1:]
    product = band_product_split(intersection, vectors, halo, owners)
    grouped = lax.all_to_all(product, "row", 0, 0, tiled=True).reshape(vectors.shape)

    def share_out(panel, after, after_crossing):
        stacked = stack(panel, direct, after)
        mine = pair(stacked, swap_with(stacked, "vec", 2), after_crossing)
        return mine, swap_with(mine, "vec", 1)

    tile_rows = PANELS * panel_rows
    pivots = [a.reshape(pivot_diag.shape[0] // DIAG, -1) for a in (pivot_sizes, pivot_diag, pivot_off)]
    keep, swap, *left = make_ready(place, factor, pivots, tile_rows, product)
    shared = share_out(0, keep, ())
    (first,) = order_rows(0, [panel_rows], pivot_rows, grouped, place)
    prepared = invert_panel(0, place, factor, shared, owners, shares, panel_rows, first, HEAVY)
    rest_rows = factor.shape[0] - tile_rows
    second, rest = order_rows(panel_rows, [tile_rows - panel_rows, rest_rows], pivot_rows, grouped, first)
    later = share_out(1, first, (prepared[2], second))
    pieces = from_all(first, "row")
    y, second = first_solve(place, pieces, prepared, factor, second, panel_rows)
    pieces = from_all(second, "row")
    rest = middle_update(rest, y, factor, tile_rows)
    prepared = invert_panel(1, place, factor, later, owners, shares, panel_rows, y, LIGHT)
    return last_solve(place, pieces, prepared, y, (keep, swap), left, rest, tile_rows)


def padded_2(shard, sides, width):
    for axis, dim in sides:
        devices, length = (lax.axis_size(axis), shard.shape[dim])
        up = [(i, (i + 1) % devices) for i in range(devices - 1)]
        down = [(j, i) for i, j in up]
        last = lax.slice_in_dim(shard, length - width, length, axis=dim)
        leading = lax.slice_in_dim(shard, 0, width, axis=dim)
        before = lax.ppermute(last, axis, up)
        after = lax.ppermute(leading, axis, down)
        shard = jnp.concatenate([before, shard, after], axis=dim)
    return shard


def band_product(intersection, padded, blocks_here):
    band_width = intersection.shape[1] // 3
    band_rows = intersection.reshape(blocks_here, band_width, 3 * band_width)
    result = jnp.zeros((blocks_here, band_width, padded.shape[1]), jnp.float32)
    for offset in range(3):
        window = padded[offset * band_width : offset * band_width + blocks_here * band_width]
        window = window.reshape(blocks_here, band_width, padded.shape[1])
        result = result + jnp.einsum(
            "kij,kjv->kiv",
            band_rows[:, :, offset * band_width : (offset + 1) * band_width],
            window,
            precision=lax.Precision.HIGHEST,
        )
    return result.reshape(blocks_here * band_width, padded.shape[1])


def scale_pivots(values, sizes_here, diag_here, off_here):
    paired = values.reshape(-1, 2, values.shape[1])
    leading = paired[:, 0]
    trailing = paired[:, 1]
    diag_lead = diag_here[0::2][:, None]
    diag_next = diag_here[1::2][:, None]
    coupling = off_here[:, None]
    determ = diag_lead * diag_next - coupling * coupling
    is_pair = (sizes_here == 2)[:, None]
    new_lead = jnp.where(
        is_pair, (diag_next * leading - coupling * trailing) / determ, leading / diag_lead
    )
    new_next = jnp.where(
        is_pair, (diag_lead * trailing - coupling * leading) / determ, trailing / diag_next
    )
    return jnp.stack([new_lead, new_next], axis=1).reshape(values.shape)


def local_many(vectors, intersection, factor, pivot_rows, pivot_sizes, pivot_diag, pivot_off):
    owners = lax.axis_size("row")
    device = lax.axis_index("row")
    rows_here = vectors.shape[0]
    columns = vectors.shape[1]
    slot_count = PANEL // owners // CYC
    panel_rows = slot_count * CYC
    triangles = []
    quarter = PANEL // lax.axis_size("vec")
    column_idx = lax.axis_index("vec")
    for panel_num in range(PANELS):
        local_rows = factor[panel_num * panel_rows : (panel_num + 1) * panel_rows]
        column_part = lax.dynamic_slice_in_dim(
            local_rows, panel_num * PANEL + column_idx * quarter, quarter, 1
        )
        column_part = column_part.reshape(slot_count, 1, CYC, quarter)
        gathered = lax.all_gather(column_part, "row", axis=1, tiled=True)
        triangles.append(lax.all_gather(gathered, "vec", axis=3, tiled=True).reshape(PANEL, PANEL))
    padded = padded_2(vectors, (("row", 0),), BS)
    product = band_product(intersection, padded, rows_here // BS)
    grouped = product.reshape(rows_here // (CYC * owners), owners, CYC, columns)
    regrouped = lax.all_to_all(grouped, "row", split_axis=1, concat_axis=0, tiled=True).reshape(
        rows_here, columns
    )
    current = jnp.take(regrouped, pivot_rows, axis=0)
    outputs = []
    for panel_num in range(PANELS):
        row_first = panel_num * panel_rows
        row_end = row_first + panel_rows
        col_first = panel_num * PANEL
        col_end = col_first + PANEL
        rhs_local = current[row_first:row_end].reshape(slot_count, 1, CYC, columns)
        rhs_all = lax.all_gather(rhs_local, "row", axis=1, tiled=True)
        triangle = triangles[panel_num]
        block_sol = jax.scipy.linalg.solve_triangular(
            triangle, rhs_all.reshape(PANEL, columns), lower=True, unit_diagonal=True
        )
        update = jnp.dot(
            factor[row_end:, col_first:col_end], block_sol, precision=lax.Precision.HIGHEST
        )
        current = jnp.concatenate([current[:row_end], current[row_end:] - update], axis=0)
        scaled = scale_pivots(
            block_sol,
            pivot_sizes[col_first // 2 : col_end // 2],
            pivot_diag[col_first:col_end],
            pivot_off[col_first // 2 : col_end // 2],
        )
        own_rows = lax.dynamic_slice_in_dim(
            scaled.reshape(slot_count, owners, CYC, columns), device, 1, 1
        )
        outputs.append(own_rows.reshape(panel_rows, columns))
    outputs.append(current[PANELS * panel_rows :])
    return jnp.concatenate(outputs, axis=0)


def solution(mesh):
    in_specs = (
        P(("cuts", "row"), "vec"),
        P("row", None),
        P(("cuts", "row"), None),
        P(("cuts", "row")),
        P("cuts"),
        P("cuts"),
        P("cuts"),
    )
    out_specs = P(("cuts", "row"), "vec")
    owners, shares = mesh.shape["row"], mesh.shape["vec"]
    few = owners == 4 and shares == 4 and DIAG == owners * shares * CYC
    body = local if few else local_many
    return jax.shard_map(body, mesh=mesh, in_specs=in_specs, out_specs=out_specs, check_vma=False)
```

```python
import functools

import jax
import jax.numpy as jnp
from jax import lax
from jax.experimental import pallas as pl
from jax.experimental.pallas import tpu as pltpu
from jax.sharding import PartitionSpec as P

BS = 512
PANEL = 1024
PANELS = 2
CYC = 16
DIAG = 256
HALF = 128
MIB = 1024 * 1024
HEAVY = 2**37
LIGHT = 2**30
F32 = jnp.float32
BF16 = jnp.bfloat16


def params(mib):
    return pltpu.CompilerParams(vmem_limit_bytes=mib * MIB)


IN_VMEM = pl.BlockSpec(memory_space=pltpu.VMEM)
IN_SMEM = pl.BlockSpec(memory_space=pltpu.SMEM)
IN_HBM = pl.BlockSpec(memory_space=pltpu.HBM)


def shaped(*shape, dtype=F32):
    return jax.ShapeDtypeStruct(shape, dtype)


def cost(flops, moved):
    return pl.CostEstimate(flops=int(flops), bytes_accessed=int(moved), transcendentals=0)


def split(value):
    high = value.astype(BF16)
    low = (value - high.astype(F32)).astype(BF16)
    return high, low


def side_by_side(value):
    return jnp.concatenate(split(value), axis=1)


def dot(left, right):
    return jnp.dot(left, right, preferred_element_type=F32)


def fold(wide):
    width = wide.shape[1] // 2
    return wide[:, :width] + wide[:, width:]


def times(left, right_wide):
    high, low = split(left)
    return parts_times(high, low, right_wide)


def parts_times(high, low, right_wide):
    return fold(dot(high, right_wide)) + dot(low, right_wide[:, : right_wide.shape[1] // 2])


def small_times(left_wide, right):
    wide = side_by_side(right)
    return fold(dot(left_wide, jnp.concatenate([wide, wide], axis=0)))


def start_kernel(slots, shares, place_ref, factor_ref, vec_ref, *refs):
    share_ref, first_ref, last_ref, sems = refs
    groups = PANEL // DIAG
    part = place_ref[1]
    rows = vec_ref.shape[0]
    copies = [(vec_ref.at[pl.ds(rows - BS, BS)], last_ref), (vec_ref.at[pl.ds(0, BS)], first_ref)]
    for panel in range(PANELS):
        at = 0
        for k in range(groups):
            row = pl.multiple_of((panel * slots + k * shares + part) * CYC, CYC)
            for j in range(k + 1):
                source = factor_ref.at[pl.ds(row, CYC), pl.ds(panel * PANEL + j * DIAG, DIAG)]
                copies.append((source, share_ref.at[panel, at]))
                at += 1
    started = [pltpu.make_async_copy(a, b, sems.at[i]) for i, (a, b) in enumerate(copies)]
    for copy in started:
        copy.start()
    for copy in started:
        copy.wait()


def first_sends(place, factor, vectors, slots, shares):
    groups = PANEL // DIAG
    blocks = groups * (groups + 1) // 2
    edge = shaped(BS, vectors.shape[1])
    return pl.pallas_call(
        functools.partial(start_kernel, slots, shares),
        out_shape=[shaped(PANELS, blocks, CYC, DIAG), edge, edge],
        in_specs=[IN_SMEM, IN_HBM, IN_HBM],
        out_specs=[IN_VMEM] * 3,
        scratch_shapes=[pltpu.SemaphoreType.DMA((PANELS * blocks + 2,))],
        compiler_params=params(4),
        cost_estimate=cost(0, 4 * MIB),
        name="first_sends",
    )(place, factor, vectors)


def band_kernel(inter_ref, vec_ref, before_ref, after_ref, out_ref, wide_ref):
    tile = pl.program_id(0)
    rows = vec_ref.shape[0]
    tile_rows = inter_ref.shape[0]
    owners = out_ref.shape[0]

    @pl.when(tile == 0)
    def _():
        wide_ref[:BS] = side_by_side(before_ref[...])
        wide_ref[BS : BS + rows] = side_by_side(vec_ref[...])
        wide_ref[BS + rows :] = side_by_side(after_ref[...])

    window = wide_ref[pl.ds(pl.multiple_of(tile * BS, BS), 3 * BS)]
    product = times(inter_ref[...], window)
    groups = tile_rows // (owners * CYC)
    for g in range(groups):
        for owner in range(owners):
            first = (g * owners + owner) * CYC
            out_ref[owner, g * CYC : (g + 1) * CYC] = product[first : first + CYC]


def band_product_split(intersection, vectors, halo, owners):
    rows, columns = vectors.shape
    width = intersection.shape[1]
    tile_rows = BS
    slot_rows = tile_rows // owners
    whole = lambda t: (0, 0)
    return pl.pallas_call(
        band_kernel,
        out_shape=shaped(owners, rows // owners, columns),
        grid=(rows // tile_rows,),
        in_specs=[
            pl.BlockSpec((tile_rows, width), lambda t: (t, 0)),
            pl.BlockSpec((rows, columns), whole),
            pl.BlockSpec((BS, columns), whole),
            pl.BlockSpec((BS, columns), whole),
        ],
        out_specs=pl.BlockSpec((owners, slot_rows, columns), lambda t: (0, t, 0)),
        scratch_shapes=[pltpu.VMEM((rows + 2 * BS, 2 * columns), BF16)],
        compiler_params=params(16),
        cost_estimate=cost(8 * rows * width * columns, 4 * rows * width),
        name="band_product_split",
    )(intersection, vectors, *halo)


def pass_kernel(value_ref, after_ref, out_ref):
    pass


def pass_on(value, after):
    anywhere = pl.BlockSpec(memory_space=pl.ANY)
    return pl.pallas_call(
        pass_kernel,
        out_shape=shaped(*value.shape),
        in_specs=[anywhere, anywhere],
        out_specs=anywhere,
        input_output_aliases={0: 0},
        compiler_params=params(1),
        name="pass_on",
    )(value, after)


def from_others(value, after):
    end = lax.axis_size("row") - 1
    middle = [(i, end - i) for i in range(1, end)]
    across = pass_on(swap_with(value, "row", 2), after)
    near, inner = swap_with(value, "row", 1), lax.ppermute(value, "row", middle)
    outer = lax.ppermute(across, "row", [(i, i ^ 1) for i, _ in middle])
    return near, across, inner, outer


def stack_kernel(place_ref, near_ref, across_ref, inner_ref, outer_ref, after_ref, *out_refs):
    me = place_ref[0]
    end = out_refs[0].shape[0]
    for panel, out_ref in enumerate(out_refs):
        out_ref[0] = near_ref[panel]
        out_ref[1] = across_ref[panel]

    @pl.when((me > 0) & (me < end))
    def _():
        for panel, out_ref in enumerate(out_refs):
            out_ref[2] = inner_ref[panel]

    @pl.when((me == 0) | (me == end))
    def _():
        for panel, out_ref in enumerate(out_refs):
            out_ref[2] = outer_ref[panel]


def stack(place, pieces, after):
    return pl.pallas_call(
        stack_kernel,
        out_shape=[shaped(3, *pieces[0].shape[1:])] * PANELS,
        in_specs=[IN_SMEM] + [IN_VMEM] * 4 + [pl.BlockSpec(memory_space=pl.ANY)],
        out_specs=[IN_VMEM] * PANELS,
        compiler_params=params(4),
        name="stack",
    )(place, *pieces, after)


def invert_kernel(panel, owners, shares, place_ref, after_ref, factor_ref, *refs):
    pieces = refs[:shares]
    high_ref, low_ref, inv_high_ref, inv_low_ref, own_ref, tri_ref, sem = refs[-7:]
    groups = PANEL // DIAG
    me, part = place_ref[0], place_ref[1]
    rows = own_ref.shape[0]
    copy = pltpu.make_async_copy(
        factor_ref.at[pl.ds(panel * rows, rows), pl.ds(panel * PANEL, PANEL)], own_ref, sem
    )
    copy.start()
    for other in range(1, owners):
        owner = me ^ other
        for turn in range(shares):
            at = 0
            for k in range(groups):
                for j in range(k + 1):
                    piece = pieces[turn][other - 1, at]
                    to = (k * shares + (part ^ turn)) * owners + owner
                    tri_ref[to, :, j * DIAG : (j + 1) * DIAG] = piece
                    at += 1
    copy.wait()
    for k in range(groups):
        reach = (k + 1) * DIAG
        for s in range(shares):
            row = (k * shares + s) * CYC
            tri_ref[(k * shares + s) * owners + me, :, :reach] = own_ref[row : row + CYC, :reach]

    def block(row, column, size):
        part_rows = tri_ref[row // CYC : (row + size) // CYC, :, column : column + size]
        return part_rows.reshape(size, size)

    for k in range(1, groups):
        rows = slice(k * DIAG, (k + 1) * DIAG)
        left = tri_ref[rows.start // CYC : rows.stop // CYC, :, : k * DIAG].reshape(DIAG, k * DIAG)
        high_ref[rows, : k * DIAG], low_ref[rows, : k * DIAG] = split(left)

    down = lax.broadcasted_iota(jnp.int32, (HALF, HALF), 0)
    along = lax.broadcasted_iota(jnp.int32, (HALF, HALF), 1)
    eye = jnp.where(down == along, 1.0, 0.0).astype(F32)

    def below(size):
        return (down // size == along // size + 1) & ((down // size) % 2 == 1)

    count = PANEL // HALF
    diagonal = [block(i * HALF, i * HALF, HALF) for i in range(count)]
    wides = [side_by_side(d) for d in diagonal]
    inverse = [eye - jnp.where(below(1), d, 0.0) for d in diagonal]
    size = 2
    while size < HALF:
        keep = jnp.where(below(size), 1.0, 0.0).astype(BF16)
        keep = jnp.concatenate([keep, keep], axis=1)
        right = [small_times(wides[i] * keep, inverse[i]) for i in range(count)]
        inverse = [inverse[i] - small_times(side_by_side(inverse[i]), right[i]) for i in range(count)]
        size *= 2
    for k in range(groups):
        first, second = inverse[2 * k], inverse[2 * k + 1]
        corner = block(k * DIAG + HALF, k * DIAG, HALF)
        right = small_times(side_by_side(corner), first)
        corner = -small_times(side_by_side(second), right)
        empty = jnp.zeros((HALF, HALF), F32)
        whole = jnp.concatenate(
            [jnp.concatenate([first, empty], axis=1), jnp.concatenate([corner, second], axis=1)], axis=0
        )
        inv_high_ref[k], inv_low_ref[k] = split(whole)


def invert_panel(panel, place, factor, pieces, owners, shares, panel_rows, after, flops):
    groups = PANEL // DIAG
    return pl.pallas_call(
        functools.partial(invert_kernel, panel, owners, shares),
        out_shape=[shaped(PANEL, PANEL, dtype=BF16)] * 2 + [shaped(groups, DIAG, DIAG, dtype=BF16)] * 2,
        in_specs=[IN_SMEM, pl.BlockSpec(memory_space=pl.ANY), IN_HBM] + [IN_VMEM] * len(pieces),
        out_specs=[IN_VMEM] * 4,
        scratch_shapes=[
            pltpu.VMEM((panel_rows, PANEL), F32),
            pltpu.VMEM((PANEL // CYC, CYC, PANEL), F32),
            pltpu.SemaphoreType.DMA,
        ],
        compiler_params=params(16),
        cost_estimate=cost(flops, 12 * MIB),
        name="invert_panel",
    )(place, after, factor, *pieces)


def order_kernel(first, pivot_ref, grouped_ref, after_ref, *out_refs):
    for out_ref in out_refs:
        pick_rows(pivot_ref, first, grouped_ref, out_ref)
        first += out_ref.shape[0]


def pick_rows(pivot_ref, first, source_ref, target_ref):
    step = 8

    def body(i, _):
        base = i * step
        rows = [source_ref[pl.ds(pivot_ref[first + base + j], 1)] for j in range(step)]
        target_ref[pl.ds(pl.multiple_of(base, step), step)] = jnp.concatenate(rows, axis=0)
        return 0

    lax.fori_loop(0, target_ref.shape[0] // step, body, 0, unroll=4)


def order_rows(first, counts, pivot_rows, grouped, after):
    return pl.pallas_call(
        functools.partial(order_kernel, first),
        out_shape=[shaped(count, grouped.shape[1]) for count in counts],
        in_specs=[IN_SMEM, IN_VMEM, pl.BlockSpec(memory_space=pl.ANY)],
        out_specs=[IN_VMEM] * len(counts),
        compiler_params=params(4),
        cost_estimate=cost(0, 2 * MIB),
        name="order_rows",
    )(pivot_rows, grouped, after)


def solve_into(me, owners, pieces, high_ref, low_ref, inv_high_ref, inv_low_ref, rhs_ref, wide_ref, y_ref):
    slots = pieces[0].shape[0] // CYC
    columns = pieces[0].shape[1]
    for k in range(owners):
        for s in range(slots):
            rhs_ref[s * owners + (me ^ k)] = pieces[k][s * CYC : (s + 1) * CYC]
    for k in range(PANEL // DIAG):
        rows = slice(k * DIAG, (k + 1) * DIAG)
        rhs = rhs_ref[rows.start // CYC : rows.stop // CYC].reshape(DIAG, columns)
        if k:
            done = wide_ref[: k * DIAG]
            rhs = rhs - parts_times(high_ref[rows, : k * DIAG], low_ref[rows, : k * DIAG], done)
        wide = side_by_side(rhs)
        block = parts_times(inv_high_ref[k], inv_low_ref[k], wide)
        wide_ref[rows] = side_by_side(block)
        y_ref[rows.start // CYC : rows.stop // CYC] = block.reshape(DIAG // CYC, CYC, columns)


def first_kernel(owners, place_ref, factor_ref, *refs):
    pieces = refs[:owners]
    high, low, inv_high, inv_low, current_ref = refs[owners : owners + 5]
    y_ref, next_ref, rhs_ref, wide_ref, left_ref, sem = refs[owners + 5 :]
    rows = left_ref.shape[0]
    copy = pltpu.make_async_copy(factor_ref.at[pl.ds(rows, rows), pl.ds(0, PANEL)], left_ref, sem)
    copy.start()
    solve_into(place_ref[0], owners, pieces, high, low, inv_high, inv_low, rhs_ref, wide_ref, y_ref)
    copy.wait()
    next_ref[...] = current_ref[...] - times(left_ref[...], wide_ref[...])


def first_solve(place, pieces, prepared, factor, current, panel_rows):
    owners = len(pieces)
    columns = current.shape[1]
    return pl.pallas_call(
        functools.partial(first_kernel, owners),
        out_shape=[shaped(PANEL // CYC, CYC, columns), shaped(panel_rows, columns)],
        in_specs=[IN_SMEM, IN_HBM] + [IN_VMEM] * (owners + 5),
        out_specs=[IN_VMEM] * 2,
        scratch_shapes=[
            pltpu.VMEM((PANEL // CYC, CYC, columns), F32),
            pltpu.VMEM((PANEL, 2 * columns), BF16),
            pltpu.VMEM((panel_rows, PANEL), F32),
            pltpu.SemaphoreType.DMA,
        ],
        compiler_params=params(8),
        cost_estimate=cost(HEAVY, 6 * MIB),
        name="first_solve",
    )(place, factor, *pieces, *prepared, current)


def pivot_weights(me, sizes, diag, off):
    pairs, lanes = off.shape[1], diag.shape[1]
    spread = lax.broadcasted_iota(jnp.int32, (pairs, lanes), 1) // 2 == lax.broadcasted_iota(
        jnp.int32, (pairs, lanes), 0
    )
    spread = jnp.where(spread, 1.0, 0.0).astype(F32)
    off = jnp.dot(off, spread, precision=lax.Precision.HIGHEST, preferred_element_type=F32)
    sizes = jnp.dot(sizes.astype(F32), spread, precision=lax.Precision.HIGHEST, preferred_element_type=F32)
    odd = lax.broadcasted_iota(jnp.int32, diag.shape, 1) % 2 == 1
    other = jnp.where(odd, pltpu.roll(diag, 1, 1), pltpu.roll(diag, lanes - 1, 1))
    determ = diag * other - off * off
    is_pair = sizes > 1.5
    keep = jnp.where(is_pair, other / determ, 1.0 / diag)
    swap = jnp.where(is_pair, -off / determ, 0.0)
    turned = []
    for weight in (keep, swap):
        weight = pltpu.roll(weight, lax.rem(lanes - CYC * me, lanes), 1)
        tall = jnp.concatenate([weight] * (HALF // weight.shape[0]), axis=0)
        turned.append(tall.T)
    return turned


def weights_kernel(place_ref, after_ref, sizes_ref, diag_ref, off_ref, keep_ref, swap_ref):
    keep_ref[...], swap_ref[...] = pivot_weights(place_ref[0], sizes_ref[...], diag_ref[...], off_ref[...])


def own_weights(place, pivots, after):
    weight = shaped(pivots[1].shape[1], HALF)
    return pl.pallas_call(
        weights_kernel,
        out_shape=[weight, weight],
        in_specs=[IN_SMEM, pl.BlockSpec(memory_space=pl.ANY)] + [IN_VMEM] * len(pivots),
        out_specs=[IN_VMEM] * 2,
        compiler_params=params(4),
        cost_estimate=cost(HEAVY, 0),
        name="own_weights",
    )(place, after, *pivots)


def halve_kernel(tile_rows, factor_ref, after_ref, out_ref, token_ref, left_ref, parts_ref, in_sems, out_sems):
    token_ref[...] = jnp.zeros_like(token_ref)
    tiles = left_ref.shape[0]
    loads, stores = [], []
    for t in range(tiles):
        source = factor_ref.at[pl.ds((t + 1) * tile_rows, tile_rows), pl.ds((PANELS - 1) * PANEL, PANEL)]
        loads.append(pltpu.make_async_copy(source, left_ref.at[t], in_sems.at[t]))
        loads[t].start()
    for t in range(tiles):
        loads[t].wait()
        parts_ref[t, 0], parts_ref[t, 1] = split(left_ref[t])
        stores.append(pltpu.make_async_copy(parts_ref.at[t], out_ref.at[t], out_sems.at[t]))
        stores[t].start()
    for store in stores:
        store.wait()


def halve_last(factor, tile_rows, after):
    tiles = factor.shape[0] // tile_rows - 1
    return pl.pallas_call(
        functools.partial(halve_kernel, tile_rows),
        out_shape=[shaped(tiles, 2, tile_rows, PANEL, dtype=BF16), shaped(8, HALF)],
        in_specs=[IN_HBM, pl.BlockSpec(memory_space=pl.ANY)],
        out_specs=[IN_HBM, IN_VMEM],
        scratch_shapes=[
            pltpu.VMEM((tiles, tile_rows, PANEL), F32),
            pltpu.VMEM((tiles, 2, tile_rows, PANEL), BF16),
            pltpu.SemaphoreType.DMA((tiles,)),
            pltpu.SemaphoreType.DMA((tiles,)),
        ],
        compiler_params=params(18),
        cost_estimate=cost(LIGHT, 12 * MIB),
        name="halve_last",
    )(factor, after)


def middle_kernel(tile_rows, factor_ref, rest_ref, y_ref, out_ref, wide_ref, left_ref, sems):
    tiles = left_ref.shape[0]
    loads = []
    for t in range(tiles):
        source = factor_ref.at[pl.ds((t + 1) * tile_rows, tile_rows), pl.ds(0, PANEL)]
        loads.append(pltpu.make_async_copy(source, left_ref.at[t], sems.at[t]))
        loads[t].start()
    wide_ref[...] = side_by_side(y_ref[...].reshape(PANEL, y_ref.shape[2]))
    for t in range(tiles):
        loads[t].wait()
        rows = slice(t * tile_rows, (t + 1) * tile_rows)
        out_ref[rows] = rest_ref[rows] - times(left_ref[t], wide_ref[...])


def middle_update(rest, y, factor, tile_rows):
    rows, columns = rest.shape
    tiles = rows // tile_rows
    return pl.pallas_call(
        functools.partial(middle_kernel, tile_rows),
        out_shape=shaped(rows, columns),
        in_specs=[IN_HBM] + [IN_VMEM] * 2,
        out_specs=IN_VMEM,
        scratch_shapes=[
            pltpu.VMEM((PANEL, 2 * columns), BF16),
            pltpu.VMEM((tiles, tile_rows, PANEL), F32),
            pltpu.SemaphoreType.DMA((tiles,)),
        ],
        compiler_params=params(12),
        cost_estimate=cost(8 * rows * PANEL * columns, 8 * MIB),
        name="middle_update",
    )(factor, rest, y)


def last_kernel(owners, tile_rows, place_ref, left_ref, *refs):
    pieces = refs[:owners]
    high, low, inv_high, inv_low, y_ref, keep_ref, swap_ref, rest_ref = refs[owners : owners + 8]
    out_ref, rhs_ref, wide_ref, second_ref, stage_ref, sems = refs[owners + 8 :]
    me = place_ref[0]
    solve_into(me, owners, pieces, high, low, inv_high, inv_low, rhs_ref, wide_ref, second_ref)
    stores = []
    for t in range(stage_ref.shape[0]):
        if t:
            rows = slice((t - 1) * tile_rows, t * tile_rows)
            stage_ref[t] = rest_ref[rows] - parts_times(left_ref[t - 1, 0], left_ref[t - 1, 1], wide_ref[...])
        else:
            scale_own_rows(me, owners, y_ref, second_ref, keep_ref, swap_ref, stage_ref)
        target = out_ref.at[pl.ds(t * tile_rows, tile_rows)]
        stores.append(pltpu.make_async_copy(stage_ref.at[t], target, sems.at[t]))
        stores[t].start()
    for store in stores:
        store.wait()


def scale_own_rows(me, owners, first_ref, second_ref, keep_ref, swap_ref, stage_ref):
    slots = first_ref.shape[0] // owners
    runs = keep_ref.shape[0] // (owners * CYC)
    for panel, source in enumerate((first_ref, second_ref)):
        for s in range(slots):
            at = panel * slots + s
            rows = source[s * owners + me]
            odd = lax.broadcasted_iota(jnp.int32, rows.shape, 0) % 2 == 1
            other = jnp.where(odd, pltpu.roll(rows, 1, 0), pltpu.roll(rows, CYC - 1, 0))
            first = (at % runs) * owners * CYC
            keep = keep_ref[first : first + CYC, at // runs : at // runs + 1]
            swap = swap_ref[first : first + CYC, at // runs : at // runs + 1]
            mixed = keep * rows + jnp.where(swap != 0, swap * other, 0.0)
            stage_ref[0, at * CYC : (at + 1) * CYC] = mixed


def last_solve(place, parts, pieces, prepared, y, weights, rest, tile_rows):
    owners = len(pieces)
    columns = rest.shape[1]
    rows = rest.shape[0] + tile_rows
    return pl.pallas_call(
        functools.partial(last_kernel, owners, tile_rows),
        out_shape=shaped(rows, columns),
        in_specs=[IN_SMEM] + [IN_VMEM] * (owners + 9),
        out_specs=IN_HBM,
        scratch_shapes=[
            pltpu.VMEM((PANEL // CYC, CYC, columns), F32),
            pltpu.VMEM((PANEL, 2 * columns), BF16),
            pltpu.VMEM((PANEL // CYC, CYC, columns), F32),
            pltpu.VMEM((rows // tile_rows, tile_rows, columns), F32),
            pltpu.SemaphoreType.DMA((rows // tile_rows,)),
        ],
        compiler_params=params(16),
        cost_estimate=cost(8 * rows * PANEL * columns, 12 * MIB),
        name="last_solve",
    )(place, parts, *pieces, *prepared, y, *weights, rest)


def swap_with(value, axis, distance):
    size = lax.axis_size(axis)
    return lax.ppermute(value, axis, [(i, i ^ distance) for i in range(size)])


def from_all(value, axis):
    return [value] + [swap_with(value, axis, k) for k in range(1, lax.axis_size(axis))]


def local(vectors, intersection, factor, pivot_rows, pivot_sizes, pivot_diag, pivot_off):
    owners, shares = lax.axis_size("row"), lax.axis_size("vec")
    slots = PANEL // owners // CYC
    panel_rows = slots * CYC
    place = jnp.stack([lax.axis_index("row"), lax.axis_index("vec")]).astype(jnp.int32)
    intersection, factor = (pltpu.with_memory_space_constraint(a, pltpu.HBM) for a in (intersection, factor))

    share, first, last = first_sends(
        place, factor, pltpu.with_memory_space_constraint(vectors, pltpu.HBM), slots, shares
    )
    up = [(i, i + 1) for i in range(owners - 1)]
    down = [(j, i) for i, j in up]
    halo = lax.ppermute(last, "row", up), lax.ppermute(first, "row", down)
    product = band_product_split(intersection, vectors, halo, owners)
    grouped = lax.all_to_all(product, "row", 0, 0, tiled=True).reshape(vectors.shape)

    def share_out(stacked, after):
        across = pass_on(swap_with(stacked, "vec", 2), after)
        return stacked, swap_with(stacked, "vec", 1), across, swap_with(across, "vec", 1)

    tile_rows = PANELS * panel_rows
    pivots = [a.reshape(pivot_diag.shape[0] // DIAG, -1) for a in (pivot_sizes, pivot_diag, pivot_off)]
    keep, swap = own_weights(place, pivots, product)
    direct = from_others(share, keep)
    parts, halved = halve_last(factor, tile_rows, keep)
    (first,) = order_rows(0, [panel_rows], pivot_rows, grouped, halved)
    stacked = stack(place, direct, keep)
    shared = share_out(stacked[0], first)
    prepared = invert_panel(0, place, factor, shared, owners, shares, panel_rows, first, HEAVY)
    rest_rows = factor.shape[0] - tile_rows
    second, rest = order_rows(panel_rows, [tile_rows - panel_rows, rest_rows], pivot_rows, grouped, prepared[2])
    later = share_out(stacked[1], second)
    pieces = from_all(first, "row")
    y, second = first_solve(place, pieces, prepared, factor, second, panel_rows)
    pieces = from_all(second, "row")
    rest = middle_update(rest, y, factor, tile_rows)
    prepared = invert_panel(1, place, factor, later, owners, shares, panel_rows, y, LIGHT)
    return last_solve(place, parts, pieces, prepared, y, (keep, swap), rest, tile_rows)


def padded_2(shard, sides, width):
    for axis, dim in sides:
        devices, length = (lax.axis_size(axis), shard.shape[dim])
        up = [(i, (i + 1) % devices) for i in range(devices - 1)]
        down = [(j, i) for i, j in up]
        last = lax.slice_in_dim(shard, length - width, length, axis=dim)
        leading = lax.slice_in_dim(shard, 0, width, axis=dim)
        before = lax.ppermute(last, axis, up)
        after = lax.ppermute(leading, axis, down)
        shard = jnp.concatenate([before, shard, after], axis=dim)
    return shard


def band_product(intersection, padded, blocks_here):
    band_width = intersection.shape[1] // 3
    band_rows = intersection.reshape(blocks_here, band_width, 3 * band_width)
    result = jnp.zeros((blocks_here, band_width, padded.shape[1]), jnp.float32)
    for offset in range(3):
        window = padded[offset * band_width : offset * band_width + blocks_here * band_width]
        window = window.reshape(blocks_here, band_width, padded.shape[1])
        result = result + jnp.einsum(
            "kij,kjv->kiv",
            band_rows[:, :, offset * band_width : (offset + 1) * band_width],
            window,
            precision=lax.Precision.HIGHEST,
        )
    return result.reshape(blocks_here * band_width, padded.shape[1])


def scale_pivots(values, sizes_here, diag_here, off_here):
    paired = values.reshape(-1, 2, values.shape[1])
    leading = paired[:, 0]
    trailing = paired[:, 1]
    diag_lead = diag_here[0::2][:, None]
    diag_next = diag_here[1::2][:, None]
    coupling = off_here[:, None]
    determ = diag_lead * diag_next - coupling * coupling
    is_pair = (sizes_here == 2)[:, None]
    new_lead = jnp.where(
        is_pair, (diag_next * leading - coupling * trailing) / determ, leading / diag_lead
    )
    new_next = jnp.where(
        is_pair, (diag_lead * trailing - coupling * leading) / determ, trailing / diag_next
    )
    return jnp.stack([new_lead, new_next], axis=1).reshape(values.shape)


def local_many(vectors, intersection, factor, pivot_rows, pivot_sizes, pivot_diag, pivot_off):
    owners = lax.axis_size("row")
    device = lax.axis_index("row")
    rows_here = vectors.shape[0]
    columns = vectors.shape[1]
    slot_count = PANEL // owners // CYC
    panel_rows = slot_count * CYC
    triangles = []
    quarter = PANEL // lax.axis_size("vec")
    column_idx = lax.axis_index("vec")
    for panel_num in range(PANELS):
        local_rows = factor[panel_num * panel_rows : (panel_num + 1) * panel_rows]
        column_part = lax.dynamic_slice_in_dim(
            local_rows, panel_num * PANEL + column_idx * quarter, quarter, 1
        )
        column_part = column_part.reshape(slot_count, 1, CYC, quarter)
        gathered = lax.all_gather(column_part, "row", axis=1, tiled=True)
        triangles.append(lax.all_gather(gathered, "vec", axis=3, tiled=True).reshape(PANEL, PANEL))
    padded = padded_2(vectors, (("row", 0),), BS)
    product = band_product(intersection, padded, rows_here // BS)
    grouped = product.reshape(rows_here // (CYC * owners), owners, CYC, columns)
    regrouped = lax.all_to_all(grouped, "row", split_axis=1, concat_axis=0, tiled=True).reshape(
        rows_here, columns
    )
    current = jnp.take(regrouped, pivot_rows, axis=0)
    outputs = []
    for panel_num in range(PANELS):
        row_first = panel_num * panel_rows
        row_end = row_first + panel_rows
        col_first = panel_num * PANEL
        col_end = col_first + PANEL
        rhs_local = current[row_first:row_end].reshape(slot_count, 1, CYC, columns)
        rhs_all = lax.all_gather(rhs_local, "row", axis=1, tiled=True)
        triangle = triangles[panel_num]
        block_sol = jax.scipy.linalg.solve_triangular(
            triangle, rhs_all.reshape(PANEL, columns), lower=True, unit_diagonal=True
        )
        update = jnp.dot(
            factor[row_end:, col_first:col_end], block_sol, precision=lax.Precision.HIGHEST
        )
        current = jnp.concatenate([current[:row_end], current[row_end:] - update], axis=0)
        scaled = scale_pivots(
            block_sol,
            pivot_sizes[col_first // 2 : col_end // 2],
            pivot_diag[col_first:col_end],
            pivot_off[col_first // 2 : col_end // 2],
        )
        own_rows = lax.dynamic_slice_in_dim(
            scaled.reshape(slot_count, owners, CYC, columns), device, 1, 1
        )
        outputs.append(own_rows.reshape(panel_rows, columns))
    outputs.append(current[PANELS * panel_rows :])
    return jnp.concatenate(outputs, axis=0)


def solution(mesh):
    in_specs = (
        P(("cuts", "row"), "vec"),
        P("row", None),
        P(("cuts", "row"), None),
        P(("cuts", "row")),
        P("cuts"),
        P("cuts"),
        P("cuts"),
    )
    out_specs = P(("cuts", "row"), "vec")
    owners, shares = mesh.shape["row"], mesh.shape["vec"]
    few = owners == 4 and shares == 4 and DIAG == owners * shares * CYC
    body = local if few else local_many
    return jax.shard_map(body, mesh=mesh, in_specs=in_specs, out_specs=out_specs, check_vma=False)
```

```python
import functools

import jax
import jax.numpy as jnp
from jax import lax
from jax.experimental import pallas as pl
from jax.experimental.pallas import tpu as pltpu
from jax.sharding import PartitionSpec as P

BS = 512
PANEL = 1024
PANELS = 2
CYC = 16
DIAG = 256
HALF = 128
MIB = 1024 * 1024
HEAVY = 2**37
LIGHT = 2**30
F32 = jnp.float32
BF16 = jnp.bfloat16


def params(mib):
    return pltpu.CompilerParams(vmem_limit_bytes=mib * MIB)


IN_VMEM = pl.BlockSpec(memory_space=pltpu.VMEM)
IN_SMEM = pl.BlockSpec(memory_space=pltpu.SMEM)
IN_HBM = pl.BlockSpec(memory_space=pltpu.HBM)


def shaped(*shape, dtype=F32):
    return jax.ShapeDtypeStruct(shape, dtype)


def cost(flops, moved):
    return pl.CostEstimate(flops=int(flops), bytes_accessed=int(moved), transcendentals=0)


def split(value):
    high = value.astype(BF16)
    low = (value - high.astype(F32)).astype(BF16)
    return high, low


def side_by_side(value):
    return jnp.concatenate(split(value), axis=1)


def dot(left, right):
    return jnp.dot(left, right, preferred_element_type=F32)


def fold(wide):
    width = wide.shape[1] // 2
    return wide[:, :width] + wide[:, width:]


def times(left, right_wide):
    high, low = split(left)
    return parts_times(high, low, right_wide)


def parts_times(high, low, right_wide):
    return fold(dot(high, right_wide)) + dot(low, right_wide[:, : right_wide.shape[1] // 2])


def small_times(left_wide, right):
    wide = side_by_side(right)
    return fold(dot(left_wide, jnp.concatenate([wide, wide], axis=0)))


def fold_back(run, part, shares):
    return part if run % 2 == 0 else shares - 1 - part


def lower_run(pair, part, shares):
    early = part < shares // 2
    return 2 * pair + jnp.where(early, 1, 0), jnp.where(early, shares - 1 - part, part)


def start_kernel(slots, shares, place_ref, factor_ref, vec_ref, share_ref, first_ref, last_ref, sems):
    part = place_ref[1]
    rows = vec_ref.shape[0]
    copies = [(vec_ref.at[pl.ds(rows - BS, BS)], last_ref), (vec_ref.at[pl.ds(0, BS)], first_ref)]
    runs = PANEL // DIAG

    def source(panel, run, block, column, width):
        row = pl.multiple_of((panel * slots + run * shares + block) * CYC, CYC)
        column = pl.multiple_of(panel * PANEL + column, HALF)
        return factor_ref.at[pl.ds(row, CYC), pl.ds(column, width)]

    for panel in range(PANELS):
        for run in range(runs):
            width = (2 * run + 1) * HALF
            target = share_ref.at[panel, :, pl.ds(run * run * HALF, width)]
            copies.append((source(panel, run, fold_back(run, part, shares), 0, width), target))
        for pair in range(runs // 2):
            run, block = lower_run(pair, part, shares)
            target = share_ref.at[panel, :, pl.ds((runs * runs + pair) * HALF, HALF)]
            copies.append((source(panel, run, block, (2 * run + 1) * HALF, HALF), target))
    started = [pltpu.make_async_copy(a, b, sems.at[i]) for i, (a, b) in enumerate(copies)]
    for copy in started:
        copy.start()
    for copy in started:
        copy.wait()


def first_sends(place, factor, vectors, slots, shares):
    runs = PANEL // DIAG
    edge = shaped(BS, vectors.shape[1])
    return pl.pallas_call(
        functools.partial(start_kernel, slots, shares),
        out_shape=[shaped(PANELS, CYC, (runs * runs + runs // 2) * HALF), edge, edge],
        in_specs=[IN_SMEM, IN_HBM, IN_HBM],
        out_specs=[IN_VMEM] * 3,
        scratch_shapes=[pltpu.SemaphoreType.DMA((PANELS * (runs + runs // 2) + 2,))],
        compiler_params=params(4),
        cost_estimate=cost(0, 4 * MIB),
        name="first_sends",
    )(place, factor, vectors)


def band_kernel(inter_ref, vec_ref, before_ref, after_ref, out_ref, wide_ref):
    tile = pl.program_id(0)
    rows = vec_ref.shape[0]
    tile_rows = inter_ref.shape[0]
    owners = out_ref.shape[0]

    @pl.when(tile == 0)
    def _():
        wide_ref[:BS] = side_by_side(before_ref[...])
        wide_ref[BS : BS + rows] = side_by_side(vec_ref[...])
        wide_ref[BS + rows :] = side_by_side(after_ref[...])

    window = wide_ref[pl.ds(pl.multiple_of(tile * BS, BS), 3 * BS)]
    product = times(inter_ref[...], window)
    groups = tile_rows // (owners * CYC)
    for g in range(groups):
        for owner in range(owners):
            first = (g * owners + owner) * CYC
            out_ref[owner, g * CYC : (g + 1) * CYC] = product[first : first + CYC]


def band_product_split(intersection, vectors, halo, owners):
    rows, columns = vectors.shape
    width = intersection.shape[1]
    tile_rows = BS
    slot_rows = tile_rows // owners
    whole = lambda t: (0, 0)
    return pl.pallas_call(
        band_kernel,
        out_shape=shaped(owners, rows // owners, columns),
        grid=(rows // tile_rows,),
        in_specs=[
            pl.BlockSpec((tile_rows, width), lambda t: (t, 0)),
            pl.BlockSpec((rows, columns), whole),
            pl.BlockSpec((BS, columns), whole),
            pl.BlockSpec((BS, columns), whole),
        ],
        out_specs=pl.BlockSpec((owners, slot_rows, columns), lambda t: (0, t, 0)),
        scratch_shapes=[pltpu.VMEM((rows + 2 * BS, 2 * columns), BF16)],
        compiler_params=params(16),
        cost_estimate=cost(8 * rows * width * columns, 4 * rows * width),
        name="band_product_split",
    )(intersection, vectors, *halo)


def pass_kernel(value_ref, after_ref, out_ref):
    pass


def pass_on(value, after):
    anywhere = pl.BlockSpec(memory_space=pl.ANY)
    return pl.pallas_call(
        pass_kernel,
        out_shape=shaped(*value.shape),
        in_specs=[anywhere, anywhere],
        out_specs=anywhere,
        input_output_aliases={0: 0},
        compiler_params=params(1),
        name="pass_on",
    )(value, after)


def from_others(value, after):
    end = lax.axis_size("row") - 1
    middle = [(i, end - i) for i in range(1, end)]
    across = pass_on(swap_with(value, "row", 2), after)
    near, inner = swap_with(value, "row", 1), lax.ppermute(value, "row", middle)
    outer = lax.ppermute(across, "row", [(i, i ^ 1) for i, _ in middle])
    return near, across, inner, outer


def stack_kernel(place_ref, near_ref, across_ref, inner_ref, outer_ref, after_ref, *out_refs):
    me = place_ref[0]
    end = out_refs[0].shape[0]
    for panel, out_ref in enumerate(out_refs):
        out_ref[0] = near_ref[panel]
        out_ref[1] = across_ref[panel]

    @pl.when((me > 0) & (me < end))
    def _():
        for panel, out_ref in enumerate(out_refs):
            out_ref[2] = inner_ref[panel]

    @pl.when((me == 0) | (me == end))
    def _():
        for panel, out_ref in enumerate(out_refs):
            out_ref[2] = outer_ref[panel]


def stack(place, pieces, after):
    return pl.pallas_call(
        stack_kernel,
        out_shape=[shaped(3, *pieces[0].shape[1:])] * PANELS,
        in_specs=[IN_SMEM] + [IN_VMEM] * 4 + [pl.BlockSpec(memory_space=pl.ANY)],
        out_specs=[IN_VMEM] * PANELS,
        compiler_params=params(4),
        name="stack",
    )(place, *pieces, after)


def invert_kernel(panel, owners, shares, place_ref, after_ref, own_ref, *refs):
    pieces = refs[:shares]
    high_ref, low_ref, inv_high_ref, inv_low_ref, near_ref = refs[shares:]
    runs = PANEL // DIAG
    me, part = place_ref[0], place_ref[1]

    def place_left(run, row_block, values):
        if run:
            rows = pl.ds(pl.multiple_of(row_block * CYC, CYC), CYC)
            high_ref[rows, : run * DIAG], low_ref[rows, : run * DIAG] = split(values)

    for run in range(runs):
        for s in range(shares):
            row_block = (run * shares + s) * owners + me
            rows = slice((run * shares + s) * CYC, (run * shares + s + 1) * CYC)
            place_left(run, row_block, own_ref[panel, rows, : run * DIAG])
            near_ref[row_block] = own_ref[panel, rows, run * DIAG : (run + 1) * DIAG]
    for other in range(1, owners):
        owner = me ^ other
        for turn in range(shares):
            piece = pieces[turn]
            sender = part ^ turn
            for run in range(runs):
                row_block = (run * shares + fold_back(run, sender, shares)) * owners + owner
                first = run * run * HALF
                middle = first + run * DIAG
                place_left(run, row_block, piece[other - 1, :, first:middle])
                near_ref[row_block, :, :HALF] = piece[other - 1, :, middle : middle + HALF]
            for pair in range(runs // 2):
                run, block = lower_run(pair, sender, shares)
                first = (runs * runs + pair) * HALF
                near_ref[(run * shares + block) * owners + owner, :, HALF:] = piece[
                    other - 1, :, first : first + HALF
                ]

    def near(i, side):
        blocks = HALF // CYC
        return near_ref[i * blocks : (i + 1) * blocks, :, side * HALF : (side + 1) * HALF].reshape(HALF, HALF)

    down = lax.broadcasted_iota(jnp.int32, (HALF, HALF), 0)
    along = lax.broadcasted_iota(jnp.int32, (HALF, HALF), 1)
    eye = jnp.where(down == along, 1.0, 0.0).astype(F32)

    def below(size):
        return (down // size == along // size + 1) & ((down // size) % 2 == 1)

    count = PANEL // HALF
    diagonal = [near(i, i % 2) for i in range(count)]
    wides = [side_by_side(d) for d in diagonal]
    inverse = [eye - jnp.where(below(1), d, 0.0) for d in diagonal]
    size = 2
    while size < HALF:
        keep = jnp.where(below(size), 1.0, 0.0).astype(BF16)
        keep = jnp.concatenate([keep, keep], axis=1)
        right = [small_times(wides[i] * keep, inverse[i]) for i in range(count)]
        inverse = [inverse[i] - small_times(side_by_side(inverse[i]), right[i]) for i in range(count)]
        size *= 2
    for run in range(runs):
        first, second = inverse[2 * run], inverse[2 * run + 1]
        right = small_times(side_by_side(near(2 * run + 1, 0)), first)
        corner = -small_times(side_by_side(second), right)
        inv_high_ref[run, :HALF, :HALF], inv_low_ref[run, :HALF, :HALF] = split(first)
        inv_high_ref[run, HALF:, HALF:], inv_low_ref[run, HALF:, HALF:] = split(second)
        inv_high_ref[run, HALF:, :HALF], inv_low_ref[run, HALF:, :HALF] = split(corner)
        empty = jnp.zeros((HALF, HALF), BF16)
        inv_high_ref[run, :HALF, HALF:] = empty
        inv_low_ref[run, :HALF, HALF:] = empty


def invert_panel(panel, place, own, pieces, owners, shares, after, flops):
    groups = PANEL // DIAG
    return pl.pallas_call(
        functools.partial(invert_kernel, panel, owners, shares),
        out_shape=[shaped(PANEL, PANEL, dtype=BF16)] * 2 + [shaped(groups, DIAG, DIAG, dtype=BF16)] * 2,
        in_specs=[IN_SMEM, pl.BlockSpec(memory_space=pl.ANY)] + [IN_VMEM] * (len(pieces) + 1),
        out_specs=[IN_VMEM] * 4,
        scratch_shapes=[
            pltpu.VMEM((PANEL // CYC, CYC, DIAG), F32),
        ],
        compiler_params=params(16),
        cost_estimate=cost(flops, 12 * MIB),
        name="invert_panel",
    )(place, after, own, *pieces)


def order_kernel(first, pivot_ref, grouped_ref, after_ref, *out_refs):
    for out_ref in out_refs:
        pick_rows(pivot_ref, first, grouped_ref, out_ref)
        first += out_ref.shape[0]


def pick_rows(pivot_ref, first, source_ref, target_ref):
    step = 8

    def body(i, _):
        base = i * step
        rows = [source_ref[pl.ds(pivot_ref[first + base + j], 1)] for j in range(step)]
        target_ref[pl.ds(pl.multiple_of(base, step), step)] = jnp.concatenate(rows, axis=0)
        return 0

    lax.fori_loop(0, target_ref.shape[0] // step, body, 0, unroll=4)


def order_rows(first, counts, pivot_rows, grouped, after):
    return pl.pallas_call(
        functools.partial(order_kernel, first),
        out_shape=[shaped(count, grouped.shape[1]) for count in counts],
        in_specs=[IN_SMEM, IN_VMEM, pl.BlockSpec(memory_space=pl.ANY)],
        out_specs=[IN_VMEM] * len(counts),
        compiler_params=params(4),
        cost_estimate=cost(0, 2 * MIB),
        name="order_rows",
    )(pivot_rows, grouped, after)


def solve_into(me, owners, pieces, high_ref, low_ref, inv_high_ref, inv_low_ref, rhs_ref, y_ref, use):
    slots = pieces[0].shape[0] // CYC
    columns = pieces[0].shape[1]
    for k in range(owners):
        for s in range(slots):
            rhs_ref[s * owners + (me ^ k)] = pieces[k][s * CYC : (s + 1) * CYC]
    runs = [slice(k * DIAG, (k + 1) * DIAG) for k in range(PANEL // DIAG)]
    rhs = [rhs_ref[r.start // CYC : r.stop // CYC].reshape(DIAG, columns) for r in runs]

    def take_off(row, k, wide):
        rhs[row] = rhs[row] - parts_times(high_ref[runs[row], runs[k]], low_ref[runs[row], runs[k]], wide)

    wide = None
    for k in range(len(runs)):
        block = parts_times(inv_high_ref[k], inv_low_ref[k], side_by_side(rhs[k]))
        if k:
            for row in range(k + 1, len(runs)):
                take_off(row, k - 1, wide)
            use(k - 1, wide)
        wide = side_by_side(block)
        if k + 1 < len(runs):
            take_off(k + 1, k, wide)
        y_ref[runs[k].start // CYC : runs[k].stop // CYC] = block.reshape(DIAG // CYC, CYC, columns)
    use(len(runs) - 1, wide)


def first_kernel(owners, place_ref, *refs):
    pieces = refs[:owners]
    high, low, inv_high, inv_low, left_ref, current_ref, y_ref, next_ref, rhs_ref = refs[owners:]
    next_ref[...] = current_ref[...]

    def use(k, wide):
        columns = slice(k * DIAG, (k + 1) * DIAG)
        next_ref[...] -= parts_times(left_ref[0, :, columns], left_ref[1, :, columns], wide)

    solve_into(place_ref[0], owners, pieces, high, low, inv_high, inv_low, rhs_ref, y_ref, use)


def first_solve(place, pieces, prepared, left, current):
    owners = len(pieces)
    panel_rows, columns = current.shape
    return pl.pallas_call(
        functools.partial(first_kernel, owners),
        out_shape=[shaped(PANEL // CYC, CYC, columns), shaped(panel_rows, columns)],
        in_specs=[IN_SMEM] + [IN_VMEM] * (owners + 6),
        out_specs=[IN_VMEM] * 2,
        scratch_shapes=[pltpu.VMEM((PANEL // CYC, CYC, columns), F32)],
        compiler_params=params(8),
        cost_estimate=cost(HEAVY, 6 * MIB),
        name="first_solve",
    )(place, *pieces, *prepared, left, current)


def pivot_weights(me, sizes, diag, off):
    pairs, lanes = off.shape[1], diag.shape[1]
    spread = lax.broadcasted_iota(jnp.int32, (pairs, lanes), 1) // 2 == lax.broadcasted_iota(
        jnp.int32, (pairs, lanes), 0
    )
    spread = jnp.where(spread, 1.0, 0.0).astype(F32)
    off = jnp.dot(off, spread, precision=lax.Precision.HIGHEST, preferred_element_type=F32)
    sizes = jnp.dot(sizes.astype(F32), spread, precision=lax.Precision.HIGHEST, preferred_element_type=F32)
    odd = lax.broadcasted_iota(jnp.int32, diag.shape, 1) % 2 == 1
    other = jnp.where(odd, pltpu.roll(diag, 1, 1), pltpu.roll(diag, lanes - 1, 1))
    determ = diag * other - off * off
    is_pair = sizes > 1.5
    keep = jnp.where(is_pair, other / determ, 1.0 / diag)
    swap = jnp.where(is_pair, -off / determ, 0.0)
    turned = []
    for weight in (keep, swap):
        weight = pltpu.roll(weight, lax.rem(lanes - CYC * me, lanes), 1)
        tall = jnp.concatenate([weight] * (HALF // weight.shape[0]), axis=0)
        turned.append(tall.T)
    return turned


def weights_kernel(place_ref, after_ref, sizes_ref, diag_ref, off_ref, keep_ref, swap_ref):
    keep_ref[...], swap_ref[...] = pivot_weights(place_ref[0], sizes_ref[...], diag_ref[...], off_ref[...])


def own_weights(place, pivots, after):
    weight = shaped(pivots[1].shape[1], HALF)
    return pl.pallas_call(
        weights_kernel,
        out_shape=[weight, weight],
        in_specs=[IN_SMEM, pl.BlockSpec(memory_space=pl.ANY)] + [IN_VMEM] * len(pivots),
        out_specs=[IN_VMEM] * 2,
        compiler_params=params(4),
        cost_estimate=cost(HEAVY, 0),
        name="own_weights",
    )(place, after, *pivots)


def halve_kernel(
    tile_rows, factor_ref, after_ref, out_ref, own_ref, next_ref, left_ref, below_ref, parts_ref, in_sems, out_sems,
    own_sems,
):
    tiles = left_ref.shape[0]
    rows = own_ref.shape[1]
    below = pltpu.make_async_copy(factor_ref.at[pl.ds(rows, rows), pl.ds(0, PANEL)], below_ref, own_sems.at[PANELS])
    below.start()
    loads, stores, owns = [], [], []
    for t in range(tiles):
        source = factor_ref.at[pl.ds((t + 1) * tile_rows, tile_rows), pl.ds((PANELS - 1) * PANEL, PANEL)]
        loads.append(pltpu.make_async_copy(source, left_ref.at[t], in_sems.at[t]))
        loads[t].start()
    for panel in range(PANELS):
        source = factor_ref.at[pl.ds(panel * rows, rows), pl.ds(panel * PANEL, PANEL)]
        owns.append(pltpu.make_async_copy(source, own_ref.at[panel], own_sems.at[panel]))
        owns[panel].start()
    below.wait()
    next_ref[0], next_ref[1] = split(below_ref[...])
    for t in range(tiles):
        loads[t].wait()
        parts_ref[t, 0], parts_ref[t, 1] = split(left_ref[t])
        stores.append(pltpu.make_async_copy(parts_ref.at[t], out_ref.at[t], out_sems.at[t]))
        stores[t].start()
    for copy in owns + stores:
        copy.wait()


def halve_last(factor, panel_rows, after):
    tile_rows = PANELS * panel_rows
    tiles = factor.shape[0] // tile_rows - 1
    return pl.pallas_call(
        functools.partial(halve_kernel, tile_rows),
        out_shape=[
            shaped(tiles, 2, tile_rows, PANEL, dtype=BF16),
            shaped(PANELS, panel_rows, PANEL),
            shaped(2, panel_rows, PANEL, dtype=BF16),
        ],
        in_specs=[IN_HBM, pl.BlockSpec(memory_space=pl.ANY)],
        out_specs=[IN_HBM, IN_VMEM, IN_VMEM],
        scratch_shapes=[
            pltpu.VMEM((tiles, tile_rows, PANEL), F32),
            pltpu.VMEM((panel_rows, PANEL), F32),
            pltpu.VMEM((tiles, 2, tile_rows, PANEL), BF16),
            pltpu.SemaphoreType.DMA((tiles,)),
            pltpu.SemaphoreType.DMA((tiles,)),
            pltpu.SemaphoreType.DMA((PANELS + 1,)),
        ],
        compiler_params=params(18),
        cost_estimate=cost(LIGHT, 12 * MIB),
        name="halve_last",
    )(factor, after)


def middle_kernel(tile_rows, factor_ref, rest_ref, y_ref, out_ref, wide_ref, left_ref, sems):
    tiles = left_ref.shape[0]
    loads = []
    for t in range(tiles):
        source = factor_ref.at[pl.ds((t + 1) * tile_rows, tile_rows), pl.ds(0, PANEL)]
        loads.append(pltpu.make_async_copy(source, left_ref.at[t], sems.at[t]))
        loads[t].start()
    wide_ref[...] = side_by_side(y_ref[...].reshape(PANEL, y_ref.shape[2]))
    for t in range(tiles):
        loads[t].wait()
        rows = slice(t * tile_rows, (t + 1) * tile_rows)
        out_ref[rows] = rest_ref[rows] - times(left_ref[t], wide_ref[...])


def middle_update(rest, y, factor, tile_rows):
    rows, columns = rest.shape
    tiles = rows // tile_rows
    return pl.pallas_call(
        functools.partial(middle_kernel, tile_rows),
        out_shape=shaped(rows, columns),
        in_specs=[IN_HBM] + [IN_VMEM] * 2,
        out_specs=IN_VMEM,
        scratch_shapes=[
            pltpu.VMEM((PANEL, 2 * columns), BF16),
            pltpu.VMEM((tiles, tile_rows, PANEL), F32),
            pltpu.SemaphoreType.DMA((tiles,)),
        ],
        compiler_params=params(12),
        cost_estimate=cost(8 * rows * PANEL * columns, 8 * MIB),
        name="middle_update",
    )(factor, rest, y)


def last_kernel(owners, tile_rows, place_ref, left_ref, *refs):
    pieces = refs[:owners]
    high, low, inv_high, inv_low, y_ref, keep_ref, swap_ref, rest_ref = refs[owners : owners + 8]
    out_ref, rhs_ref, second_ref, stage_ref, sems = refs[owners + 8 :]
    me = place_ref[0]
    last = PANEL // DIAG - 1
    stores = []

    def store(t):
        target = out_ref.at[pl.ds(t * tile_rows, tile_rows)]
        stores.append(pltpu.make_async_copy(stage_ref.at[t], target, sems.at[t]))
        stores[-1].start()

    def use(k, wide):
        columns = slice(k * DIAG, (k + 1) * DIAG)
        for t in range(left_ref.shape[0]):
            rows = slice(t * tile_rows, (t + 1) * tile_rows)
            before = stage_ref[t + 1] if k else rest_ref[rows]
            stage_ref[t + 1] = before - parts_times(left_ref[t, 0, :, columns], left_ref[t, 1, :, columns], wide)
            if k == last:
                store(t + 1)

    solve_into(me, owners, pieces, high, low, inv_high, inv_low, rhs_ref, second_ref, use)
    scale_own_rows(me, owners, y_ref, second_ref, keep_ref, swap_ref, stage_ref)
    store(0)
    for copy in stores:
        copy.wait()


def scale_own_rows(me, owners, first_ref, second_ref, keep_ref, swap_ref, stage_ref):
    slots = first_ref.shape[0] // owners
    runs = keep_ref.shape[0] // (owners * CYC)
    for panel, source in enumerate((first_ref, second_ref)):
        for s in range(slots):
            at = panel * slots + s
            rows = source[s * owners + me]
            odd = lax.broadcasted_iota(jnp.int32, rows.shape, 0) % 2 == 1
            other = jnp.where(odd, pltpu.roll(rows, 1, 0), pltpu.roll(rows, CYC - 1, 0))
            first = (at % runs) * owners * CYC
            keep = keep_ref[first : first + CYC, at // runs : at // runs + 1]
            swap = swap_ref[first : first + CYC, at // runs : at // runs + 1]
            mixed = keep * rows + jnp.where(swap != 0, swap * other, 0.0)
            stage_ref[0, at * CYC : (at + 1) * CYC] = mixed


def last_solve(place, parts, pieces, prepared, y, weights, rest, tile_rows):
    owners = len(pieces)
    columns = rest.shape[1]
    rows = rest.shape[0] + tile_rows
    return pl.pallas_call(
        functools.partial(last_kernel, owners, tile_rows),
        out_shape=shaped(rows, columns),
        in_specs=[IN_SMEM] + [IN_VMEM] * (owners + 9),
        out_specs=IN_HBM,
        scratch_shapes=[
            pltpu.VMEM((PANEL // CYC, CYC, columns), F32),
            pltpu.VMEM((PANEL // CYC, CYC, columns), F32),
            pltpu.VMEM((rows // tile_rows, tile_rows, columns), F32),
            pltpu.SemaphoreType.DMA((rows // tile_rows,)),
        ],
        compiler_params=params(16),
        cost_estimate=cost(8 * rows * PANEL * columns, 12 * MIB),
        name="last_solve",
    )(place, parts, *pieces, *prepared, y, *weights, rest)


def swap_with(value, axis, distance):
    size = lax.axis_size(axis)
    return lax.ppermute(value, axis, [(i, i ^ distance) for i in range(size)])


def from_all(value, axis):
    return [value] + [swap_with(value, axis, k) for k in range(1, lax.axis_size(axis))]


def local(vectors, intersection, factor, pivot_rows, pivot_sizes, pivot_diag, pivot_off):
    owners, shares = lax.axis_size("row"), lax.axis_size("vec")
    slots = PANEL // owners // CYC
    panel_rows = slots * CYC
    place = jnp.stack([lax.axis_index("row"), lax.axis_index("vec")]).astype(jnp.int32)
    intersection, factor = (pltpu.with_memory_space_constraint(a, pltpu.HBM) for a in (intersection, factor))

    share, first, last = first_sends(
        place, factor, pltpu.with_memory_space_constraint(vectors, pltpu.HBM), slots, shares
    )
    up = [(i, i + 1) for i in range(owners - 1)]
    down = [(j, i) for i, j in up]
    halo = lax.ppermute(last, "row", up), lax.ppermute(first, "row", down)
    product = band_product_split(intersection, vectors, halo, owners)
    grouped = lax.all_to_all(product, "row", 0, 0, tiled=True).reshape(vectors.shape)

    def share_out(stacked, after):
        across = pass_on(swap_with(stacked, "vec", 2), after)
        return stacked, swap_with(stacked, "vec", 1), across, swap_with(across, "vec", 1)

    tile_rows = PANELS * panel_rows
    pivots = [a.reshape(pivot_diag.shape[0] // DIAG, -1) for a in (pivot_sizes, pivot_diag, pivot_off)]
    keep, swap = own_weights(place, pivots, product)
    direct = from_others(share, keep)
    (first,) = order_rows(0, [panel_rows], pivot_rows, grouped, place)
    parts, own, left = halve_last(factor, panel_rows, keep)
    stacked = stack(place, direct, own)
    shared = share_out(stacked[0], first)
    prepared = invert_panel(0, place, own, shared, owners, shares, first, HEAVY)
    rest_rows = factor.shape[0] - tile_rows
    second, rest = order_rows(panel_rows, [tile_rows - panel_rows, rest_rows], pivot_rows, grouped, prepared[2])
    later = share_out(stacked[1], second)
    pieces = from_all(first, "row")
    y, second = first_solve(place, pieces, prepared, left, second)
    pieces = from_all(second, "row")
    rest = middle_update(rest, y, factor, tile_rows)
    prepared = invert_panel(1, place, own, later, owners, shares, y, LIGHT)
    return last_solve(place, parts, pieces, prepared, y, (keep, swap), rest, tile_rows)


def padded_2(shard, sides, width):
    for axis, dim in sides:
        devices, length = (lax.axis_size(axis), shard.shape[dim])
        up = [(i, (i + 1) % devices) for i in range(devices - 1)]
        down = [(j, i) for i, j in up]
        last = lax.slice_in_dim(shard, length - width, length, axis=dim)
        leading = lax.slice_in_dim(shard, 0, width, axis=dim)
        before = lax.ppermute(last, axis, up)
        after = lax.ppermute(leading, axis, down)
        shard = jnp.concatenate([before, shard, after], axis=dim)
    return shard


def band_product(intersection, padded, blocks_here):
    band_width = intersection.shape[1] // 3
    band_rows = intersection.reshape(blocks_here, band_width, 3 * band_width)
    result = jnp.zeros((blocks_here, band_width, padded.shape[1]), jnp.float32)
    for offset in range(3):
        window = padded[offset * band_width : offset * band_width + blocks_here * band_width]
        window = window.reshape(blocks_here, band_width, padded.shape[1])
        result = result + jnp.einsum(
            "kij,kjv->kiv",
            band_rows[:, :, offset * band_width : (offset + 1) * band_width],
            window,
            precision=lax.Precision.HIGHEST,
        )
    return result.reshape(blocks_here * band_width, padded.shape[1])


def scale_pivots(values, sizes_here, diag_here, off_here):
    paired = values.reshape(-1, 2, values.shape[1])
    leading = paired[:, 0]
    trailing = paired[:, 1]
    diag_lead = diag_here[0::2][:, None]
    diag_next = diag_here[1::2][:, None]
    coupling = off_here[:, None]
    determ = diag_lead * diag_next - coupling * coupling
    is_pair = (sizes_here == 2)[:, None]
    new_lead = jnp.where(
        is_pair, (diag_next * leading - coupling * trailing) / determ, leading / diag_lead
    )
    new_next = jnp.where(
        is_pair, (diag_lead * trailing - coupling * leading) / determ, trailing / diag_next
    )
    return jnp.stack([new_lead, new_next], axis=1).reshape(values.shape)


def local_many(vectors, intersection, factor, pivot_rows, pivot_sizes, pivot_diag, pivot_off):
    owners = lax.axis_size("row")
    device = lax.axis_index("row")
    rows_here = vectors.shape[0]
    columns = vectors.shape[1]
    slot_count = PANEL // owners // CYC
    panel_rows = slot_count * CYC
    triangles = []
    quarter = PANEL // lax.axis_size("vec")
    column_idx = lax.axis_index("vec")
    for panel_num in range(PANELS):
        local_rows = factor[panel_num * panel_rows : (panel_num + 1) * panel_rows]
        column_part = lax.dynamic_slice_in_dim(
            local_rows, panel_num * PANEL + column_idx * quarter, quarter, 1
        )
        column_part = column_part.reshape(slot_count, 1, CYC, quarter)
        gathered = lax.all_gather(column_part, "row", axis=1, tiled=True)
        triangles.append(lax.all_gather(gathered, "vec", axis=3, tiled=True).reshape(PANEL, PANEL))
    padded = padded_2(vectors, (("row", 0),), BS)
    product = band_product(intersection, padded, rows_here // BS)
    grouped = product.reshape(rows_here // (CYC * owners), owners, CYC, columns)
    regrouped = lax.all_to_all(grouped, "row", split_axis=1, concat_axis=0, tiled=True).reshape(
        rows_here, columns
    )
    current = jnp.take(regrouped, pivot_rows, axis=0)
    outputs = []
    for panel_num in range(PANELS):
        row_first = panel_num * panel_rows
        row_end = row_first + panel_rows
        col_first = panel_num * PANEL
        col_end = col_first + PANEL
        rhs_local = current[row_first:row_end].reshape(slot_count, 1, CYC, columns)
        rhs_all = lax.all_gather(rhs_local, "row", axis=1, tiled=True)
        triangle = triangles[panel_num]
        block_sol = jax.scipy.linalg.solve_triangular(
            triangle, rhs_all.reshape(PANEL, columns), lower=True, unit_diagonal=True
        )
        update = jnp.dot(
            factor[row_end:, col_first:col_end], block_sol, precision=lax.Precision.HIGHEST
        )
        current = jnp.concatenate([current[:row_end], current[row_end:] - update], axis=0)
        scaled = scale_pivots(
            block_sol,
            pivot_sizes[col_first // 2 : col_end // 2],
            pivot_diag[col_first:col_end],
            pivot_off[col_first // 2 : col_end // 2],
        )
        own_rows = lax.dynamic_slice_in_dim(
            scaled.reshape(slot_count, owners, CYC, columns), device, 1, 1
        )
        outputs.append(own_rows.reshape(panel_rows, columns))
    outputs.append(current[PANELS * panel_rows :])
    return jnp.concatenate(outputs, axis=0)


def solution(mesh):
    in_specs = (
        P(("cuts", "row"), "vec"),
        P("row", None),
        P(("cuts", "row"), None),
        P(("cuts", "row")),
        P("cuts"),
        P("cuts"),
        P("cuts"),
    )
    out_specs = P(("cuts", "row"), "vec")
    owners, shares = mesh.shape["row"], mesh.shape["vec"]
    few = owners == 4 and shares == 4 and DIAG == owners * shares * CYC
    body = local if few else local_many
    return jax.shard_map(body, mesh=mesh, in_specs=in_specs, out_specs=out_specs, check_vma=False)
```

```python
import functools

import jax
import jax.numpy as jnp
from jax import lax
from jax.experimental import pallas as pl
from jax.experimental.pallas import tpu as pltpu
from jax.sharding import PartitionSpec as P

BS = 512
PANEL = 1024
PANELS = 2
CYC = 16
DIAG = 256
HALF = 128
MIB = 1024 * 1024
HEAVY = 2**37
LIGHT = 2**30
F32 = jnp.float32
BF16 = jnp.bfloat16


def params(mib):
    return pltpu.CompilerParams(vmem_limit_bytes=mib * MIB)


IN_VMEM = pl.BlockSpec(memory_space=pltpu.VMEM)
IN_SMEM = pl.BlockSpec(memory_space=pltpu.SMEM)
IN_HBM = pl.BlockSpec(memory_space=pltpu.HBM)


def shaped(*shape, dtype=F32):
    return jax.ShapeDtypeStruct(shape, dtype)


def cost(flops, moved):
    return pl.CostEstimate(flops=int(flops), bytes_accessed=int(moved), transcendentals=0)


def split(value):
    high = value.astype(BF16)
    low = (value - high.astype(F32)).astype(BF16)
    return high, low


def side_by_side(value):
    return jnp.concatenate(split(value), axis=1)


def dot(left, right):
    return jnp.dot(left, right, preferred_element_type=F32)


def fold(wide):
    width = wide.shape[1] // 2
    return wide[:, :width] + wide[:, width:]


def times(left, right_wide):
    high, low = split(left)
    return parts_times(high, low, right_wide)


def parts_times(high, low, right_wide):
    return fold(dot(high, right_wide)) + dot(low, right_wide[:, : right_wide.shape[1] // 2])


def small_times(left_wide, right):
    wide = side_by_side(right)
    return fold(dot(left_wide, jnp.concatenate([wide, wide], axis=0)))


def fold_back(run, part, shares):
    return part if run % 2 == 0 else shares - 1 - part


def lower_run(pair, part, shares):
    early = part < shares // 2
    return 2 * pair + jnp.where(early, 1, 0), jnp.where(early, shares - 1 - part, part)


def start_kernel(slots, shares, place_ref, factor_ref, vec_ref, share_ref, first_ref, last_ref, sems):
    part = place_ref[1]
    rows = vec_ref.shape[0]
    copies = [(vec_ref.at[pl.ds(rows - BS, BS)], last_ref), (vec_ref.at[pl.ds(0, BS)], first_ref)]
    runs = PANEL // DIAG

    def source(panel, run, block, column, width):
        row = pl.multiple_of((panel * slots + run * shares + block) * CYC, CYC)
        column = pl.multiple_of(panel * PANEL + column, HALF)
        return factor_ref.at[pl.ds(row, CYC), pl.ds(column, width)]

    for panel in range(PANELS):
        for run in range(runs):
            width = (2 * run + 1) * HALF
            target = share_ref.at[panel, :, pl.ds(run * run * HALF, width)]
            copies.append((source(panel, run, fold_back(run, part, shares), 0, width), target))
        for pair in range(runs // 2):
            run, block = lower_run(pair, part, shares)
            target = share_ref.at[panel, :, pl.ds((runs * runs + pair) * HALF, HALF)]
            copies.append((source(panel, run, block, (2 * run + 1) * HALF, HALF), target))
    started = [pltpu.make_async_copy(a, b, sems.at[i]) for i, (a, b) in enumerate(copies)]
    for copy in started:
        copy.start()
    for copy in started:
        copy.wait()


def first_sends(place, factor, vectors, slots, shares):
    runs = PANEL // DIAG
    edge = shaped(BS, vectors.shape[1])
    return pl.pallas_call(
        functools.partial(start_kernel, slots, shares),
        out_shape=[shaped(PANELS, CYC, (runs * runs + runs // 2) * HALF), edge, edge],
        in_specs=[IN_SMEM, IN_HBM, IN_HBM],
        out_specs=[IN_VMEM] * 3,
        scratch_shapes=[pltpu.SemaphoreType.DMA((PANELS * (runs + runs // 2) + 2,))],
        compiler_params=params(4),
        cost_estimate=cost(0, 4 * MIB),
        name="first_sends",
    )(place, factor, vectors)


def band_kernel(inter_ref, vec_ref, after_ref, before_ref, out_ref, wide_ref):
    tile = pl.program_id(0)
    rows = vec_ref.shape[0]
    tile_rows = inter_ref.shape[0]
    owners = out_ref.shape[0]

    @pl.when(tile == 0)
    def _():
        wide_ref[:BS] = side_by_side(before_ref[...])
        wide_ref[BS : BS + rows] = side_by_side(vec_ref[...])
        wide_ref[BS + rows :] = side_by_side(after_ref[...])

    window = wide_ref[pl.ds(pl.multiple_of(tile * BS, BS), 3 * BS)]
    product = times(inter_ref[...], window)
    groups = tile_rows // (owners * CYC)
    for g in range(groups):
        for owner in range(owners):
            first = (g * owners + owner) * CYC
            out_ref[owner, g * CYC : (g + 1) * CYC] = product[first : first + CYC]


def band_product_split(intersection, vectors, halo, owners):
    rows, columns = vectors.shape
    width = intersection.shape[1]
    tile_rows = BS
    slot_rows = tile_rows // owners
    whole = lambda t: (0, 0)
    return pl.pallas_call(
        band_kernel,
        out_shape=shaped(owners, rows // owners, columns),
        grid=(rows // tile_rows,),
        in_specs=[
            pl.BlockSpec((tile_rows, width), lambda t: (t, 0)),
            pl.BlockSpec((rows, columns), whole),
            pl.BlockSpec((BS, columns), whole),
            pl.BlockSpec((BS, columns), whole),
        ],
        out_specs=pl.BlockSpec((owners, slot_rows, columns), lambda t: (0, t, 0)),
        scratch_shapes=[pltpu.VMEM((rows + 2 * BS, 2 * columns), BF16)],
        compiler_params=params(16),
        cost_estimate=cost(8 * rows * width * columns, 4 * rows * width),
        name="band_product_split",
    )(intersection, vectors, *halo)


def pass_kernel(value_ref, after_ref, out_ref):
    pass


def pass_on(value, after):
    anywhere = pl.BlockSpec(memory_space=pl.ANY)
    return pl.pallas_call(
        pass_kernel,
        out_shape=shaped(*value.shape),
        in_specs=[anywhere, anywhere],
        out_specs=anywhere,
        input_output_aliases={0: 0},
        compiler_params=params(1),
        name="pass_on",
    )(value, after)


def from_others(value, after):
    end = lax.axis_size("row") - 1
    middle = [(i, end - i) for i in range(1, end)]
    across = pass_on(swap_with(value, "row", 2), after)
    near, inner = swap_with(value, "row", 1), lax.ppermute(value, "row", middle)
    outer = lax.ppermute(across, "row", [(i, i ^ 1) for i, _ in middle])
    return near, across, inner, outer


def stack_kernel(place_ref, near_ref, across_ref, inner_ref, outer_ref, after_ref, *out_refs):
    me = place_ref[0]
    end = out_refs[0].shape[0]
    for panel, out_ref in enumerate(out_refs):
        out_ref[0] = near_ref[panel]
        out_ref[1] = across_ref[panel]

    @pl.when((me > 0) & (me < end))
    def _():
        for panel, out_ref in enumerate(out_refs):
            out_ref[2] = inner_ref[panel]

    @pl.when((me == 0) | (me == end))
    def _():
        for panel, out_ref in enumerate(out_refs):
            out_ref[2] = outer_ref[panel]


def stack(place, pieces, after):
    return pl.pallas_call(
        stack_kernel,
        out_shape=[shaped(3, *pieces[0].shape[1:])] * PANELS,
        in_specs=[IN_SMEM] + [IN_VMEM] * 4 + [pl.BlockSpec(memory_space=pl.ANY)],
        out_specs=[IN_VMEM] * PANELS,
        compiler_params=params(4),
        name="stack",
    )(place, *pieces, after)


def invert_kernel(panel, owners, shares, place_ref, after_ref, own_ref, *refs):
    pieces = refs[:shares]
    high_ref, low_ref, inv_high_ref, inv_low_ref, near_ref = refs[shares:]
    runs = PANEL // DIAG
    me, part = place_ref[0], place_ref[1]

    def place_left(run, row_block, values):
        if run:
            rows = pl.ds(pl.multiple_of(row_block * CYC, CYC), CYC)
            high_ref[rows, : run * DIAG], low_ref[rows, : run * DIAG] = split(values)

    for run in range(runs):
        for s in range(shares):
            row_block = (run * shares + s) * owners + me
            rows = slice((run * shares + s) * CYC, (run * shares + s + 1) * CYC)
            place_left(run, row_block, own_ref[panel, rows, : run * DIAG])
            near_ref[row_block] = own_ref[panel, rows, run * DIAG : (run + 1) * DIAG]
    for other in range(1, owners):
        owner = me ^ other
        for turn in range(shares):
            piece = pieces[turn]
            sender = part ^ turn
            for run in range(runs):
                row_block = (run * shares + fold_back(run, sender, shares)) * owners + owner
                first = run * run * HALF
                middle = first + run * DIAG
                place_left(run, row_block, piece[other - 1, :, first:middle])
                near_ref[row_block, :, :HALF] = piece[other - 1, :, middle : middle + HALF]
            for pair in range(runs // 2):
                run, block = lower_run(pair, sender, shares)
                first = (runs * runs + pair) * HALF
                near_ref[(run * shares + block) * owners + owner, :, HALF:] = piece[
                    other - 1, :, first : first + HALF
                ]

    def near(i, side):
        blocks = HALF // CYC
        return near_ref[i * blocks : (i + 1) * blocks, :, side * HALF : (side + 1) * HALF].reshape(HALF, HALF)

    down = lax.broadcasted_iota(jnp.int32, (HALF, HALF), 0)
    along = lax.broadcasted_iota(jnp.int32, (HALF, HALF), 1)
    eye = jnp.where(down == along, 1.0, 0.0).astype(F32)

    def below(size):
        return (down // size == along // size + 1) & ((down // size) % 2 == 1)

    count = PANEL // HALF
    diagonal = [near(i, i % 2) for i in range(count)]
    wides = [side_by_side(d) for d in diagonal]
    inverse = [eye - jnp.where(below(1), d, 0.0) for d in diagonal]
    size = 2
    while size < HALF:
        keep = jnp.where(below(size), 1.0, 0.0).astype(BF16)
        keep = jnp.concatenate([keep, keep], axis=1)
        right = [small_times(wides[i] * keep, inverse[i]) for i in range(count)]
        inverse = [inverse[i] - small_times(side_by_side(inverse[i]), right[i]) for i in range(count)]
        size *= 2
    for run in range(runs):
        first, second = inverse[2 * run], inverse[2 * run + 1]
        right = small_times(side_by_side(near(2 * run + 1, 0)), first)
        corner = -small_times(side_by_side(second), right)
        inv_high_ref[run, :HALF, :HALF], inv_low_ref[run, :HALF, :HALF] = split(first)
        inv_high_ref[run, HALF:, HALF:], inv_low_ref[run, HALF:, HALF:] = split(second)
        inv_high_ref[run, HALF:, :HALF], inv_low_ref[run, HALF:, :HALF] = split(corner)
        empty = jnp.zeros((HALF, HALF), BF16)
        inv_high_ref[run, :HALF, HALF:] = empty
        inv_low_ref[run, :HALF, HALF:] = empty


def invert_panel(panel, place, own, pieces, owners, shares, after, flops):
    groups = PANEL // DIAG
    return pl.pallas_call(
        functools.partial(invert_kernel, panel, owners, shares),
        out_shape=[shaped(PANEL, PANEL, dtype=BF16)] * 2 + [shaped(groups, DIAG, DIAG, dtype=BF16)] * 2,
        in_specs=[IN_SMEM, pl.BlockSpec(memory_space=pl.ANY)] + [IN_VMEM] * (len(pieces) + 1),
        out_specs=[IN_VMEM] * 4,
        scratch_shapes=[
            pltpu.VMEM((PANEL // CYC, CYC, DIAG), F32),
        ],
        compiler_params=params(16),
        cost_estimate=cost(flops, 12 * MIB),
        name="invert_panel",
    )(place, after, own, *pieces)


def order_kernel(first, pivot_ref, grouped_ref, after_ref, *out_refs):
    for out_ref in out_refs:
        pick_rows(pivot_ref, first, grouped_ref, out_ref)
        first += out_ref.shape[0]


def pick_rows(pivot_ref, first, source_ref, target_ref):
    step = 8

    def body(i, _):
        base = i * step
        rows = [source_ref[pl.ds(pivot_ref[first + base + j], 1)] for j in range(step)]
        target_ref[pl.ds(pl.multiple_of(base, step), step)] = jnp.concatenate(rows, axis=0)
        return 0

    lax.fori_loop(0, target_ref.shape[0] // step, body, 0, unroll=4)


def order_rows(first, counts, pivot_rows, grouped, after):
    return pl.pallas_call(
        functools.partial(order_kernel, first),
        out_shape=[shaped(count, grouped.shape[1]) for count in counts],
        in_specs=[IN_SMEM, IN_VMEM, pl.BlockSpec(memory_space=pl.ANY)],
        out_specs=[IN_VMEM] * len(counts),
        compiler_params=params(4),
        cost_estimate=cost(0, 2 * MIB),
        name="order_rows",
    )(pivot_rows, grouped, after)


def solve_into(me, owners, pieces, high_ref, low_ref, inv_high_ref, inv_low_ref, rhs_ref, y_ref, use):
    slots = pieces[0].shape[0] // CYC
    columns = pieces[0].shape[1]
    for piece, distance in zip(pieces, (0, *far_first(owners))):
        for s in range(slots):
            rhs_ref[s * owners + (me ^ distance)] = piece[s * CYC : (s + 1) * CYC]
    runs = [slice(k * DIAG, (k + 1) * DIAG) for k in range(PANEL // DIAG)]
    rhs = [rhs_ref[r.start // CYC : r.stop // CYC].reshape(DIAG, columns) for r in runs]

    def take_off(row, k, wide):
        rhs[row] = rhs[row] - parts_times(high_ref[runs[row], runs[k]], low_ref[runs[row], runs[k]], wide)

    wide = None
    for k in range(len(runs)):
        block = parts_times(inv_high_ref[k], inv_low_ref[k], side_by_side(rhs[k]))
        if k:
            for row in range(k + 1, len(runs)):
                take_off(row, k - 1, wide)
            use(k - 1, wide)
        wide = side_by_side(block)
        if k + 1 < len(runs):
            take_off(k + 1, k, wide)
        y_ref[runs[k].start // CYC : runs[k].stop // CYC] = block.reshape(DIAG // CYC, CYC, columns)
    use(len(runs) - 1, wide)


def first_kernel(owners, place_ref, *refs):
    pieces = refs[:owners]
    high, low, inv_high, inv_low, left_ref, current_ref, y_ref, next_ref, rhs_ref = refs[owners:]
    next_ref[...] = current_ref[...]

    def use(k, wide):
        columns = slice(k * DIAG, (k + 1) * DIAG)
        next_ref[...] -= parts_times(left_ref[0, :, columns], left_ref[1, :, columns], wide)

    solve_into(place_ref[0], owners, pieces, high, low, inv_high, inv_low, rhs_ref, y_ref, use)


def first_solve(place, pieces, prepared, left, current):
    owners = len(pieces)
    panel_rows, columns = current.shape
    return pl.pallas_call(
        functools.partial(first_kernel, owners),
        out_shape=[shaped(PANEL // CYC, CYC, columns), shaped(panel_rows, columns)],
        in_specs=[IN_SMEM] + [IN_VMEM] * (owners + 6),
        out_specs=[IN_VMEM] * 2,
        scratch_shapes=[pltpu.VMEM((PANEL // CYC, CYC, columns), F32)],
        compiler_params=params(8),
        cost_estimate=cost(HEAVY, 6 * MIB),
        name="first_solve",
    )(place, *pieces, *prepared, left, current)


def pivot_weights(me, sizes, diag, off):
    pairs, lanes = off.shape[1], diag.shape[1]
    spread = lax.broadcasted_iota(jnp.int32, (pairs, lanes), 1) // 2 == lax.broadcasted_iota(
        jnp.int32, (pairs, lanes), 0
    )
    spread = jnp.where(spread, 1.0, 0.0).astype(F32)
    off = jnp.dot(off, spread, precision=lax.Precision.HIGHEST, preferred_element_type=F32)
    sizes = jnp.dot(sizes.astype(F32), spread, precision=lax.Precision.HIGHEST, preferred_element_type=F32)
    odd = lax.broadcasted_iota(jnp.int32, diag.shape, 1) % 2 == 1
    other = jnp.where(odd, pltpu.roll(diag, 1, 1), pltpu.roll(diag, lanes - 1, 1))
    determ = diag * other - off * off
    is_pair = sizes > 1.5
    keep = jnp.where(is_pair, other / determ, 1.0 / diag)
    swap = jnp.where(is_pair, -off / determ, 0.0)
    turned = []
    for weight in (keep, swap):
        weight = pltpu.roll(weight, lax.rem(lanes - CYC * me, lanes), 1)
        tall = jnp.concatenate([weight] * (HALF // weight.shape[0]), axis=0)
        turned.append(tall.T)
    return turned


def weights_kernel(place_ref, after_ref, sizes_ref, diag_ref, off_ref, keep_ref, swap_ref):
    keep_ref[...], swap_ref[...] = pivot_weights(place_ref[0], sizes_ref[...], diag_ref[...], off_ref[...])


def own_weights(place, pivots, after):
    weight = shaped(pivots[1].shape[1], HALF)
    return pl.pallas_call(
        weights_kernel,
        out_shape=[weight, weight],
        in_specs=[IN_SMEM, pl.BlockSpec(memory_space=pl.ANY)] + [IN_VMEM] * len(pivots),
        out_specs=[IN_VMEM] * 2,
        compiler_params=params(4),
        cost_estimate=cost(HEAVY, 0),
        name="own_weights",
    )(place, after, *pivots)


def halve_kernel(
    tile_rows, factor_ref, after_ref, out_ref, own_ref, next_ref, left_ref, below_ref, parts_ref, in_sems, out_sems,
    own_sems,
):
    tiles = left_ref.shape[0]
    rows = own_ref.shape[1]
    below = pltpu.make_async_copy(factor_ref.at[pl.ds(rows, rows), pl.ds(0, PANEL)], below_ref, own_sems.at[PANELS])
    below.start()
    loads, stores, owns = [], [], []
    for t in range(tiles):
        source = factor_ref.at[pl.ds((t + 1) * tile_rows, tile_rows), pl.ds((PANELS - 1) * PANEL, PANEL)]
        loads.append(pltpu.make_async_copy(source, left_ref.at[t], in_sems.at[t]))
        loads[t].start()
    for panel in range(PANELS):
        source = factor_ref.at[pl.ds(panel * rows, rows), pl.ds(panel * PANEL, PANEL)]
        owns.append(pltpu.make_async_copy(source, own_ref.at[panel], own_sems.at[panel]))
        owns[panel].start()
    below.wait()
    next_ref[0], next_ref[1] = split(below_ref[...])
    for t in range(tiles):
        loads[t].wait()
        parts_ref[t, 0], parts_ref[t, 1] = split(left_ref[t])
        stores.append(pltpu.make_async_copy(parts_ref.at[t], out_ref.at[t], out_sems.at[t]))
        stores[t].start()
    for copy in owns + stores:
        copy.wait()


def halve_last(factor, panel_rows, after):
    tile_rows = PANELS * panel_rows
    tiles = factor.shape[0] // tile_rows - 1
    return pl.pallas_call(
        functools.partial(halve_kernel, tile_rows),
        out_shape=[
            shaped(tiles, 2, tile_rows, PANEL, dtype=BF16),
            shaped(PANELS, panel_rows, PANEL),
            shaped(2, panel_rows, PANEL, dtype=BF16),
        ],
        in_specs=[IN_HBM, pl.BlockSpec(memory_space=pl.ANY)],
        out_specs=[IN_HBM, IN_VMEM, IN_VMEM],
        scratch_shapes=[
            pltpu.VMEM((tiles, tile_rows, PANEL), F32),
            pltpu.VMEM((panel_rows, PANEL), F32),
            pltpu.VMEM((tiles, 2, tile_rows, PANEL), BF16),
            pltpu.SemaphoreType.DMA((tiles,)),
            pltpu.SemaphoreType.DMA((tiles,)),
            pltpu.SemaphoreType.DMA((PANELS + 1,)),
        ],
        compiler_params=params(18),
        cost_estimate=cost(LIGHT, 12 * MIB),
        name="halve_last",
    )(factor, after)


def middle_kernel(tile_rows, factor_ref, rest_ref, y_ref, out_ref, wide_ref, left_ref, sems):
    tiles = left_ref.shape[0]
    loads = []
    for t in range(tiles):
        source = factor_ref.at[pl.ds((t + 1) * tile_rows, tile_rows), pl.ds(0, PANEL)]
        loads.append(pltpu.make_async_copy(source, left_ref.at[t], sems.at[t]))
        loads[t].start()
    wide_ref[...] = side_by_side(y_ref[...].reshape(PANEL, y_ref.shape[2]))
    for t in range(tiles):
        loads[t].wait()
        rows = slice(t * tile_rows, (t + 1) * tile_rows)
        out_ref[rows] = rest_ref[rows] - times(left_ref[t], wide_ref[...])


def middle_update(rest, y, factor, tile_rows):
    rows, columns = rest.shape
    tiles = rows // tile_rows
    return pl.pallas_call(
        functools.partial(middle_kernel, tile_rows),
        out_shape=shaped(rows, columns),
        in_specs=[IN_HBM] + [IN_VMEM] * 2,
        out_specs=IN_VMEM,
        scratch_shapes=[
            pltpu.VMEM((PANEL, 2 * columns), BF16),
            pltpu.VMEM((tiles, tile_rows, PANEL), F32),
            pltpu.SemaphoreType.DMA((tiles,)),
        ],
        compiler_params=params(12),
        cost_estimate=cost(8 * rows * PANEL * columns, 8 * MIB),
        name="middle_update",
    )(factor, rest, y)


def last_kernel(owners, tile_rows, place_ref, left_ref, *refs):
    pieces = refs[:owners]
    high, low, inv_high, inv_low, y_ref, keep_ref, swap_ref, rest_ref = refs[owners : owners + 8]
    out_ref, rhs_ref, second_ref, stage_ref, sems = refs[owners + 8 :]
    me = place_ref[0]
    last = PANEL // DIAG - 1
    stores = []

    def store(t):
        target = out_ref.at[pl.ds(t * tile_rows, tile_rows)]
        stores.append(pltpu.make_async_copy(stage_ref.at[t], target, sems.at[t]))
        stores[-1].start()

    def use(k, wide):
        columns = slice(k * DIAG, (k + 1) * DIAG)
        for t in range(left_ref.shape[0]):
            rows = slice(t * tile_rows, (t + 1) * tile_rows)
            before = stage_ref[t + 1] if k else rest_ref[rows]
            stage_ref[t + 1] = before - parts_times(left_ref[t, 0, :, columns], left_ref[t, 1, :, columns], wide)
            if k == last:
                store(t + 1)

    solve_into(me, owners, pieces, high, low, inv_high, inv_low, rhs_ref, second_ref, use)
    scale_own_rows(me, owners, y_ref, second_ref, keep_ref, swap_ref, stage_ref)
    store(0)
    for copy in stores:
        copy.wait()


def scale_own_rows(me, owners, first_ref, second_ref, keep_ref, swap_ref, stage_ref):
    slots = first_ref.shape[0] // owners
    runs = keep_ref.shape[0] // (owners * CYC)
    for panel, source in enumerate((first_ref, second_ref)):
        for s in range(slots):
            at = panel * slots + s
            rows = source[s * owners + me]
            odd = lax.broadcasted_iota(jnp.int32, rows.shape, 0) % 2 == 1
            other = jnp.where(odd, pltpu.roll(rows, 1, 0), pltpu.roll(rows, CYC - 1, 0))
            first = (at % runs) * owners * CYC
            keep = keep_ref[first : first + CYC, at // runs : at // runs + 1]
            swap = swap_ref[first : first + CYC, at // runs : at // runs + 1]
            mixed = keep * rows + jnp.where(swap != 0, swap * other, 0.0)
            stage_ref[0, at * CYC : (at + 1) * CYC] = mixed


def last_solve(place, parts, pieces, prepared, y, weights, rest, tile_rows):
    owners = len(pieces)
    columns = rest.shape[1]
    rows = rest.shape[0] + tile_rows
    return pl.pallas_call(
        functools.partial(last_kernel, owners, tile_rows),
        out_shape=shaped(rows, columns),
        in_specs=[IN_SMEM] + [IN_VMEM] * (owners + 9),
        out_specs=IN_HBM,
        scratch_shapes=[
            pltpu.VMEM((PANEL // CYC, CYC, columns), F32),
            pltpu.VMEM((PANEL // CYC, CYC, columns), F32),
            pltpu.VMEM((rows // tile_rows, tile_rows, columns), F32),
            pltpu.SemaphoreType.DMA((rows // tile_rows,)),
        ],
        compiler_params=params(16),
        cost_estimate=cost(8 * rows * PANEL * columns, 12 * MIB),
        name="last_solve",
    )(place, parts, *pieces, *prepared, y, *weights, rest)


def swap_with(value, axis, distance):
    size = lax.axis_size(axis)
    return lax.ppermute(value, axis, [(i, i ^ distance) for i in range(size)])


def far_first(owners):
    return [*range(2, owners), 1]


def from_all(value, axis):
    return [value] + [swap_with(value, axis, k) for k in far_first(lax.axis_size(axis))]


def local(vectors, intersection, factor, pivot_rows, pivot_sizes, pivot_diag, pivot_off):
    owners, shares = lax.axis_size("row"), lax.axis_size("vec")
    slots = PANEL // owners // CYC
    panel_rows = slots * CYC
    place = jnp.stack([lax.axis_index("row"), lax.axis_index("vec")]).astype(jnp.int32)
    vectors, intersection, factor = (
        pltpu.with_memory_space_constraint(a, pltpu.HBM) for a in (vectors, intersection, factor)
    )

    share, first, last = first_sends(place, factor, vectors, slots, shares)
    up = [(i, i + 1) for i in range(owners - 1)]
    down = [(j, i) for i, j in up]
    halo = lax.ppermute(first, "row", down), lax.ppermute(last, "row", up)
    product = band_product_split(intersection, vectors, halo, owners)
    grouped = lax.all_to_all(product, "row", 0, 0, tiled=True).reshape(vectors.shape)

    def share_out(stacked, after):
        across = pass_on(swap_with(stacked, "vec", 2), after)
        return stacked, swap_with(stacked, "vec", 1), across, swap_with(across, "vec", 1)

    tile_rows = PANELS * panel_rows
    pivots = [a.reshape(pivot_diag.shape[0] // DIAG, -1) for a in (pivot_sizes, pivot_diag, pivot_off)]
    keep, swap = own_weights(place, pivots, product)
    direct = from_others(share, keep)
    (first,) = order_rows(0, [panel_rows], pivot_rows, grouped, place)
    parts, own, left = halve_last(factor, panel_rows, keep)
    stacked = stack(place, direct, own)
    shared = share_out(stacked[0], first)
    prepared = invert_panel(0, place, own, shared, owners, shares, first, HEAVY)
    rest_rows = factor.shape[0] - tile_rows
    second, rest = order_rows(panel_rows, [tile_rows - panel_rows, rest_rows], pivot_rows, grouped, prepared[2])
    later = share_out(stacked[1], second)
    pieces = from_all(first, "row")
    y, second = first_solve(place, pieces, prepared, left, second)
    pieces = from_all(second, "row")
    rest = middle_update(rest, y, factor, tile_rows)
    prepared = invert_panel(1, place, own, later, owners, shares, y, LIGHT)
    return last_solve(place, parts, pieces, prepared, y, (keep, swap), rest, tile_rows)


def padded_2(shard, sides, width):
    for axis, dim in sides:
        devices, length = (lax.axis_size(axis), shard.shape[dim])
        up = [(i, (i + 1) % devices) for i in range(devices - 1)]
        down = [(j, i) for i, j in up]
        last = lax.slice_in_dim(shard, length - width, length, axis=dim)
        leading = lax.slice_in_dim(shard, 0, width, axis=dim)
        before = lax.ppermute(last, axis, up)
        after = lax.ppermute(leading, axis, down)
        shard = jnp.concatenate([before, shard, after], axis=dim)
    return shard


def band_product(intersection, padded, blocks_here):
    band_width = intersection.shape[1] // 3
    band_rows = intersection.reshape(blocks_here, band_width, 3 * band_width)
    result = jnp.zeros((blocks_here, band_width, padded.shape[1]), jnp.float32)
    for offset in range(3):
        window = padded[offset * band_width : offset * band_width + blocks_here * band_width]
        window = window.reshape(blocks_here, band_width, padded.shape[1])
        result = result + jnp.einsum(
            "kij,kjv->kiv",
            band_rows[:, :, offset * band_width : (offset + 1) * band_width],
            window,
            precision=lax.Precision.HIGHEST,
        )
    return result.reshape(blocks_here * band_width, padded.shape[1])


def scale_pivots(values, sizes_here, diag_here, off_here):
    paired = values.reshape(-1, 2, values.shape[1])
    leading = paired[:, 0]
    trailing = paired[:, 1]
    diag_lead = diag_here[0::2][:, None]
    diag_next = diag_here[1::2][:, None]
    coupling = off_here[:, None]
    determ = diag_lead * diag_next - coupling * coupling
    is_pair = (sizes_here == 2)[:, None]
    new_lead = jnp.where(
        is_pair, (diag_next * leading - coupling * trailing) / determ, leading / diag_lead
    )
    new_next = jnp.where(
        is_pair, (diag_lead * trailing - coupling * leading) / determ, trailing / diag_next
    )
    return jnp.stack([new_lead, new_next], axis=1).reshape(values.shape)


def local_many(vectors, intersection, factor, pivot_rows, pivot_sizes, pivot_diag, pivot_off):
    owners = lax.axis_size("row")
    device = lax.axis_index("row")
    rows_here = vectors.shape[0]
    columns = vectors.shape[1]
    slot_count = PANEL // owners // CYC
    panel_rows = slot_count * CYC
    triangles = []
    quarter = PANEL // lax.axis_size("vec")
    column_idx = lax.axis_index("vec")
    for panel_num in range(PANELS):
        local_rows = factor[panel_num * panel_rows : (panel_num + 1) * panel_rows]
        column_part = lax.dynamic_slice_in_dim(
            local_rows, panel_num * PANEL + column_idx * quarter, quarter, 1
        )
        column_part = column_part.reshape(slot_count, 1, CYC, quarter)
        gathered = lax.all_gather(column_part, "row", axis=1, tiled=True)
        triangles.append(lax.all_gather(gathered, "vec", axis=3, tiled=True).reshape(PANEL, PANEL))
    padded = padded_2(vectors, (("row", 0),), BS)
    product = band_product(intersection, padded, rows_here // BS)
    grouped = product.reshape(rows_here // (CYC * owners), owners, CYC, columns)
    regrouped = lax.all_to_all(grouped, "row", split_axis=1, concat_axis=0, tiled=True).reshape(
        rows_here, columns
    )
    current = jnp.take(regrouped, pivot_rows, axis=0)
    outputs = []
    for panel_num in range(PANELS):
        row_first = panel_num * panel_rows
        row_end = row_first + panel_rows
        col_first = panel_num * PANEL
        col_end = col_first + PANEL
        rhs_local = current[row_first:row_end].reshape(slot_count, 1, CYC, columns)
        rhs_all = lax.all_gather(rhs_local, "row", axis=1, tiled=True)
        triangle = triangles[panel_num]
        block_sol = jax.scipy.linalg.solve_triangular(
            triangle, rhs_all.reshape(PANEL, columns), lower=True, unit_diagonal=True
        )
        update = jnp.dot(
            factor[row_end:, col_first:col_end], block_sol, precision=lax.Precision.HIGHEST
        )
        current = jnp.concatenate([current[:row_end], current[row_end:] - update], axis=0)
        scaled = scale_pivots(
            block_sol,
            pivot_sizes[col_first // 2 : col_end // 2],
            pivot_diag[col_first:col_end],
            pivot_off[col_first // 2 : col_end // 2],
        )
        own_rows = lax.dynamic_slice_in_dim(
            scaled.reshape(slot_count, owners, CYC, columns), device, 1, 1
        )
        outputs.append(own_rows.reshape(panel_rows, columns))
    outputs.append(current[PANELS * panel_rows :])
    return jnp.concatenate(outputs, axis=0)


def solution(mesh):
    in_specs = (
        P(("cuts", "row"), "vec"),
        P("row", None),
        P(("cuts", "row"), None),
        P(("cuts", "row")),
        P("cuts"),
        P("cuts"),
        P("cuts"),
    )
    out_specs = P(("cuts", "row"), "vec")
    owners, shares = mesh.shape["row"], mesh.shape["vec"]
    few = owners == 4 and shares == 4 and DIAG == owners * shares * CYC
    body = local if few else local_many
    return jax.shard_map(body, mesh=mesh, in_specs=in_specs, out_specs=out_specs, check_vma=False)
```

```python
import functools

import jax
import jax.numpy as jnp
from jax import lax
from jax.experimental import pallas as pl
from jax.experimental.pallas import tpu as pltpu
from jax.sharding import PartitionSpec as P

BS = 512
PANEL = 1024
PANELS = 2
CYC = 16
DIAG = 256
HALF = 128
MIB = 1024 * 1024
HEAVY = 2**37
LIGHT = 2**30
F32 = jnp.float32
BF16 = jnp.bfloat16


def params(mib):
    return pltpu.CompilerParams(vmem_limit_bytes=mib * MIB)


IN_VMEM = pl.BlockSpec(memory_space=pltpu.VMEM)
IN_SMEM = pl.BlockSpec(memory_space=pltpu.SMEM)
IN_HBM = pl.BlockSpec(memory_space=pltpu.HBM)


def shaped(*shape, dtype=F32):
    return jax.ShapeDtypeStruct(shape, dtype)


def cost(flops, moved):
    return pl.CostEstimate(flops=int(flops), bytes_accessed=int(moved), transcendentals=0)


def split(value):
    high = value.astype(BF16)
    low = (value - high.astype(F32)).astype(BF16)
    return high, low


def side_by_side(value):
    return jnp.concatenate(split(value), axis=1)


def dot(left, right):
    return jnp.dot(left, right, preferred_element_type=F32)


def fold(wide):
    width = wide.shape[1] // 2
    return wide[:, :width] + wide[:, width:]


def times(left, right_wide):
    high, low = split(left)
    return parts_times(high, low, right_wide)


def parts_times(high, low, right_wide):
    return fold(dot(high, right_wide)) + dot(low, right_wide[:, : right_wide.shape[1] // 2])


def small_times(left_wide, right):
    wide = side_by_side(right)
    return fold(dot(left_wide, jnp.concatenate([wide, wide], axis=0)))


def fold_back(run, part, shares):
    return part if run % 2 == 0 else shares - 1 - part


def lower_run(pair, part, shares):
    early = part < shares // 2
    return 2 * pair + jnp.where(early, 1, 0), jnp.where(early, shares - 1 - part, part)


def start_kernel(slots, shares, place_ref, factor_ref, vec_ref, share_ref, first_ref, last_ref, sems):
    part = place_ref[1]
    rows = vec_ref.shape[0]
    copies = [(vec_ref.at[pl.ds(rows - BS, BS)], last_ref), (vec_ref.at[pl.ds(0, BS)], first_ref)]
    runs = PANEL // DIAG

    def source(panel, run, block, column, width):
        row = pl.multiple_of((panel * slots + run * shares + block) * CYC, CYC)
        column = pl.multiple_of(panel * PANEL + column, HALF)
        return factor_ref.at[pl.ds(row, CYC), pl.ds(column, width)]

    for panel in range(PANELS):
        for run in range(runs):
            width = (2 * run + 1) * HALF
            target = share_ref.at[panel, :, pl.ds(run * run * HALF, width)]
            copies.append((source(panel, run, fold_back(run, part, shares), 0, width), target))
        for pair in range(runs // 2):
            run, block = lower_run(pair, part, shares)
            target = share_ref.at[panel, :, pl.ds((runs * runs + pair) * HALF, HALF)]
            copies.append((source(panel, run, block, (2 * run + 1) * HALF, HALF), target))
    started = [pltpu.make_async_copy(a, b, sems.at[i]) for i, (a, b) in enumerate(copies)]
    for copy in started:
        copy.start()
    for copy in started:
        copy.wait()


def first_sends(place, factor, vectors, slots, shares):
    runs = PANEL // DIAG
    edge = shaped(BS, vectors.shape[1])
    return pl.pallas_call(
        functools.partial(start_kernel, slots, shares),
        out_shape=[shaped(PANELS, CYC, (runs * runs + runs // 2) * HALF), edge, edge],
        in_specs=[IN_SMEM, IN_HBM, IN_HBM],
        out_specs=[IN_VMEM] * 3,
        scratch_shapes=[pltpu.SemaphoreType.DMA((PANELS * (runs + runs // 2) + 2,))],
        compiler_params=params(4),
        cost_estimate=cost(0, 4 * MIB),
        name="first_sends",
    )(place, factor, vectors)


def band_kernel(inter_ref, vec_ref, after_ref, before_ref, out_ref, wide_ref):
    tile = pl.program_id(0)
    rows = vec_ref.shape[0]
    tile_rows = inter_ref.shape[0]
    owners = out_ref.shape[0]

    @pl.when(tile == 0)
    def _():
        wide_ref[:BS] = side_by_side(before_ref[...])
        wide_ref[BS : BS + rows] = side_by_side(vec_ref[...])
        wide_ref[BS + rows :] = side_by_side(after_ref[...])

    window = wide_ref[pl.ds(pl.multiple_of(tile * BS, BS), 3 * BS)]
    product = times(inter_ref[...], window)
    groups = tile_rows // (owners * CYC)
    for g in range(groups):
        for owner in range(owners):
            first = (g * owners + owner) * CYC
            out_ref[owner, g * CYC : (g + 1) * CYC] = product[first : first + CYC]


def band_product_split(intersection, vectors, halo, owners):
    rows, columns = vectors.shape
    width = intersection.shape[1]
    tile_rows = BS
    slot_rows = tile_rows // owners
    whole = lambda t: (0, 0)
    return pl.pallas_call(
        band_kernel,
        out_shape=shaped(owners, rows // owners, columns),
        grid=(rows // tile_rows,),
        in_specs=[
            pl.BlockSpec((tile_rows, width), lambda t: (t, 0)),
            pl.BlockSpec((rows, columns), whole),
            pl.BlockSpec((BS, columns), whole),
            pl.BlockSpec((BS, columns), whole),
        ],
        out_specs=pl.BlockSpec((owners, slot_rows, columns), lambda t: (0, t, 0)),
        scratch_shapes=[pltpu.VMEM((rows + 2 * BS, 2 * columns), BF16)],
        compiler_params=params(16),
        cost_estimate=cost(8 * rows * width * columns, 4 * rows * width),
        name="band_product_split",
    )(intersection, vectors, *halo)


def pass_kernel(value_ref, after_ref, out_ref):
    pass


def pass_on(value, after):
    anywhere = pl.BlockSpec(memory_space=pl.ANY)
    return pl.pallas_call(
        pass_kernel,
        out_shape=shaped(*value.shape),
        in_specs=[anywhere, anywhere],
        out_specs=anywhere,
        input_output_aliases={0: 0},
        compiler_params=params(1),
        name="pass_on",
    )(value, after)


def from_others(value, after):
    end = lax.axis_size("row") - 1
    middle = [(i, end - i) for i in range(1, end)]
    across = pass_on(swap_with(value, "row", 2), after)
    near, inner = swap_with(value, "row", 1), lax.ppermute(value, "row", middle)
    outer = lax.ppermute(across, "row", [(i, i ^ 1) for i, _ in middle])
    return near, across, inner, outer


def stack_kernel(place_ref, near_ref, across_ref, inner_ref, outer_ref, after_ref, *out_refs):
    me = place_ref[0]
    end = out_refs[0].shape[0]
    for panel, out_ref in enumerate(out_refs):
        out_ref[0] = near_ref[panel]
        out_ref[1] = across_ref[panel]

    @pl.when((me > 0) & (me < end))
    def _():
        for panel, out_ref in enumerate(out_refs):
            out_ref[2] = inner_ref[panel]

    @pl.when((me == 0) | (me == end))
    def _():
        for panel, out_ref in enumerate(out_refs):
            out_ref[2] = outer_ref[panel]


def stack(place, pieces, after):
    return pl.pallas_call(
        stack_kernel,
        out_shape=[shaped(3, *pieces[0].shape[1:])] * PANELS,
        in_specs=[IN_SMEM] + [IN_VMEM] * 4 + [pl.BlockSpec(memory_space=pl.ANY)],
        out_specs=[IN_VMEM] * PANELS,
        compiler_params=params(4),
        name="stack",
    )(place, *pieces, after)


def invert_kernel(panel, owners, shares, place_ref, after_ref, own_ref, *refs):
    pieces = refs[:shares]
    high_ref, low_ref, inv_high_ref, inv_low_ref, near_ref = refs[shares:]
    runs = PANEL // DIAG
    me, part = place_ref[0], place_ref[1]

    def place_left(run, row_block, values):
        if run:
            rows = pl.ds(pl.multiple_of(row_block * CYC, CYC), CYC)
            high_ref[rows, : run * DIAG], low_ref[rows, : run * DIAG] = split(values)

    for run in range(runs):
        for s in range(shares):
            row_block = (run * shares + s) * owners + me
            rows = slice((run * shares + s) * CYC, (run * shares + s + 1) * CYC)
            place_left(run, row_block, own_ref[panel, rows, : run * DIAG])
            near_ref[row_block] = own_ref[panel, rows, run * DIAG : (run + 1) * DIAG]
    for other in range(1, owners):
        owner = me ^ other
        for turn in range(shares):
            piece = pieces[turn]
            sender = part ^ turn
            for run in range(runs):
                row_block = (run * shares + fold_back(run, sender, shares)) * owners + owner
                first = run * run * HALF
                middle = first + run * DIAG
                place_left(run, row_block, piece[other - 1, :, first:middle])
                near_ref[row_block, :, :HALF] = piece[other - 1, :, middle : middle + HALF]
            for pair in range(runs // 2):
                run, block = lower_run(pair, sender, shares)
                first = (runs * runs + pair) * HALF
                near_ref[(run * shares + block) * owners + owner, :, HALF:] = piece[
                    other - 1, :, first : first + HALF
                ]

    def near(i, side):
        blocks = HALF // CYC
        return near_ref[i * blocks : (i + 1) * blocks, :, side * HALF : (side + 1) * HALF].reshape(HALF, HALF)

    down = lax.broadcasted_iota(jnp.int32, (HALF, HALF), 0)
    along = lax.broadcasted_iota(jnp.int32, (HALF, HALF), 1)
    eye = jnp.where(down == along, 1.0, 0.0).astype(F32)

    def below(size):
        return (down // size == along // size + 1) & ((down // size) % 2 == 1)

    count = PANEL // HALF
    diagonal = [near(i, i % 2) for i in range(count)]
    wides = [side_by_side(d) for d in diagonal]
    inverse = [eye - jnp.where(below(1), d, 0.0) for d in diagonal]
    size = 2
    while size < HALF:
        keep = jnp.where(below(size), 1.0, 0.0).astype(BF16)
        keep = jnp.concatenate([keep, keep], axis=1)
        right = [small_times(wides[i] * keep, inverse[i]) for i in range(count)]
        inverse = [inverse[i] - small_times(side_by_side(inverse[i]), right[i]) for i in range(count)]
        size *= 2
    for run in range(runs):
        first, second = inverse[2 * run], inverse[2 * run + 1]
        right = small_times(side_by_side(near(2 * run + 1, 0)), first)
        corner = -small_times(side_by_side(second), right)
        inv_high_ref[run, :HALF, :HALF], inv_low_ref[run, :HALF, :HALF] = split(first)
        inv_high_ref[run, HALF:, HALF:], inv_low_ref[run, HALF:, HALF:] = split(second)
        inv_high_ref[run, HALF:, :HALF], inv_low_ref[run, HALF:, :HALF] = split(corner)
        empty = jnp.zeros((HALF, HALF), BF16)
        inv_high_ref[run, :HALF, HALF:] = empty
        inv_low_ref[run, :HALF, HALF:] = empty


def invert_panel(panel, place, own, pieces, owners, shares, after, flops):
    groups = PANEL // DIAG
    return pl.pallas_call(
        functools.partial(invert_kernel, panel, owners, shares),
        out_shape=[shaped(PANEL, PANEL, dtype=BF16)] * 2 + [shaped(groups, DIAG, DIAG, dtype=BF16)] * 2,
        in_specs=[IN_SMEM, pl.BlockSpec(memory_space=pl.ANY)] + [IN_VMEM] * (len(pieces) + 1),
        out_specs=[IN_VMEM] * 4,
        scratch_shapes=[
            pltpu.VMEM((PANEL // CYC, CYC, DIAG), F32),
        ],
        compiler_params=params(16),
        cost_estimate=cost(flops, 12 * MIB),
        name="invert_panel",
    )(place, after, own, *pieces)


def order_kernel(first, pivot_ref, grouped_ref, after_ref, *out_refs):
    for out_ref in out_refs:
        pick_rows(pivot_ref, first, grouped_ref, out_ref)
        first += out_ref.shape[0]


def pick_rows(pivot_ref, first, source_ref, target_ref):
    step = 8

    def body(i, _):
        base = i * step
        rows = [source_ref[pl.ds(pivot_ref[first + base + j], 1)] for j in range(step)]
        target_ref[pl.ds(pl.multiple_of(base, step), step)] = jnp.concatenate(rows, axis=0)
        return 0

    lax.fori_loop(0, target_ref.shape[0] // step, body, 0, unroll=4)


def order_rows(first, counts, pivot_rows, grouped, after):
    return pl.pallas_call(
        functools.partial(order_kernel, first),
        out_shape=[shaped(count, grouped.shape[1]) for count in counts],
        in_specs=[IN_SMEM, IN_VMEM, pl.BlockSpec(memory_space=pl.ANY)],
        out_specs=[IN_VMEM] * len(counts),
        compiler_params=params(4),
        cost_estimate=cost(0, 2 * MIB),
        name="order_rows",
    )(pivot_rows, grouped, after)


def solve_into(me, owners, pieces, high_ref, low_ref, inv_high_ref, inv_low_ref, rhs_ref, y_ref, use):
    slots = pieces[0].shape[0] // CYC
    columns = pieces[0].shape[1]
    for piece, distance in zip(pieces, (0, *far_first(owners))):
        for s in range(slots):
            rhs_ref[s * owners + (me ^ distance)] = piece[s * CYC : (s + 1) * CYC]
    runs = [slice(k * DIAG, (k + 1) * DIAG) for k in range(PANEL // DIAG)]
    rhs = [rhs_ref[r.start // CYC : r.stop // CYC].reshape(DIAG, columns) for r in runs]

    def take_off(row, k, wide):
        rhs[row] = rhs[row] - parts_times(high_ref[runs[row], runs[k]], low_ref[runs[row], runs[k]], wide)

    wide = None
    for k in range(len(runs)):
        block = parts_times(inv_high_ref[k], inv_low_ref[k], side_by_side(rhs[k]))
        if k:
            for row in range(k + 1, len(runs)):
                take_off(row, k - 1, wide)
            use(k - 1, wide)
        wide = side_by_side(block)
        if k + 1 < len(runs):
            take_off(k + 1, k, wide)
        y_ref[runs[k].start // CYC : runs[k].stop // CYC] = block.reshape(DIAG // CYC, CYC, columns)
    use(len(runs) - 1, wide)


def first_kernel(owners, place_ref, *refs):
    pieces = refs[:owners]
    high, low, inv_high, inv_low, left_ref, current_ref, y_ref, next_ref, rhs_ref = refs[owners:]
    next_ref[...] = current_ref[...]

    def use(k, wide):
        columns = slice(k * DIAG, (k + 1) * DIAG)
        next_ref[...] -= parts_times(left_ref[0, :, columns], left_ref[1, :, columns], wide)

    solve_into(place_ref[0], owners, pieces, high, low, inv_high, inv_low, rhs_ref, y_ref, use)


def first_solve(place, pieces, prepared, left, current):
    owners = len(pieces)
    panel_rows, columns = current.shape
    return pl.pallas_call(
        functools.partial(first_kernel, owners),
        out_shape=[shaped(PANEL // CYC, CYC, columns), shaped(panel_rows, columns)],
        in_specs=[IN_SMEM] + [IN_VMEM] * (owners + 6),
        out_specs=[IN_VMEM] * 2,
        scratch_shapes=[pltpu.VMEM((PANEL // CYC, CYC, columns), F32)],
        compiler_params=params(8),
        cost_estimate=cost(HEAVY, 6 * MIB),
        name="first_solve",
    )(place, *pieces, *prepared, left, current)


def pivot_weights(me, sizes, diag, off):
    pairs, lanes = off.shape[1], diag.shape[1]
    spread = lax.broadcasted_iota(jnp.int32, (pairs, lanes), 1) // 2 == lax.broadcasted_iota(
        jnp.int32, (pairs, lanes), 0
    )
    spread = jnp.where(spread, 1.0, 0.0).astype(F32)
    off = jnp.dot(off, spread, precision=lax.Precision.HIGHEST, preferred_element_type=F32)
    sizes = jnp.dot(sizes.astype(F32), spread, precision=lax.Precision.HIGHEST, preferred_element_type=F32)
    odd = lax.broadcasted_iota(jnp.int32, diag.shape, 1) % 2 == 1
    other = jnp.where(odd, pltpu.roll(diag, 1, 1), pltpu.roll(diag, lanes - 1, 1))
    determ = diag * other - off * off
    is_pair = sizes > 1.5
    keep = jnp.where(is_pair, other / determ, 1.0 / diag)
    swap = jnp.where(is_pair, -off / determ, 0.0)
    turned = []
    for weight in (keep, swap):
        weight = pltpu.roll(weight, lax.rem(lanes - CYC * me, lanes), 1)
        tall = jnp.concatenate([weight] * (HALF // weight.shape[0]), axis=0)
        turned.append(tall.T)
    return turned


def mark_kernel(after_ref, out_ref):
    out_ref[...] = jnp.zeros_like(out_ref)


def mark(after):
    return pl.pallas_call(
        mark_kernel,
        out_shape=shaped(8, HALF),
        in_specs=[pl.BlockSpec(memory_space=pl.ANY)],
        out_specs=IN_VMEM,
        compiler_params=params(1),
        cost_estimate=cost(HEAVY, 0),
        name="mark",
    )(after)


def halve_kernel(
    tile_rows, place_ref, factor_ref, sizes_ref, diag_ref, off_ref, after_ref, out_ref, own_ref, next_ref, keep_ref,
    swap_ref, left_ref, below_ref, parts_ref, in_sems, out_sems, own_sems,
):
    tiles = left_ref.shape[0]
    rows = own_ref.shape[1]
    below = pltpu.make_async_copy(factor_ref.at[pl.ds(rows, rows), pl.ds(0, PANEL)], below_ref, own_sems.at[PANELS])
    below.start()
    loads, stores, owns = [], [], []
    for t in range(tiles):
        source = factor_ref.at[pl.ds((t + 1) * tile_rows, tile_rows), pl.ds((PANELS - 1) * PANEL, PANEL)]
        loads.append(pltpu.make_async_copy(source, left_ref.at[t], in_sems.at[t]))
        loads[t].start()
    for panel in range(PANELS):
        source = factor_ref.at[pl.ds(panel * rows, rows), pl.ds(panel * PANEL, PANEL)]
        owns.append(pltpu.make_async_copy(source, own_ref.at[panel], own_sems.at[panel]))
        owns[panel].start()
    keep_ref[...], swap_ref[...] = pivot_weights(place_ref[0], sizes_ref[...], diag_ref[...], off_ref[...])
    below.wait()
    next_ref[0], next_ref[1] = split(below_ref[...])
    for t in range(tiles):
        loads[t].wait()
        parts_ref[t, 0], parts_ref[t, 1] = split(left_ref[t])
        stores.append(pltpu.make_async_copy(parts_ref.at[t], out_ref.at[t], out_sems.at[t]))
        stores[t].start()
    for copy in owns + stores:
        copy.wait()


def halve_last(place, factor, pivots, panel_rows, after):
    tile_rows = PANELS * panel_rows
    tiles = factor.shape[0] // tile_rows - 1
    weight = shaped(pivots[1].shape[1], HALF)
    return pl.pallas_call(
        functools.partial(halve_kernel, tile_rows),
        out_shape=[
            shaped(tiles, 2, tile_rows, PANEL, dtype=BF16),
            shaped(PANELS, panel_rows, PANEL),
            shaped(2, panel_rows, PANEL, dtype=BF16),
            weight,
            weight,
        ],
        in_specs=[IN_SMEM, IN_HBM] + [IN_VMEM] * len(pivots) + [pl.BlockSpec(memory_space=pl.ANY)],
        out_specs=[IN_HBM] + [IN_VMEM] * 4,
        scratch_shapes=[
            pltpu.VMEM((tiles, tile_rows, PANEL), F32),
            pltpu.VMEM((panel_rows, PANEL), F32),
            pltpu.VMEM((tiles, 2, tile_rows, PANEL), BF16),
            pltpu.SemaphoreType.DMA((tiles,)),
            pltpu.SemaphoreType.DMA((tiles,)),
            pltpu.SemaphoreType.DMA((PANELS + 1,)),
        ],
        compiler_params=params(18),
        cost_estimate=cost(LIGHT, 12 * MIB),
        name="halve_last",
    )(place, factor, *pivots, after)


def middle_kernel(tile_rows, factor_ref, rest_ref, y_ref, out_ref, wide_ref, left_ref, sems):
    tiles = left_ref.shape[0]
    loads = []
    for t in range(tiles):
        source = factor_ref.at[pl.ds((t + 1) * tile_rows, tile_rows), pl.ds(0, PANEL)]
        loads.append(pltpu.make_async_copy(source, left_ref.at[t], sems.at[t]))
        loads[t].start()
    wide_ref[...] = side_by_side(y_ref[...].reshape(PANEL, y_ref.shape[2]))
    for t in range(tiles):
        loads[t].wait()
        rows = slice(t * tile_rows, (t + 1) * tile_rows)
        out_ref[rows] = rest_ref[rows] - times(left_ref[t], wide_ref[...])


def middle_update(rest, y, factor, tile_rows):
    rows, columns = rest.shape
    tiles = rows // tile_rows
    return pl.pallas_call(
        functools.partial(middle_kernel, tile_rows),
        out_shape=shaped(rows, columns),
        in_specs=[IN_HBM] + [IN_VMEM] * 2,
        out_specs=IN_VMEM,
        scratch_shapes=[
            pltpu.VMEM((PANEL, 2 * columns), BF16),
            pltpu.VMEM((tiles, tile_rows, PANEL), F32),
            pltpu.SemaphoreType.DMA((tiles,)),
        ],
        compiler_params=params(12),
        cost_estimate=cost(8 * rows * PANEL * columns, 8 * MIB),
        name="middle_update",
    )(factor, rest, y)


def last_kernel(owners, tile_rows, place_ref, left_ref, *refs):
    pieces = refs[:owners]
    high, low, inv_high, inv_low, y_ref, keep_ref, swap_ref, rest_ref = refs[owners : owners + 8]
    out_ref, rhs_ref, second_ref, stage_ref, sems = refs[owners + 8 :]
    me = place_ref[0]
    last = PANEL // DIAG - 1
    stores = []

    def store(t):
        target = out_ref.at[pl.ds(t * tile_rows, tile_rows)]
        stores.append(pltpu.make_async_copy(stage_ref.at[t], target, sems.at[t]))
        stores[-1].start()

    def use(k, wide):
        columns = slice(k * DIAG, (k + 1) * DIAG)
        for t in range(left_ref.shape[0]):
            rows = slice(t * tile_rows, (t + 1) * tile_rows)
            before = stage_ref[t + 1] if k else rest_ref[rows]
            stage_ref[t + 1] = before - parts_times(left_ref[t, 0, :, columns], left_ref[t, 1, :, columns], wide)
            if k == last:
                store(t + 1)

    solve_into(me, owners, pieces, high, low, inv_high, inv_low, rhs_ref, second_ref, use)
    scale_own_rows(me, owners, y_ref, second_ref, keep_ref, swap_ref, stage_ref)
    store(0)
    for copy in stores:
        copy.wait()


def scale_own_rows(me, owners, first_ref, second_ref, keep_ref, swap_ref, stage_ref):
    slots = first_ref.shape[0] // owners
    runs = keep_ref.shape[0] // (owners * CYC)
    for panel, source in enumerate((first_ref, second_ref)):
        for s in range(slots):
            at = panel * slots + s
            rows = source[s * owners + me]
            odd = lax.broadcasted_iota(jnp.int32, rows.shape, 0) % 2 == 1
            other = jnp.where(odd, pltpu.roll(rows, 1, 0), pltpu.roll(rows, CYC - 1, 0))
            first = (at % runs) * owners * CYC
            keep = keep_ref[first : first + CYC, at // runs : at // runs + 1]
            swap = swap_ref[first : first + CYC, at // runs : at // runs + 1]
            mixed = keep * rows + jnp.where(swap != 0, swap * other, 0.0)
            stage_ref[0, at * CYC : (at + 1) * CYC] = mixed


def last_solve(place, parts, pieces, prepared, y, weights, rest, tile_rows):
    owners = len(pieces)
    columns = rest.shape[1]
    rows = rest.shape[0] + tile_rows
    return pl.pallas_call(
        functools.partial(last_kernel, owners, tile_rows),
        out_shape=shaped(rows, columns),
        in_specs=[IN_SMEM] + [IN_VMEM] * (owners + 9),
        out_specs=IN_HBM,
        scratch_shapes=[
            pltpu.VMEM((PANEL // CYC, CYC, columns), F32),
            pltpu.VMEM((PANEL // CYC, CYC, columns), F32),
            pltpu.VMEM((rows // tile_rows, tile_rows, columns), F32),
            pltpu.SemaphoreType.DMA((rows // tile_rows,)),
        ],
        compiler_params=params(16),
        cost_estimate=cost(8 * rows * PANEL * columns, 12 * MIB),
        name="last_solve",
    )(place, parts, *pieces, *prepared, y, *weights, rest)


def swap_with(value, axis, distance):
    size = lax.axis_size(axis)
    return lax.ppermute(value, axis, [(i, i ^ distance) for i in range(size)])


def far_first(owners):
    return [*range(2, owners), 1]


def from_all(value, axis):
    return [value] + [swap_with(value, axis, k) for k in far_first(lax.axis_size(axis))]


def local(vectors, intersection, factor, pivot_rows, pivot_sizes, pivot_diag, pivot_off):
    owners, shares = lax.axis_size("row"), lax.axis_size("vec")
    slots = PANEL // owners // CYC
    panel_rows = slots * CYC
    place = jnp.stack([lax.axis_index("row"), lax.axis_index("vec")]).astype(jnp.int32)
    vectors, intersection, factor = (
        pltpu.with_memory_space_constraint(a, pltpu.HBM) for a in (vectors, intersection, factor)
    )

    share, first, last = first_sends(place, factor, vectors, slots, shares)
    up = [(i, i + 1) for i in range(owners - 1)]
    down = [(j, i) for i, j in up]
    halo = lax.ppermute(first, "row", down), lax.ppermute(last, "row", up)
    product = band_product_split(intersection, vectors, halo, owners)
    grouped = lax.all_to_all(product, "row", 0, 0, tiled=True).reshape(vectors.shape)

    def share_out(stacked, after):
        across = pass_on(swap_with(stacked, "vec", 2), after)
        return stacked, swap_with(stacked, "vec", 1), across, swap_with(across, "vec", 1)

    tile_rows = PANELS * panel_rows
    pivots = [a.reshape(pivot_diag.shape[0] // DIAG, -1) for a in (pivot_sizes, pivot_diag, pivot_off)]
    started = mark(product)
    direct = from_others(share, started)
    (first,) = order_rows(0, [panel_rows], pivot_rows, grouped, place)
    parts, own, left, keep, swap = halve_last(place, factor, pivots, panel_rows, started)
    stacked = stack(place, direct, own)
    shared = share_out(stacked[0], first)
    prepared = invert_panel(0, place, own, shared, owners, shares, first, HEAVY)
    rest_rows = factor.shape[0] - tile_rows
    second, rest = order_rows(panel_rows, [tile_rows - panel_rows, rest_rows], pivot_rows, grouped, prepared[2])
    later = share_out(stacked[1], second)
    pieces = from_all(first, "row")
    y, second = first_solve(place, pieces, prepared, left, second)
    pieces = from_all(second, "row")
    rest = middle_update(rest, y, factor, tile_rows)
    prepared = invert_panel(1, place, own, later, owners, shares, y, LIGHT)
    return last_solve(place, parts, pieces, prepared, y, (keep, swap), rest, tile_rows)


def padded_2(shard, sides, width):
    for axis, dim in sides:
        devices, length = (lax.axis_size(axis), shard.shape[dim])
        up = [(i, (i + 1) % devices) for i in range(devices - 1)]
        down = [(j, i) for i, j in up]
        last = lax.slice_in_dim(shard, length - width, length, axis=dim)
        leading = lax.slice_in_dim(shard, 0, width, axis=dim)
        before = lax.ppermute(last, axis, up)
        after = lax.ppermute(leading, axis, down)
        shard = jnp.concatenate([before, shard, after], axis=dim)
    return shard


def band_product(intersection, padded, blocks_here):
    band_width = intersection.shape[1] // 3
    band_rows = intersection.reshape(blocks_here, band_width, 3 * band_width)
    result = jnp.zeros((blocks_here, band_width, padded.shape[1]), jnp.float32)
    for offset in range(3):
        window = padded[offset * band_width : offset * band_width + blocks_here * band_width]
        window = window.reshape(blocks_here, band_width, padded.shape[1])
        result = result + jnp.einsum(
            "kij,kjv->kiv",
            band_rows[:, :, offset * band_width : (offset + 1) * band_width],
            window,
            precision=lax.Precision.HIGHEST,
        )
    return result.reshape(blocks_here * band_width, padded.shape[1])


def scale_pivots(values, sizes_here, diag_here, off_here):
    paired = values.reshape(-1, 2, values.shape[1])
    leading = paired[:, 0]
    trailing = paired[:, 1]
    diag_lead = diag_here[0::2][:, None]
    diag_next = diag_here[1::2][:, None]
    coupling = off_here[:, None]
    determ = diag_lead * diag_next - coupling * coupling
    is_pair = (sizes_here == 2)[:, None]
    new_lead = jnp.where(
        is_pair, (diag_next * leading - coupling * trailing) / determ, leading / diag_lead
    )
    new_next = jnp.where(
        is_pair, (diag_lead * trailing - coupling * leading) / determ, trailing / diag_next
    )
    return jnp.stack([new_lead, new_next], axis=1).reshape(values.shape)


def local_many(vectors, intersection, factor, pivot_rows, pivot_sizes, pivot_diag, pivot_off):
    owners = lax.axis_size("row")
    device = lax.axis_index("row")
    rows_here = vectors.shape[0]
    columns = vectors.shape[1]
    slot_count = PANEL // owners // CYC
    panel_rows = slot_count * CYC
    triangles = []
    quarter = PANEL // lax.axis_size("vec")
    column_idx = lax.axis_index("vec")
    for panel_num in range(PANELS):
        local_rows = factor[panel_num * panel_rows : (panel_num + 1) * panel_rows]
        column_part = lax.dynamic_slice_in_dim(
            local_rows, panel_num * PANEL + column_idx * quarter, quarter, 1
        )
        column_part = column_part.reshape(slot_count, 1, CYC, quarter)
        gathered = lax.all_gather(column_part, "row", axis=1, tiled=True)
        triangles.append(lax.all_gather(gathered, "vec", axis=3, tiled=True).reshape(PANEL, PANEL))
    padded = padded_2(vectors, (("row", 0),), BS)
    product = band_product(intersection, padded, rows_here // BS)
    grouped = product.reshape(rows_here // (CYC * owners), owners, CYC, columns)
    regrouped = lax.all_to_all(grouped, "row", split_axis=1, concat_axis=0, tiled=True).reshape(
        rows_here, columns
    )
    current = jnp.take(regrouped, pivot_rows, axis=0)
    outputs = []
    for panel_num in range(PANELS):
        row_first = panel_num * panel_rows
        row_end = row_first + panel_rows
        col_first = panel_num * PANEL
        col_end = col_first + PANEL
        rhs_local = current[row_first:row_end].reshape(slot_count, 1, CYC, columns)
        rhs_all = lax.all_gather(rhs_local, "row", axis=1, tiled=True)
        triangle = triangles[panel_num]
        block_sol = jax.scipy.linalg.solve_triangular(
            triangle, rhs_all.reshape(PANEL, columns), lower=True, unit_diagonal=True
        )
        update = jnp.dot(
            factor[row_end:, col_first:col_end], block_sol, precision=lax.Precision.HIGHEST
        )
        current = jnp.concatenate([current[:row_end], current[row_end:] - update], axis=0)
        scaled = scale_pivots(
            block_sol,
            pivot_sizes[col_first // 2 : col_end // 2],
            pivot_diag[col_first:col_end],
            pivot_off[col_first // 2 : col_end // 2],
        )
        own_rows = lax.dynamic_slice_in_dim(
            scaled.reshape(slot_count, owners, CYC, columns), device, 1, 1
        )
        outputs.append(own_rows.reshape(panel_rows, columns))
    outputs.append(current[PANELS * panel_rows :])
    return jnp.concatenate(outputs, axis=0)


def solution(mesh):
    in_specs = (
        P(("cuts", "row"), "vec"),
        P("row", None),
        P(("cuts", "row"), None),
        P(("cuts", "row")),
        P("cuts"),
        P("cuts"),
        P("cuts"),
    )
    out_specs = P(("cuts", "row"), "vec")
    owners, shares = mesh.shape["row"], mesh.shape["vec"]
    few = owners == 4 and shares == 4 and DIAG == owners * shares * CYC
    body = local if few else local_many
    return jax.shard_map(body, mesh=mesh, in_specs=in_specs, out_specs=out_specs, check_vma=False)
```

```python
import functools

import jax
import jax.numpy as jnp
from jax import lax
from jax.experimental import pallas as pl
from jax.experimental.pallas import tpu as pltpu
from jax.sharding import PartitionSpec as P

BS = 512
PANEL = 1024
PANELS = 2
CYC = 16
DIAG = 256
HALF = 128
MIB = 1024 * 1024
HEAVY = 2**37
LIGHT = 2**30
F32 = jnp.float32
BF16 = jnp.bfloat16


def params(mib):
    return pltpu.CompilerParams(vmem_limit_bytes=mib * MIB)


IN_VMEM = pl.BlockSpec(memory_space=pltpu.VMEM)
IN_SMEM = pl.BlockSpec(memory_space=pltpu.SMEM)
IN_HBM = pl.BlockSpec(memory_space=pltpu.HBM)


def shaped(*shape, dtype=F32):
    return jax.ShapeDtypeStruct(shape, dtype)


def cost(flops, moved):
    return pl.CostEstimate(flops=int(flops), bytes_accessed=int(moved), transcendentals=0)


def split(value):
    high = value.astype(BF16)
    low = (value - high.astype(F32)).astype(BF16)
    return high, low


def side_by_side(value):
    return jnp.concatenate(split(value), axis=1)


def dot(left, right):
    return jnp.dot(left, right, preferred_element_type=F32)


def fold(wide):
    width = wide.shape[1] // 2
    return wide[:, :width] + wide[:, width:]


def times(left, right_wide):
    high, low = split(left)
    return parts_times(high, low, right_wide)


def parts_times(high, low, right_wide):
    return fold(dot(high, right_wide)) + dot(low, right_wide[:, : right_wide.shape[1] // 2])


def small_times(left_wide, right):
    wide = side_by_side(right)
    return fold(dot(left_wide, jnp.concatenate([wide, wide], axis=0)))


def fold_back(run, part, shares):
    return part if run % 2 == 0 else shares - 1 - part


def lower_run(pair, part, shares):
    early = part < shares // 2
    return 2 * pair + jnp.where(early, 1, 0), jnp.where(early, shares - 1 - part, part)


def start_kernel(slots, shares, place_ref, factor_ref, vec_ref, share_ref, first_ref, last_ref, sems):
    part = place_ref[1]
    rows = vec_ref.shape[0]
    copies = [(vec_ref.at[pl.ds(rows - BS, BS)], last_ref), (vec_ref.at[pl.ds(0, BS)], first_ref)]
    runs = PANEL // DIAG

    def source(panel, run, block, column, width):
        row = pl.multiple_of((panel * slots + run * shares + block) * CYC, CYC)
        column = pl.multiple_of(panel * PANEL + column, HALF)
        return factor_ref.at[pl.ds(row, CYC), pl.ds(column, width)]

    for panel in range(PANELS):
        for run in range(runs):
            width = (2 * run + 1) * HALF
            target = share_ref.at[panel, :, pl.ds(run * run * HALF, width)]
            copies.append((source(panel, run, fold_back(run, part, shares), 0, width), target))
        for pair in range(runs // 2):
            run, block = lower_run(pair, part, shares)
            target = share_ref.at[panel, :, pl.ds((runs * runs + pair) * HALF, HALF)]
            copies.append((source(panel, run, block, (2 * run + 1) * HALF, HALF), target))
    started = [pltpu.make_async_copy(a, b, sems.at[i]) for i, (a, b) in enumerate(copies)]
    for copy in started:
        copy.start()
    for copy in started:
        copy.wait()


def first_sends(place, factor, vectors, slots, shares):
    runs = PANEL // DIAG
    edge = shaped(BS, vectors.shape[1])
    return pl.pallas_call(
        functools.partial(start_kernel, slots, shares),
        out_shape=[shaped(PANELS, CYC, (runs * runs + runs // 2) * HALF), edge, edge],
        in_specs=[IN_SMEM, IN_HBM, IN_HBM],
        out_specs=[IN_VMEM, IN_HBM, IN_HBM],
        scratch_shapes=[pltpu.SemaphoreType.DMA((PANELS * (runs + runs // 2) + 2,))],
        compiler_params=params(4),
        cost_estimate=cost(0, 4 * MIB),
        name="first_sends",
    )(place, factor, vectors)


def band_kernel(inter_ref, vec_ref, after_ref, before_ref, out_ref, wide_ref):
    tile = pl.program_id(0)
    rows = vec_ref.shape[0]
    tile_rows = inter_ref.shape[0]
    owners = out_ref.shape[0]

    @pl.when(tile == 0)
    def _():
        wide_ref[:BS] = side_by_side(before_ref[...])
        wide_ref[BS : BS + rows] = side_by_side(vec_ref[...])
        wide_ref[BS + rows :] = side_by_side(after_ref[...])

    window = wide_ref[pl.ds(pl.multiple_of(tile * BS, BS), 3 * BS)]
    product = times(inter_ref[...], window)
    groups = tile_rows // (owners * CYC)
    for g in range(groups):
        for owner in range(owners):
            first = (g * owners + owner) * CYC
            out_ref[owner, g * CYC : (g + 1) * CYC] = product[first : first + CYC]


def band_product_split(intersection, vectors, halo, owners):
    rows, columns = vectors.shape
    width = intersection.shape[1]
    tile_rows = BS
    slot_rows = tile_rows // owners
    whole = lambda t: (0, 0)
    return pl.pallas_call(
        band_kernel,
        out_shape=shaped(owners, rows // owners, columns),
        grid=(rows // tile_rows,),
        in_specs=[
            pl.BlockSpec((tile_rows, width), lambda t: (t, 0)),
            pl.BlockSpec((rows, columns), whole),
            pl.BlockSpec((BS, columns), whole),
            pl.BlockSpec((BS, columns), whole),
        ],
        out_specs=pl.BlockSpec((owners, slot_rows, columns), lambda t: (0, t, 0)),
        scratch_shapes=[pltpu.VMEM((rows + 2 * BS, 2 * columns), BF16)],
        compiler_params=params(16),
        cost_estimate=cost(8 * rows * width * columns, 4 * rows * width),
        name="band_product_split",
    )(intersection, vectors, *halo)


def pass_kernel(value_ref, after_ref, out_ref):
    pass


def pass_on(value, after):
    anywhere = pl.BlockSpec(memory_space=pl.ANY)
    return pl.pallas_call(
        pass_kernel,
        out_shape=shaped(*value.shape),
        in_specs=[anywhere, anywhere],
        out_specs=anywhere,
        input_output_aliases={0: 0},
        compiler_params=params(1),
        name="pass_on",
    )(value, after)


def from_others(value, after):
    end = lax.axis_size("row") - 1
    middle = [(i, end - i) for i in range(1, end)]
    across = pass_on(swap_with(value, "row", 2), after)
    near, inner = swap_with(value, "row", 1), lax.ppermute(value, "row", middle)
    outer = lax.ppermute(across, "row", [(i, i ^ 1) for i, _ in middle])
    return near, across, inner, outer


def stack_kernel(place_ref, near_ref, across_ref, inner_ref, outer_ref, after_ref, *out_refs):
    me = place_ref[0]
    end = out_refs[0].shape[0]
    for panel, out_ref in enumerate(out_refs):
        out_ref[0] = near_ref[panel]
        out_ref[1] = across_ref[panel]

    @pl.when((me > 0) & (me < end))
    def _():
        for panel, out_ref in enumerate(out_refs):
            out_ref[2] = inner_ref[panel]

    @pl.when((me == 0) | (me == end))
    def _():
        for panel, out_ref in enumerate(out_refs):
            out_ref[2] = outer_ref[panel]


def stack(place, pieces, after):
    return pl.pallas_call(
        stack_kernel,
        out_shape=[shaped(3, *pieces[0].shape[1:])] * PANELS,
        in_specs=[IN_SMEM] + [IN_VMEM] * 4 + [pl.BlockSpec(memory_space=pl.ANY)],
        out_specs=[IN_VMEM] * PANELS,
        compiler_params=params(4),
        name="stack",
    )(place, *pieces, after)


def invert_kernel(panel, owners, shares, place_ref, after_ref, own_ref, *refs):
    pieces = refs[:shares]
    high_ref, low_ref, inv_high_ref, inv_low_ref, near_ref = refs[shares:]
    runs = PANEL // DIAG
    me, part = place_ref[0], place_ref[1]

    def place_left(run, row_block, values):
        if run:
            rows = pl.ds(pl.multiple_of(row_block * CYC, CYC), CYC)
            high_ref[rows, : run * DIAG], low_ref[rows, : run * DIAG] = split(values)

    for run in range(runs):
        for s in range(shares):
            row_block = (run * shares + s) * owners + me
            rows = slice((run * shares + s) * CYC, (run * shares + s + 1) * CYC)
            place_left(run, row_block, own_ref[panel, rows, : run * DIAG])
            near_ref[row_block] = own_ref[panel, rows, run * DIAG : (run + 1) * DIAG]
    for other in range(1, owners):
        owner = me ^ other
        for turn in range(shares):
            piece = pieces[turn]
            sender = part ^ turn
            for run in range(runs):
                row_block = (run * shares + fold_back(run, sender, shares)) * owners + owner
                first = run * run * HALF
                middle = first + run * DIAG
                place_left(run, row_block, piece[other - 1, :, first:middle])
                near_ref[row_block, :, :HALF] = piece[other - 1, :, middle : middle + HALF]
            for pair in range(runs // 2):
                run, block = lower_run(pair, sender, shares)
                first = (runs * runs + pair) * HALF
                near_ref[(run * shares + block) * owners + owner, :, HALF:] = piece[
                    other - 1, :, first : first + HALF
                ]

    def near(i, side):
        blocks = HALF // CYC
        return near_ref[i * blocks : (i + 1) * blocks, :, side * HALF : (side + 1) * HALF].reshape(HALF, HALF)

    down = lax.broadcasted_iota(jnp.int32, (HALF, HALF), 0)
    along = lax.broadcasted_iota(jnp.int32, (HALF, HALF), 1)
    eye = jnp.where(down == along, 1.0, 0.0).astype(F32)

    def below(size):
        return (down // size == along // size + 1) & ((down // size) % 2 == 1)

    count = PANEL // HALF
    diagonal = [near(i, i % 2) for i in range(count)]
    wides = [side_by_side(d) for d in diagonal]
    inverse = [eye - jnp.where(below(1), d, 0.0) for d in diagonal]
    size = 2
    while size < HALF:
        keep = jnp.where(below(size), 1.0, 0.0).astype(BF16)
        keep = jnp.concatenate([keep, keep], axis=1)
        right = [small_times(wides[i] * keep, inverse[i]) for i in range(count)]
        inverse = [inverse[i] - small_times(side_by_side(inverse[i]), right[i]) for i in range(count)]
        size *= 2
    for run in range(runs):
        first, second = inverse[2 * run], inverse[2 * run + 1]
        right = small_times(side_by_side(near(2 * run + 1, 0)), first)
        corner = -small_times(side_by_side(second), right)
        inv_high_ref[run, :HALF, :HALF], inv_low_ref[run, :HALF, :HALF] = split(first)
        inv_high_ref[run, HALF:, HALF:], inv_low_ref[run, HALF:, HALF:] = split(second)
        inv_high_ref[run, HALF:, :HALF], inv_low_ref[run, HALF:, :HALF] = split(corner)
        empty = jnp.zeros((HALF, HALF), BF16)
        inv_high_ref[run, :HALF, HALF:] = empty
        inv_low_ref[run, :HALF, HALF:] = empty


def invert_panel(panel, place, own, pieces, owners, shares, after, flops):
    groups = PANEL // DIAG
    return pl.pallas_call(
        functools.partial(invert_kernel, panel, owners, shares),
        out_shape=[shaped(PANEL, PANEL, dtype=BF16)] * 2 + [shaped(groups, DIAG, DIAG, dtype=BF16)] * 2,
        in_specs=[IN_SMEM, pl.BlockSpec(memory_space=pl.ANY)] + [IN_VMEM] * (len(pieces) + 1),
        out_specs=[IN_VMEM] * 4,
        scratch_shapes=[
            pltpu.VMEM((PANEL // CYC, CYC, DIAG), F32),
        ],
        compiler_params=params(16),
        cost_estimate=cost(flops, 12 * MIB),
        name="invert_panel",
    )(place, after, own, *pieces)


def order_kernel(first, pivot_ref, grouped_ref, after_ref, *out_refs):
    for out_ref in out_refs:
        pick_rows(pivot_ref, first, grouped_ref, out_ref)
        first += out_ref.shape[0]


def pick_rows(pivot_ref, first, source_ref, target_ref):
    step = 8

    def body(i, _):
        base = i * step
        rows = [source_ref[pl.ds(pivot_ref[first + base + j], 1)] for j in range(step)]
        target_ref[pl.ds(pl.multiple_of(base, step), step)] = jnp.concatenate(rows, axis=0)
        return 0

    lax.fori_loop(0, target_ref.shape[0] // step, body, 0, unroll=4)


def order_rows(first, counts, pivot_rows, grouped, after):
    return pl.pallas_call(
        functools.partial(order_kernel, first),
        out_shape=[shaped(count, grouped.shape[1]) for count in counts],
        in_specs=[IN_SMEM, IN_VMEM, pl.BlockSpec(memory_space=pl.ANY)],
        out_specs=[IN_VMEM] * len(counts),
        compiler_params=params(4),
        cost_estimate=cost(0, 2 * MIB),
        name="order_rows",
    )(pivot_rows, grouped, after)


def solve_into(me, owners, pieces, high_ref, low_ref, inv_high_ref, inv_low_ref, rhs_ref, y_ref, use):
    slots = pieces[0].shape[0] // CYC
    columns = pieces[0].shape[1]
    for piece, distance in zip(pieces, (0, *far_first(owners))):
        for s in range(slots):
            rhs_ref[s * owners + (me ^ distance)] = piece[s * CYC : (s + 1) * CYC]
    runs = [slice(k * DIAG, (k + 1) * DIAG) for k in range(PANEL // DIAG)]
    rhs = [rhs_ref[r.start // CYC : r.stop // CYC].reshape(DIAG, columns) for r in runs]

    def take_off(row, k, wide):
        rhs[row] = rhs[row] - parts_times(high_ref[runs[row], runs[k]], low_ref[runs[row], runs[k]], wide)

    wide = None
    for k in range(len(runs)):
        block = parts_times(inv_high_ref[k], inv_low_ref[k], side_by_side(rhs[k]))
        if k:
            for row in range(k + 1, len(runs)):
                take_off(row, k - 1, wide)
            use(k - 1, wide)
        wide = side_by_side(block)
        if k + 1 < len(runs):
            take_off(k + 1, k, wide)
        y_ref[runs[k].start // CYC : runs[k].stop // CYC] = block.reshape(DIAG // CYC, CYC, columns)
    use(len(runs) - 1, wide)


def first_kernel(owners, place_ref, *refs):
    pieces = refs[:owners]
    high, low, inv_high, inv_low, left_ref, current_ref, y_ref, next_ref, rhs_ref = refs[owners:]
    next_ref[...] = current_ref[...]

    def use(k, wide):
        columns = slice(k * DIAG, (k + 1) * DIAG)
        next_ref[...] -= parts_times(left_ref[0, :, columns], left_ref[1, :, columns], wide)

    solve_into(place_ref[0], owners, pieces, high, low, inv_high, inv_low, rhs_ref, y_ref, use)


def first_solve(place, pieces, prepared, left, current):
    owners = len(pieces)
    panel_rows, columns = current.shape
    return pl.pallas_call(
        functools.partial(first_kernel, owners),
        out_shape=[shaped(PANEL // CYC, CYC, columns), shaped(panel_rows, columns)],
        in_specs=[IN_SMEM] + [IN_VMEM] * (owners + 6),
        out_specs=[IN_VMEM] * 2,
        scratch_shapes=[pltpu.VMEM((PANEL // CYC, CYC, columns), F32)],
        compiler_params=params(8),
        cost_estimate=cost(HEAVY, 6 * MIB),
        name="first_solve",
    )(place, *pieces, *prepared, left, current)


def pivot_weights(me, sizes, diag, off):
    pairs, lanes = off.shape[1], diag.shape[1]
    spread = lax.broadcasted_iota(jnp.int32, (pairs, lanes), 1) // 2 == lax.broadcasted_iota(
        jnp.int32, (pairs, lanes), 0
    )
    spread = jnp.where(spread, 1.0, 0.0).astype(F32)
    off = jnp.dot(off, spread, precision=lax.Precision.HIGHEST, preferred_element_type=F32)
    sizes = jnp.dot(sizes.astype(F32), spread, precision=lax.Precision.HIGHEST, preferred_element_type=F32)
    odd = lax.broadcasted_iota(jnp.int32, diag.shape, 1) % 2 == 1
    other = jnp.where(odd, pltpu.roll(diag, 1, 1), pltpu.roll(diag, lanes - 1, 1))
    determ = diag * other - off * off
    is_pair = sizes > 1.5
    keep = jnp.where(is_pair, other / determ, 1.0 / diag)
    swap = jnp.where(is_pair, -off / determ, 0.0)
    turned = []
    for weight in (keep, swap):
        weight = pltpu.roll(weight, lax.rem(lanes - CYC * me, lanes), 1)
        tall = jnp.concatenate([weight] * (HALF // weight.shape[0]), axis=0)
        turned.append(tall.T)
    return turned


def weights_kernel(place_ref, after_ref, sizes_ref, diag_ref, off_ref, keep_ref, swap_ref):
    keep_ref[...], swap_ref[...] = pivot_weights(place_ref[0], sizes_ref[...], diag_ref[...], off_ref[...])


def own_weights(place, pivots, after):
    weight = shaped(pivots[1].shape[1], HALF)
    return pl.pallas_call(
        weights_kernel,
        out_shape=[weight, weight],
        in_specs=[IN_SMEM, pl.BlockSpec(memory_space=pl.ANY)] + [IN_VMEM] * len(pivots),
        out_specs=[IN_VMEM] * 2,
        compiler_params=params(4),
        cost_estimate=cost(HEAVY, 0),
        name="own_weights",
    )(place, after, *pivots)


def halve_kernel(
    tile_rows, factor_ref, after_ref, out_ref, own_ref, next_ref, left_ref, below_ref, parts_ref, in_sems, out_sems,
    own_sems,
):
    tiles = left_ref.shape[0]
    rows = own_ref.shape[1]
    below = pltpu.make_async_copy(factor_ref.at[pl.ds(rows, rows), pl.ds(0, PANEL)], below_ref, own_sems.at[PANELS])
    below.start()
    loads, stores, owns = [], [], []
    for t in range(tiles):
        source = factor_ref.at[pl.ds((t + 1) * tile_rows, tile_rows), pl.ds((PANELS - 1) * PANEL, PANEL)]
        loads.append(pltpu.make_async_copy(source, left_ref.at[t], in_sems.at[t]))
        loads[t].start()
    for panel in range(PANELS):
        source = factor_ref.at[pl.ds(panel * rows, rows), pl.ds(panel * PANEL, PANEL)]
        owns.append(pltpu.make_async_copy(source, own_ref.at[panel], own_sems.at[panel]))
        owns[panel].start()
    below.wait()
    next_ref[0], next_ref[1] = split(below_ref[...])
    for t in range(tiles):
        loads[t].wait()
        parts_ref[t, 0], parts_ref[t, 1] = split(left_ref[t])
        stores.append(pltpu.make_async_copy(parts_ref.at[t], out_ref.at[t], out_sems.at[t]))
        stores[t].start()
    for copy in owns + stores:
        copy.wait()


def halve_last(factor, panel_rows, after):
    tile_rows = PANELS * panel_rows
    tiles = factor.shape[0] // tile_rows - 1
    return pl.pallas_call(
        functools.partial(halve_kernel, tile_rows),
        out_shape=[
            shaped(tiles, 2, tile_rows, PANEL, dtype=BF16),
            shaped(PANELS, panel_rows, PANEL),
            shaped(2, panel_rows, PANEL, dtype=BF16),
        ],
        in_specs=[IN_HBM, pl.BlockSpec(memory_space=pl.ANY)],
        out_specs=[IN_HBM, IN_VMEM, IN_VMEM],
        scratch_shapes=[
            pltpu.VMEM((tiles, tile_rows, PANEL), F32),
            pltpu.VMEM((panel_rows, PANEL), F32),
            pltpu.VMEM((tiles, 2, tile_rows, PANEL), BF16),
            pltpu.SemaphoreType.DMA((tiles,)),
            pltpu.SemaphoreType.DMA((tiles,)),
            pltpu.SemaphoreType.DMA((PANELS + 1,)),
        ],
        compiler_params=params(18),
        cost_estimate=cost(LIGHT, 12 * MIB),
        name="halve_last",
    )(factor, after)


def middle_kernel(tile_rows, factor_ref, rest_ref, y_ref, out_ref, wide_ref, left_ref, sems):
    tiles = left_ref.shape[0]
    loads = []
    for t in range(tiles):
        source = factor_ref.at[pl.ds((t + 1) * tile_rows, tile_rows), pl.ds(0, PANEL)]
        loads.append(pltpu.make_async_copy(source, left_ref.at[t], sems.at[t]))
        loads[t].start()
    wide_ref[...] = side_by_side(y_ref[...].reshape(PANEL, y_ref.shape[2]))
    for t in range(tiles):
        loads[t].wait()
        rows = slice(t * tile_rows, (t + 1) * tile_rows)
        out_ref[rows] = rest_ref[rows] - times(left_ref[t], wide_ref[...])


def middle_update(rest, y, factor, tile_rows):
    rows, columns = rest.shape
    tiles = rows // tile_rows
    return pl.pallas_call(
        functools.partial(middle_kernel, tile_rows),
        out_shape=shaped(rows, columns),
        in_specs=[IN_HBM] + [IN_VMEM] * 2,
        out_specs=IN_VMEM,
        scratch_shapes=[
            pltpu.VMEM((PANEL, 2 * columns), BF16),
            pltpu.VMEM((tiles, tile_rows, PANEL), F32),
            pltpu.SemaphoreType.DMA((tiles,)),
        ],
        compiler_params=params(12),
        cost_estimate=cost(8 * rows * PANEL * columns, 8 * MIB),
        name="middle_update",
    )(factor, rest, y)


def last_kernel(owners, tile_rows, place_ref, left_ref, *refs):
    pieces = refs[:owners]
    high, low, inv_high, inv_low, y_ref, keep_ref, swap_ref, rest_ref = refs[owners : owners + 8]
    out_ref, rhs_ref, second_ref, stage_ref, sems = refs[owners + 8 :]
    me = place_ref[0]
    last = PANEL // DIAG - 1
    stores = []

    def store(t):
        target = out_ref.at[pl.ds(t * tile_rows, tile_rows)]
        stores.append(pltpu.make_async_copy(stage_ref.at[t], target, sems.at[t]))
        stores[-1].start()

    def use(k, wide):
        columns = slice(k * DIAG, (k + 1) * DIAG)
        for t in range(left_ref.shape[0]):
            rows = slice(t * tile_rows, (t + 1) * tile_rows)
            before = stage_ref[t + 1] if k else rest_ref[rows]
            stage_ref[t + 1] = before - parts_times(left_ref[t, 0, :, columns], left_ref[t, 1, :, columns], wide)
            if k == last:
                store(t + 1)

    solve_into(me, owners, pieces, high, low, inv_high, inv_low, rhs_ref, second_ref, use)
    scale_own_rows(me, owners, y_ref, second_ref, keep_ref, swap_ref, stage_ref)
    store(0)
    for copy in stores:
        copy.wait()


def scale_own_rows(me, owners, first_ref, second_ref, keep_ref, swap_ref, stage_ref):
    slots = first_ref.shape[0] // owners
    runs = keep_ref.shape[0] // (owners * CYC)
    for panel, source in enumerate((first_ref, second_ref)):
        for s in range(slots):
            at = panel * slots + s
            rows = source[s * owners + me]
            odd = lax.broadcasted_iota(jnp.int32, rows.shape, 0) % 2 == 1
            other = jnp.where(odd, pltpu.roll(rows, 1, 0), pltpu.roll(rows, CYC - 1, 0))
            first = (at % runs) * owners * CYC
            keep = keep_ref[first : first + CYC, at // runs : at // runs + 1]
            swap = swap_ref[first : first + CYC, at // runs : at // runs + 1]
            mixed = keep * rows + jnp.where(swap != 0, swap * other, 0.0)
            stage_ref[0, at * CYC : (at + 1) * CYC] = mixed


def last_solve(place, parts, pieces, prepared, y, weights, rest, tile_rows):
    owners = len(pieces)
    columns = rest.shape[1]
    rows = rest.shape[0] + tile_rows
    return pl.pallas_call(
        functools.partial(last_kernel, owners, tile_rows),
        out_shape=shaped(rows, columns),
        in_specs=[IN_SMEM] + [IN_VMEM] * (owners + 9),
        out_specs=IN_HBM,
        scratch_shapes=[
            pltpu.VMEM((PANEL // CYC, CYC, columns), F32),
            pltpu.VMEM((PANEL // CYC, CYC, columns), F32),
            pltpu.VMEM((rows // tile_rows, tile_rows, columns), F32),
            pltpu.SemaphoreType.DMA((rows // tile_rows,)),
        ],
        compiler_params=params(16),
        cost_estimate=cost(8 * rows * PANEL * columns, 12 * MIB),
        name="last_solve",
    )(place, parts, *pieces, *prepared, y, *weights, rest)


def swap_with(value, axis, distance):
    size = lax.axis_size(axis)
    return lax.ppermute(value, axis, [(i, i ^ distance) for i in range(size)])


def far_first(owners):
    return [*range(2, owners), 1]


def from_all(value, axis):
    return [value] + [swap_with(value, axis, k) for k in far_first(lax.axis_size(axis))]


def local(vectors, intersection, factor, pivot_rows, pivot_sizes, pivot_diag, pivot_off):
    owners, shares = lax.axis_size("row"), lax.axis_size("vec")
    slots = PANEL // owners // CYC
    panel_rows = slots * CYC
    place = jnp.stack([lax.axis_index("row"), lax.axis_index("vec")]).astype(jnp.int32)
    vectors, intersection, factor = (
        pltpu.with_memory_space_constraint(a, pltpu.HBM) for a in (vectors, intersection, factor)
    )

    share, first, last = first_sends(place, factor, vectors, slots, shares)
    up = [(i, i + 1) for i in range(owners - 1)]
    down = [(j, i) for i, j in up]
    halo = lax.ppermute(first, "row", down), lax.ppermute(last, "row", up)
    product = band_product_split(intersection, vectors, halo, owners)
    grouped = lax.all_to_all(product, "row", 0, 0, tiled=True).reshape(vectors.shape)

    def share_out(stacked, after):
        across = pass_on(swap_with(stacked, "vec", 2), after)
        return stacked, swap_with(stacked, "vec", 1), across, swap_with(across, "vec", 1)

    tile_rows = PANELS * panel_rows
    pivots = [a.reshape(pivot_diag.shape[0] // DIAG, -1) for a in (pivot_sizes, pivot_diag, pivot_off)]
    keep, swap = own_weights(place, pivots, product)
    direct = from_others(share, keep)
    (first,) = order_rows(0, [panel_rows], pivot_rows, grouped, place)
    parts, own, left = halve_last(factor, panel_rows, keep)
    stacked = stack(place, direct, own)
    shared = share_out(stacked[0], first)
    prepared = invert_panel(0, place, own, shared, owners, shares, first, HEAVY)
    rest_rows = factor.shape[0] - tile_rows
    second, rest = order_rows(panel_rows, [tile_rows - panel_rows, rest_rows], pivot_rows, grouped, prepared[2])
    later = share_out(stacked[1], second)
    pieces = from_all(first, "row")
    y, second = first_solve(place, pieces, prepared, left, second)
    pieces = from_all(second, "row")
    rest = middle_update(rest, y, factor, tile_rows)
    prepared = invert_panel(1, place, own, later, owners, shares, y, LIGHT)
    return last_solve(place, parts, pieces, prepared, y, (keep, swap), rest, tile_rows)


def padded_2(shard, sides, width):
    for axis, dim in sides:
        devices, length = (lax.axis_size(axis), shard.shape[dim])
        up = [(i, (i + 1) % devices) for i in range(devices - 1)]
        down = [(j, i) for i, j in up]
        last = lax.slice_in_dim(shard, length - width, length, axis=dim)
        leading = lax.slice_in_dim(shard, 0, width, axis=dim)
        before = lax.ppermute(last, axis, up)
        after = lax.ppermute(leading, axis, down)
        shard = jnp.concatenate([before, shard, after], axis=dim)
    return shard


def band_product(intersection, padded, blocks_here):
    band_width = intersection.shape[1] // 3
    band_rows = intersection.reshape(blocks_here, band_width, 3 * band_width)
    result = jnp.zeros((blocks_here, band_width, padded.shape[1]), jnp.float32)
    for offset in range(3):
        window = padded[offset * band_width : offset * band_width + blocks_here * band_width]
        window = window.reshape(blocks_here, band_width, padded.shape[1])
        result = result + jnp.einsum(
            "kij,kjv->kiv",
            band_rows[:, :, offset * band_width : (offset + 1) * band_width],
            window,
            precision=lax.Precision.HIGHEST,
        )
    return result.reshape(blocks_here * band_width, padded.shape[1])


def scale_pivots(values, sizes_here, diag_here, off_here):
    paired = values.reshape(-1, 2, values.shape[1])
    leading = paired[:, 0]
    trailing = paired[:, 1]
    diag_lead = diag_here[0::2][:, None]
    diag_next = diag_here[1::2][:, None]
    coupling = off_here[:, None]
    determ = diag_lead * diag_next - coupling * coupling
    is_pair = (sizes_here == 2)[:, None]
    new_lead = jnp.where(
        is_pair, (diag_next * leading - coupling * trailing) / determ, leading / diag_lead
    )
    new_next = jnp.where(
        is_pair, (diag_lead * trailing - coupling * leading) / determ, trailing / diag_next
    )
    return jnp.stack([new_lead, new_next], axis=1).reshape(values.shape)


def local_many(vectors, intersection, factor, pivot_rows, pivot_sizes, pivot_diag, pivot_off):
    owners = lax.axis_size("row")
    device = lax.axis_index("row")
    rows_here = vectors.shape[0]
    columns = vectors.shape[1]
    slot_count = PANEL // owners // CYC
    panel_rows = slot_count * CYC
    triangles = []
    quarter = PANEL // lax.axis_size("vec")
    column_idx = lax.axis_index("vec")
    for panel_num in range(PANELS):
        local_rows = factor[panel_num * panel_rows : (panel_num + 1) * panel_rows]
        column_part = lax.dynamic_slice_in_dim(
            local_rows, panel_num * PANEL + column_idx * quarter, quarter, 1
        )
        column_part = column_part.reshape(slot_count, 1, CYC, quarter)
        gathered = lax.all_gather(column_part, "row", axis=1, tiled=True)
        triangles.append(lax.all_gather(gathered, "vec", axis=3, tiled=True).reshape(PANEL, PANEL))
    padded = padded_2(vectors, (("row", 0),), BS)
    product = band_product(intersection, padded, rows_here // BS)
    grouped = product.reshape(rows_here // (CYC * owners), owners, CYC, columns)
    regrouped = lax.all_to_all(grouped, "row", split_axis=1, concat_axis=0, tiled=True).reshape(
        rows_here, columns
    )
    current = jnp.take(regrouped, pivot_rows, axis=0)
    outputs = []
    for panel_num in range(PANELS):
        row_first = panel_num * panel_rows
        row_end = row_first + panel_rows
        col_first = panel_num * PANEL
        col_end = col_first + PANEL
        rhs_local = current[row_first:row_end].reshape(slot_count, 1, CYC, columns)
        rhs_all = lax.all_gather(rhs_local, "row", axis=1, tiled=True)
        triangle = triangles[panel_num]
        block_sol = jax.scipy.linalg.solve_triangular(
            triangle, rhs_all.reshape(PANEL, columns), lower=True, unit_diagonal=True
        )
        update = jnp.dot(
            factor[row_end:, col_first:col_end], block_sol, precision=lax.Precision.HIGHEST
        )
        current = jnp.concatenate([current[:row_end], current[row_end:] - update], axis=0)
        scaled = scale_pivots(
            block_sol,
            pivot_sizes[col_first // 2 : col_end // 2],
            pivot_diag[col_first:col_end],
            pivot_off[col_first // 2 : col_end // 2],
        )
        own_rows = lax.dynamic_slice_in_dim(
            scaled.reshape(slot_count, owners, CYC, columns), device, 1, 1
        )
        outputs.append(own_rows.reshape(panel_rows, columns))
    outputs.append(current[PANELS * panel_rows :])
    return jnp.concatenate(outputs, axis=0)


def solution(mesh):
    in_specs = (
        P(("cuts", "row"), "vec"),
        P("row", None),
        P(("cuts", "row"), None),
        P(("cuts", "row")),
        P("cuts"),
        P("cuts"),
        P("cuts"),
    )
    out_specs = P(("cuts", "row"), "vec")
    owners, shares = mesh.shape["row"], mesh.shape["vec"]
    few = owners == 4 and shares == 4 and DIAG == owners * shares * CYC
    body = local if few else local_many
    return jax.shard_map(body, mesh=mesh, in_specs=in_specs, out_specs=out_specs, check_vma=False)
```

```python
import functools

import jax
import jax.numpy as jnp
from jax import lax
from jax.experimental import pallas as pl
from jax.experimental.pallas import tpu as pltpu
from jax.sharding import PartitionSpec as P

BS = 512
PANEL = 1024
PANELS = 2
CYC = 16
DIAG = 256
HALF = 128
MIB = 1024 * 1024
HEAVY = 2**37
LIGHT = 2**30
F32 = jnp.float32
BF16 = jnp.bfloat16


def params(mib):
    return pltpu.CompilerParams(vmem_limit_bytes=mib * MIB)


IN_VMEM = pl.BlockSpec(memory_space=pltpu.VMEM)
IN_SMEM = pl.BlockSpec(memory_space=pltpu.SMEM)
IN_HBM = pl.BlockSpec(memory_space=pltpu.HBM)


def shaped(*shape, dtype=F32):
    return jax.ShapeDtypeStruct(shape, dtype)


def cost(flops, moved):
    return pl.CostEstimate(flops=int(flops), bytes_accessed=int(moved), transcendentals=0)


def split(value):
    high = value.astype(BF16)
    low = (value - high.astype(F32)).astype(BF16)
    return high, low


def side_by_side(value):
    return jnp.concatenate(split(value), axis=1)


def dot(left, right):
    return jnp.dot(left, right, preferred_element_type=F32)


def fold(wide):
    width = wide.shape[1] // 2
    return wide[:, :width] + wide[:, width:]


def times(left, right_wide):
    high, low = split(left)
    return parts_times(high, low, right_wide)


def parts_times(high, low, right_wide):
    return fold(dot(high, right_wide)) + dot(low, right_wide[:, : right_wide.shape[1] // 2])


def small_times(left_wide, right):
    wide = side_by_side(right)
    return fold(dot(left_wide, jnp.concatenate([wide, wide], axis=0)))


def fold_back(run, part, shares):
    return part if run % 2 == 0 else shares - 1 - part


def lower_run(pair, part, shares):
    early = part < shares // 2
    return 2 * pair + jnp.where(early, 1, 0), jnp.where(early, shares - 1 - part, part)


def start_kernel(slots, shares, place_ref, factor_ref, vec_ref, share_ref, first_ref, last_ref, sems):
    part = place_ref[1]
    rows = vec_ref.shape[0]
    copies = [(vec_ref.at[pl.ds(rows - BS, BS)], last_ref), (vec_ref.at[pl.ds(0, BS)], first_ref)]
    runs = PANEL // DIAG

    def source(panel, run, block, column, width):
        row = pl.multiple_of((panel * slots + run * shares + block) * CYC, CYC)
        column = pl.multiple_of(panel * PANEL + column, HALF)
        return factor_ref.at[pl.ds(row, CYC), pl.ds(column, width)]

    for panel in range(PANELS):
        for run in range(runs):
            width = (2 * run + 1) * HALF
            target = share_ref.at[panel, :, pl.ds(run * run * HALF, width)]
            copies.append((source(panel, run, fold_back(run, part, shares), 0, width), target))
        for pair in range(runs // 2):
            run, block = lower_run(pair, part, shares)
            target = share_ref.at[panel, :, pl.ds((runs * runs + pair) * HALF, HALF)]
            copies.append((source(panel, run, block, (2 * run + 1) * HALF, HALF), target))
    started = [pltpu.make_async_copy(a, b, sems.at[i]) for i, (a, b) in enumerate(copies)]
    for copy in started:
        copy.start()
    for copy in started:
        copy.wait()


def first_sends(place, factor, vectors, slots, shares):
    runs = PANEL // DIAG
    edge = shaped(BS, vectors.shape[1])
    return pl.pallas_call(
        functools.partial(start_kernel, slots, shares),
        out_shape=[shaped(PANELS, CYC, (runs * runs + runs // 2) * HALF), edge, edge],
        in_specs=[IN_SMEM, IN_HBM, IN_HBM],
        out_specs=[IN_VMEM, IN_HBM, IN_HBM],
        scratch_shapes=[pltpu.SemaphoreType.DMA((PANELS * (runs + runs // 2) + 2,))],
        compiler_params=params(4),
        cost_estimate=cost(0, 4 * MIB),
        name="first_sends",
    )(place, factor, vectors)


def band_kernel(inter_ref, vec_ref, after_ref, before_ref, out_ref, wide_ref):
    tile = pl.program_id(0)
    rows = vec_ref.shape[0]
    tile_rows = inter_ref.shape[0]
    owners = out_ref.shape[0]

    @pl.when(tile == 0)
    def _():
        wide_ref[:BS] = side_by_side(before_ref[...])
        wide_ref[BS : BS + rows] = side_by_side(vec_ref[...])
        wide_ref[BS + rows :] = side_by_side(after_ref[...])

    window = wide_ref[pl.ds(pl.multiple_of(tile * BS, BS), 3 * BS)]
    product = times(inter_ref[...], window)
    groups = tile_rows // (owners * CYC)
    for g in range(groups):
        for owner in range(owners):
            first = (g * owners + owner) * CYC
            out_ref[owner, g * CYC : (g + 1) * CYC] = product[first : first + CYC]


def band_product_split(intersection, vectors, halo, owners):
    rows, columns = vectors.shape
    width = intersection.shape[1]
    tile_rows = BS
    slot_rows = tile_rows // owners
    whole = lambda t: (0, 0)
    return pl.pallas_call(
        band_kernel,
        out_shape=shaped(owners, rows // owners, columns),
        grid=(rows // tile_rows,),
        in_specs=[
            pl.BlockSpec((tile_rows, width), lambda t: (t, 0)),
            pl.BlockSpec((rows, columns), whole),
            pl.BlockSpec((BS, columns), whole),
            pl.BlockSpec((BS, columns), whole),
        ],
        out_specs=pl.BlockSpec((owners, slot_rows, columns), lambda t: (0, t, 0)),
        scratch_shapes=[pltpu.VMEM((rows + 2 * BS, 2 * columns), BF16)],
        compiler_params=params(16),
        cost_estimate=cost(8 * rows * width * columns, 4 * rows * width),
        name="band_product_split",
    )(intersection, vectors, *halo)


def pass_kernel(value_ref, after_ref, out_ref):
    pass


def pass_on(value, after):
    anywhere = pl.BlockSpec(memory_space=pl.ANY)
    return pl.pallas_call(
        pass_kernel,
        out_shape=shaped(*value.shape),
        in_specs=[anywhere, anywhere],
        out_specs=anywhere,
        input_output_aliases={0: 0},
        compiler_params=params(1),
        name="pass_on",
    )(value, after)


def from_others(value, after):
    end = lax.axis_size("row") - 1
    middle = [(i, end - i) for i in range(1, end)]
    across = pass_on(swap_with(value, "row", 2), after)
    near, inner = swap_with(value, "row", 1), lax.ppermute(value, "row", middle)
    outer = lax.ppermute(across, "row", [(i, i ^ 1) for i, _ in middle])
    return near, across, inner, outer


def stack_kernel(place_ref, near_ref, across_ref, inner_ref, outer_ref, after_ref, *out_refs):
    me = place_ref[0]
    end = out_refs[0].shape[0]
    for panel, out_ref in enumerate(out_refs):
        out_ref[0] = near_ref[panel]
        out_ref[1] = across_ref[panel]

    @pl.when((me > 0) & (me < end))
    def _():
        for panel, out_ref in enumerate(out_refs):
            out_ref[2] = inner_ref[panel]

    @pl.when((me == 0) | (me == end))
    def _():
        for panel, out_ref in enumerate(out_refs):
            out_ref[2] = outer_ref[panel]


def stack(place, pieces, after):
    return pl.pallas_call(
        stack_kernel,
        out_shape=[shaped(3, *pieces[0].shape[1:])] * PANELS,
        in_specs=[IN_SMEM] + [IN_VMEM] * 4 + [pl.BlockSpec(memory_space=pl.ANY)],
        out_specs=[IN_VMEM] * PANELS,
        compiler_params=params(4),
        name="stack",
    )(place, *pieces, after)


def invert_kernel(panel, owners, shares, place_ref, after_ref, own_ref, *refs):
    pieces = refs[:shares]
    high_ref, low_ref, inv_high_ref, inv_low_ref, near_ref = refs[shares:]
    runs = PANEL // DIAG
    me, part = place_ref[0], place_ref[1]

    def place_left(run, row_block, values):
        if run:
            rows = pl.ds(pl.multiple_of(row_block * CYC, CYC), CYC)
            high_ref[rows, : run * DIAG], low_ref[rows, : run * DIAG] = split(values)

    for run in range(runs):
        for s in range(shares):
            row_block = (run * shares + s) * owners + me
            rows = slice((run * shares + s) * CYC, (run * shares + s + 1) * CYC)
            place_left(run, row_block, own_ref[panel, rows, : run * DIAG])
            near_ref[row_block] = own_ref[panel, rows, run * DIAG : (run + 1) * DIAG]
    for other in range(1, owners):
        owner = me ^ other
        for turn in range(shares):
            piece = pieces[turn]
            sender = part ^ turn
            for run in range(runs):
                row_block = (run * shares + fold_back(run, sender, shares)) * owners + owner
                first = run * run * HALF
                middle = first + run * DIAG
                place_left(run, row_block, piece[other - 1, :, first:middle])
                near_ref[row_block, :, :HALF] = piece[other - 1, :, middle : middle + HALF]
            for pair in range(runs // 2):
                run, block = lower_run(pair, sender, shares)
                first = (runs * runs + pair) * HALF
                near_ref[(run * shares + block) * owners + owner, :, HALF:] = piece[
                    other - 1, :, first : first + HALF
                ]

    def near(i, side):
        blocks = HALF // CYC
        return near_ref[i * blocks : (i + 1) * blocks, :, side * HALF : (side + 1) * HALF].reshape(HALF, HALF)

    down = lax.broadcasted_iota(jnp.int32, (HALF, HALF), 0)
    along = lax.broadcasted_iota(jnp.int32, (HALF, HALF), 1)
    eye = jnp.where(down == along, 1.0, 0.0).astype(F32)

    def below(size):
        return (down // size == along // size + 1) & ((down // size) % 2 == 1)

    count = PANEL // HALF
    diagonal = [near(i, i % 2) for i in range(count)]
    wides = [side_by_side(d) for d in diagonal]
    inverse = [eye - jnp.where(below(1), d, 0.0) for d in diagonal]
    size = 2
    while size < HALF:
        keep = jnp.where(below(size), 1.0, 0.0).astype(BF16)
        keep = jnp.concatenate([keep, keep], axis=1)
        right = [small_times(wides[i] * keep, inverse[i]) for i in range(count)]
        inverse = [inverse[i] - small_times(side_by_side(inverse[i]), right[i]) for i in range(count)]
        size *= 2
    for run in range(runs):
        first, second = inverse[2 * run], inverse[2 * run + 1]
        right = small_times(side_by_side(near(2 * run + 1, 0)), first)
        corner = -small_times(side_by_side(second), right)
        inv_high_ref[run, :HALF, :HALF], inv_low_ref[run, :HALF, :HALF] = split(first)
        inv_high_ref[run, HALF:, HALF:], inv_low_ref[run, HALF:, HALF:] = split(second)
        inv_high_ref[run, HALF:, :HALF], inv_low_ref[run, HALF:, :HALF] = split(corner)
        empty = jnp.zeros((HALF, HALF), BF16)
        inv_high_ref[run, :HALF, HALF:] = empty
        inv_low_ref[run, :HALF, HALF:] = empty


def invert_panel(panel, place, own, pieces, owners, shares, after, flops):
    groups = PANEL // DIAG
    return pl.pallas_call(
        functools.partial(invert_kernel, panel, owners, shares),
        out_shape=[shaped(PANEL, PANEL, dtype=BF16)] * 2 + [shaped(groups, DIAG, DIAG, dtype=BF16)] * 2,
        in_specs=[IN_SMEM, pl.BlockSpec(memory_space=pl.ANY)] + [IN_VMEM] * (len(pieces) + 1),
        out_specs=[IN_VMEM] * 4,
        scratch_shapes=[
            pltpu.VMEM((PANEL // CYC, CYC, DIAG), F32),
        ],
        compiler_params=params(16),
        cost_estimate=cost(flops, 12 * MIB),
        name="invert_panel",
    )(place, after, own, *pieces)


def order_kernel(first, pivot_ref, grouped_ref, after_ref, *out_refs):
    for out_ref in out_refs:
        pick_rows(pivot_ref, first, grouped_ref, out_ref)
        first += out_ref.shape[0]


def pick_rows(pivot_ref, first, source_ref, target_ref):
    step = 8

    def body(i, _):
        base = i * step
        rows = [source_ref[pl.ds(pivot_ref[first + base + j], 1)] for j in range(step)]
        target_ref[pl.ds(pl.multiple_of(base, step), step)] = jnp.concatenate(rows, axis=0)
        return 0

    lax.fori_loop(0, target_ref.shape[0] // step, body, 0, unroll=4)


def order_rows(first, counts, pivot_rows, grouped, after):
    return pl.pallas_call(
        functools.partial(order_kernel, first),
        out_shape=[shaped(count, grouped.shape[1]) for count in counts],
        in_specs=[IN_SMEM, IN_VMEM, pl.BlockSpec(memory_space=pl.ANY)],
        out_specs=[IN_VMEM] * len(counts),
        compiler_params=params(4),
        cost_estimate=cost(0, 2 * MIB),
        name="order_rows",
    )(pivot_rows, grouped, after)


def solve_into(me, owners, pieces, high_ref, low_ref, inv_high_ref, inv_low_ref, rhs_ref, y_ref, use):
    slots = pieces[0].shape[0] // CYC
    columns = pieces[0].shape[1]
    for piece, distance in zip(pieces, (0, *far_first(owners))):
        for s in range(slots):
            rhs_ref[s * owners + (me ^ distance)] = piece[s * CYC : (s + 1) * CYC]
    runs = [slice(k * DIAG, (k + 1) * DIAG) for k in range(PANEL // DIAG)]
    rhs = [rhs_ref[r.start // CYC : r.stop // CYC].reshape(DIAG, columns) for r in runs]

    def take_off(row, k, wide):
        rhs[row] = rhs[row] - parts_times(high_ref[runs[row], runs[k]], low_ref[runs[row], runs[k]], wide)

    wide = None
    for k in range(len(runs)):
        block = parts_times(inv_high_ref[k], inv_low_ref[k], side_by_side(rhs[k]))
        if k:
            for row in range(k + 1, len(runs)):
                take_off(row, k - 1, wide)
            use(k - 1, wide)
        wide = side_by_side(block)
        if k + 1 < len(runs):
            take_off(k + 1, k, wide)
        y_ref[runs[k].start // CYC : runs[k].stop // CYC] = block.reshape(DIAG // CYC, CYC, columns)
    use(len(runs) - 1, wide)


def first_kernel(owners, place_ref, *refs):
    pieces = refs[:owners]
    high, low, inv_high, inv_low, left_ref, current_ref, y_ref, next_ref, rhs_ref = refs[owners:]
    next_ref[...] = current_ref[...]

    def use(k, wide):
        columns = slice(k * DIAG, (k + 1) * DIAG)
        next_ref[...] -= parts_times(left_ref[0, :, columns], left_ref[1, :, columns], wide)

    solve_into(place_ref[0], owners, pieces, high, low, inv_high, inv_low, rhs_ref, y_ref, use)


def first_solve(place, pieces, prepared, left, current):
    owners = len(pieces)
    panel_rows, columns = current.shape
    return pl.pallas_call(
        functools.partial(first_kernel, owners),
        out_shape=[shaped(PANEL // CYC, CYC, columns), shaped(panel_rows, columns)],
        in_specs=[IN_SMEM] + [IN_VMEM] * (owners + 6),
        out_specs=[IN_VMEM] * 2,
        scratch_shapes=[pltpu.VMEM((PANEL // CYC, CYC, columns), F32)],
        compiler_params=params(8),
        cost_estimate=cost(HEAVY, 6 * MIB),
        name="first_solve",
    )(place, *pieces, *prepared, left, current)


def pivot_weights(me, sizes, diag, off):
    pairs, lanes = off.shape[1], diag.shape[1]
    spread = lax.broadcasted_iota(jnp.int32, (pairs, lanes), 1) // 2 == lax.broadcasted_iota(
        jnp.int32, (pairs, lanes), 0
    )
    spread = jnp.where(spread, 1.0, 0.0).astype(F32)
    off = jnp.dot(off, spread, precision=lax.Precision.HIGHEST, preferred_element_type=F32)
    sizes = jnp.dot(sizes.astype(F32), spread, precision=lax.Precision.HIGHEST, preferred_element_type=F32)
    odd = lax.broadcasted_iota(jnp.int32, diag.shape, 1) % 2 == 1
    other = jnp.where(odd, pltpu.roll(diag, 1, 1), pltpu.roll(diag, lanes - 1, 1))
    determ = diag * other - off * off
    is_pair = sizes > 1.5
    keep = jnp.where(is_pair, other / determ, 1.0 / diag)
    swap = jnp.where(is_pair, -off / determ, 0.0)
    turned = []
    for weight in (keep, swap):
        weight = pltpu.roll(weight, lax.rem(lanes - CYC * me, lanes), 1)
        tall = jnp.concatenate([weight] * (HALF // weight.shape[0]), axis=0)
        turned.append(tall.T)
    return turned


def mark_kernel(after_ref, out_ref):
    out_ref[...] = jnp.zeros_like(out_ref)


def mark(after):
    return pl.pallas_call(
        mark_kernel,
        out_shape=shaped(8, HALF),
        in_specs=[pl.BlockSpec(memory_space=pl.ANY)],
        out_specs=IN_VMEM,
        compiler_params=params(1),
        cost_estimate=cost(HEAVY, 0),
        name="mark",
    )(after)


def halve_kernel(
    tile_rows, place_ref, factor_ref, sizes_ref, diag_ref, off_ref, after_ref, out_ref, own_ref, next_ref, keep_ref,
    swap_ref, left_ref, below_ref, parts_ref, in_sems, out_sems, own_sems,
):
    tiles = left_ref.shape[0]
    rows = own_ref.shape[1]
    below = pltpu.make_async_copy(factor_ref.at[pl.ds(rows, rows), pl.ds(0, PANEL)], below_ref, own_sems.at[PANELS])
    below.start()
    loads, stores, owns = [], [], []
    for t in range(tiles):
        source = factor_ref.at[pl.ds((t + 1) * tile_rows, tile_rows), pl.ds((PANELS - 1) * PANEL, PANEL)]
        loads.append(pltpu.make_async_copy(source, left_ref.at[t], in_sems.at[t]))
        loads[t].start()
    for panel in range(PANELS):
        source = factor_ref.at[pl.ds(panel * rows, rows), pl.ds(panel * PANEL, PANEL)]
        owns.append(pltpu.make_async_copy(source, own_ref.at[panel], own_sems.at[panel]))
        owns[panel].start()
    keep_ref[...], swap_ref[...] = pivot_weights(place_ref[0], sizes_ref[...], diag_ref[...], off_ref[...])
    below.wait()
    next_ref[0], next_ref[1] = split(below_ref[...])
    for t in range(tiles):
        loads[t].wait()
        parts_ref[t, 0], parts_ref[t, 1] = split(left_ref[t])
        stores.append(pltpu.make_async_copy(parts_ref.at[t], out_ref.at[t], out_sems.at[t]))
        stores[t].start()
    for copy in owns + stores:
        copy.wait()


def halve_last(place, factor, pivots, panel_rows, after):
    tile_rows = PANELS * panel_rows
    tiles = factor.shape[0] // tile_rows - 1
    weight = shaped(pivots[1].shape[1], HALF)
    return pl.pallas_call(
        functools.partial(halve_kernel, tile_rows),
        out_shape=[
            shaped(tiles, 2, tile_rows, PANEL, dtype=BF16),
            shaped(PANELS, panel_rows, PANEL),
            shaped(2, panel_rows, PANEL, dtype=BF16),
            weight,
            weight,
        ],
        in_specs=[IN_SMEM, IN_HBM] + [IN_VMEM] * len(pivots) + [pl.BlockSpec(memory_space=pl.ANY)],
        out_specs=[IN_HBM] + [IN_VMEM] * 4,
        scratch_shapes=[
            pltpu.VMEM((tiles, tile_rows, PANEL), F32),
            pltpu.VMEM((panel_rows, PANEL), F32),
            pltpu.VMEM((tiles, 2, tile_rows, PANEL), BF16),
            pltpu.SemaphoreType.DMA((tiles,)),
            pltpu.SemaphoreType.DMA((tiles,)),
            pltpu.SemaphoreType.DMA((PANELS + 1,)),
        ],
        compiler_params=params(18),
        cost_estimate=cost(LIGHT, 12 * MIB),
        name="halve_last",
    )(place, factor, *pivots, after)


def middle_kernel(tile_rows, factor_ref, rest_ref, y_ref, out_ref, wide_ref, left_ref, sems):
    tiles = left_ref.shape[0]
    loads = []
    for t in range(tiles):
        source = factor_ref.at[pl.ds((t + 1) * tile_rows, tile_rows), pl.ds(0, PANEL)]
        loads.append(pltpu.make_async_copy(source, left_ref.at[t], sems.at[t]))
        loads[t].start()
    wide_ref[...] = side_by_side(y_ref[...].reshape(PANEL, y_ref.shape[2]))
    for t in range(tiles):
        loads[t].wait()
        rows = slice(t * tile_rows, (t + 1) * tile_rows)
        out_ref[rows] = rest_ref[rows] - times(left_ref[t], wide_ref[...])


def middle_update(rest, y, factor, tile_rows):
    rows, columns = rest.shape
    tiles = rows // tile_rows
    return pl.pallas_call(
        functools.partial(middle_kernel, tile_rows),
        out_shape=shaped(rows, columns),
        in_specs=[IN_HBM] + [IN_VMEM] * 2,
        out_specs=IN_VMEM,
        scratch_shapes=[
            pltpu.VMEM((PANEL, 2 * columns), BF16),
            pltpu.VMEM((tiles, tile_rows, PANEL), F32),
            pltpu.SemaphoreType.DMA((tiles,)),
        ],
        compiler_params=params(12),
        cost_estimate=cost(8 * rows * PANEL * columns, 8 * MIB),
        name="middle_update",
    )(factor, rest, y)


def last_kernel(owners, tile_rows, place_ref, left_ref, *refs):
    pieces = refs[:owners]
    high, low, inv_high, inv_low, y_ref, keep_ref, swap_ref, rest_ref = refs[owners : owners + 8]
    out_ref, rhs_ref, second_ref, stage_ref, sems = refs[owners + 8 :]
    me = place_ref[0]
    last = PANEL // DIAG - 1
    stores = []

    def store(t):
        target = out_ref.at[pl.ds(t * tile_rows, tile_rows)]
        stores.append(pltpu.make_async_copy(stage_ref.at[t], target, sems.at[t]))
        stores[-1].start()

    def use(k, wide):
        columns = slice(k * DIAG, (k + 1) * DIAG)
        for t in range(left_ref.shape[0]):
            rows = slice(t * tile_rows, (t + 1) * tile_rows)
            before = stage_ref[t + 1] if k else rest_ref[rows]
            stage_ref[t + 1] = before - parts_times(left_ref[t, 0, :, columns], left_ref[t, 1, :, columns], wide)
            if k == last:
                store(t + 1)

    solve_into(me, owners, pieces, high, low, inv_high, inv_low, rhs_ref, second_ref, use)
    scale_own_rows(me, owners, y_ref, second_ref, keep_ref, swap_ref, stage_ref)
    store(0)
    for copy in stores:
        copy.wait()


def scale_own_rows(me, owners, first_ref, second_ref, keep_ref, swap_ref, stage_ref):
    slots = first_ref.shape[0] // owners
    runs = keep_ref.shape[0] // (owners * CYC)
    for panel, source in enumerate((first_ref, second_ref)):
        for s in range(slots):
            at = panel * slots + s
            rows = source[s * owners + me]
            odd = lax.broadcasted_iota(jnp.int32, rows.shape, 0) % 2 == 1
            other = jnp.where(odd, pltpu.roll(rows, 1, 0), pltpu.roll(rows, CYC - 1, 0))
            first = (at % runs) * owners * CYC
            keep = keep_ref[first : first + CYC, at // runs : at // runs + 1]
            swap = swap_ref[first : first + CYC, at // runs : at // runs + 1]
            mixed = keep * rows + jnp.where(swap != 0, swap * other, 0.0)
            stage_ref[0, at * CYC : (at + 1) * CYC] = mixed


def last_solve(place, parts, pieces, prepared, y, weights, rest, tile_rows):
    owners = len(pieces)
    columns = rest.shape[1]
    rows = rest.shape[0] + tile_rows
    return pl.pallas_call(
        functools.partial(last_kernel, owners, tile_rows),
        out_shape=shaped(rows, columns),
        in_specs=[IN_SMEM] + [IN_VMEM] * (owners + 9),
        out_specs=IN_HBM,
        scratch_shapes=[
            pltpu.VMEM((PANEL // CYC, CYC, columns), F32),
            pltpu.VMEM((PANEL // CYC, CYC, columns), F32),
            pltpu.VMEM((rows // tile_rows, tile_rows, columns), F32),
            pltpu.SemaphoreType.DMA((rows // tile_rows,)),
        ],
        compiler_params=params(16),
        cost_estimate=cost(8 * rows * PANEL * columns, 12 * MIB),
        name="last_solve",
    )(place, parts, *pieces, *prepared, y, *weights, rest)


def swap_with(value, axis, distance):
    size = lax.axis_size(axis)
    return lax.ppermute(value, axis, [(i, i ^ distance) for i in range(size)])


def far_first(owners):
    return [*range(2, owners), 1]


def from_all(value, axis):
    return [value] + [swap_with(value, axis, k) for k in far_first(lax.axis_size(axis))]


def local(vectors, intersection, factor, pivot_rows, pivot_sizes, pivot_diag, pivot_off):
    owners, shares = lax.axis_size("row"), lax.axis_size("vec")
    slots = PANEL // owners // CYC
    panel_rows = slots * CYC
    place = jnp.stack([lax.axis_index("row"), lax.axis_index("vec")]).astype(jnp.int32)
    vectors, intersection, factor = (
        pltpu.with_memory_space_constraint(a, pltpu.HBM) for a in (vectors, intersection, factor)
    )

    share, first, last = first_sends(place, factor, vectors, slots, shares)
    up = [(i, i + 1) for i in range(owners - 1)]
    down = [(j, i) for i, j in up]
    halo = lax.ppermute(first, "row", down), lax.ppermute(last, "row", up)
    product = band_product_split(intersection, vectors, halo, owners)
    grouped = lax.all_to_all(product, "row", 0, 0, tiled=True).reshape(vectors.shape)

    def share_out(stacked, after):
        across = pass_on(swap_with(stacked, "vec", 2), after)
        return stacked, swap_with(stacked, "vec", 1), across, swap_with(across, "vec", 1)

    tile_rows = PANELS * panel_rows
    pivots = [a.reshape(pivot_diag.shape[0] // DIAG, -1) for a in (pivot_sizes, pivot_diag, pivot_off)]
    started = mark(product)
    direct = from_others(share, started)
    (first,) = order_rows(0, [panel_rows], pivot_rows, grouped, place)
    parts, own, left, keep, swap = halve_last(place, factor, pivots, panel_rows, started)
    stacked = stack(place, direct, own)
    shared = share_out(stacked[0], first)
    prepared = invert_panel(0, place, own, shared, owners, shares, first, HEAVY)
    rest_rows = factor.shape[0] - tile_rows
    second, rest = order_rows(panel_rows, [tile_rows - panel_rows, rest_rows], pivot_rows, grouped, prepared[2])
    later = share_out(stacked[1], second)
    pieces = from_all(first, "row")
    y, second = first_solve(place, pieces, prepared, left, second)
    pieces = from_all(second, "row")
    rest = middle_update(rest, y, factor, tile_rows)
    prepared = invert_panel(1, place, own, later, owners, shares, y, LIGHT)
    return last_solve(place, parts, pieces, prepared, y, (keep, swap), rest, tile_rows)


def padded_2(shard, sides, width):
    for axis, dim in sides:
        devices, length = (lax.axis_size(axis), shard.shape[dim])
        up = [(i, (i + 1) % devices) for i in range(devices - 1)]
        down = [(j, i) for i, j in up]
        last = lax.slice_in_dim(shard, length - width, length, axis=dim)
        leading = lax.slice_in_dim(shard, 0, width, axis=dim)
        before = lax.ppermute(last, axis, up)
        after = lax.ppermute(leading, axis, down)
        shard = jnp.concatenate([before, shard, after], axis=dim)
    return shard


def band_product(intersection, padded, blocks_here):
    band_width = intersection.shape[1] // 3
    band_rows = intersection.reshape(blocks_here, band_width, 3 * band_width)
    result = jnp.zeros((blocks_here, band_width, padded.shape[1]), jnp.float32)
    for offset in range(3):
        window = padded[offset * band_width : offset * band_width + blocks_here * band_width]
        window = window.reshape(blocks_here, band_width, padded.shape[1])
        result = result + jnp.einsum(
            "kij,kjv->kiv",
            band_rows[:, :, offset * band_width : (offset + 1) * band_width],
            window,
            precision=lax.Precision.HIGHEST,
        )
    return result.reshape(blocks_here * band_width, padded.shape[1])


def scale_pivots(values, sizes_here, diag_here, off_here):
    paired = values.reshape(-1, 2, values.shape[1])
    leading = paired[:, 0]
    trailing = paired[:, 1]
    diag_lead = diag_here[0::2][:, None]
    diag_next = diag_here[1::2][:, None]
    coupling = off_here[:, None]
    determ = diag_lead * diag_next - coupling * coupling
    is_pair = (sizes_here == 2)[:, None]
    new_lead = jnp.where(
        is_pair, (diag_next * leading - coupling * trailing) / determ, leading / diag_lead
    )
    new_next = jnp.where(
        is_pair, (diag_lead * trailing - coupling * leading) / determ, trailing / diag_next
    )
    return jnp.stack([new_lead, new_next], axis=1).reshape(values.shape)


def local_many(vectors, intersection, factor, pivot_rows, pivot_sizes, pivot_diag, pivot_off):
    owners = lax.axis_size("row")
    device = lax.axis_index("row")
    rows_here = vectors.shape[0]
    columns = vectors.shape[1]
    slot_count = PANEL // owners // CYC
    panel_rows = slot_count * CYC
    triangles = []
    quarter = PANEL // lax.axis_size("vec")
    column_idx = lax.axis_index("vec")
    for panel_num in range(PANELS):
        local_rows = factor[panel_num * panel_rows : (panel_num + 1) * panel_rows]
        column_part = lax.dynamic_slice_in_dim(
            local_rows, panel_num * PANEL + column_idx * quarter, quarter, 1
        )
        column_part = column_part.reshape(slot_count, 1, CYC, quarter)
        gathered = lax.all_gather(column_part, "row", axis=1, tiled=True)
        triangles.append(lax.all_gather(gathered, "vec", axis=3, tiled=True).reshape(PANEL, PANEL))
    padded = padded_2(vectors, (("row", 0),), BS)
    product = band_product(intersection, padded, rows_here // BS)
    grouped = product.reshape(rows_here // (CYC * owners), owners, CYC, columns)
    regrouped = lax.all_to_all(grouped, "row", split_axis=1, concat_axis=0, tiled=True).reshape(
        rows_here, columns
    )
    current = jnp.take(regrouped, pivot_rows, axis=0)
    outputs = []
    for panel_num in range(PANELS):
        row_first = panel_num * panel_rows
        row_end = row_first + panel_rows
        col_first = panel_num * PANEL
        col_end = col_first + PANEL
        rhs_local = current[row_first:row_end].reshape(slot_count, 1, CYC, columns)
        rhs_all = lax.all_gather(rhs_local, "row", axis=1, tiled=True)
        triangle = triangles[panel_num]
        block_sol = jax.scipy.linalg.solve_triangular(
            triangle, rhs_all.reshape(PANEL, columns), lower=True, unit_diagonal=True
        )
        update = jnp.dot(
            factor[row_end:, col_first:col_end], block_sol, precision=lax.Precision.HIGHEST
        )
        current = jnp.concatenate([current[:row_end], current[row_end:] - update], axis=0)
        scaled = scale_pivots(
            block_sol,
            pivot_sizes[col_first // 2 : col_end // 2],
            pivot_diag[col_first:col_end],
            pivot_off[col_first // 2 : col_end // 2],
        )
        own_rows = lax.dynamic_slice_in_dim(
            scaled.reshape(slot_count, owners, CYC, columns), device, 1, 1
        )
        outputs.append(own_rows.reshape(panel_rows, columns))
    outputs.append(current[PANELS * panel_rows :])
    return jnp.concatenate(outputs, axis=0)


def solution(mesh):
    in_specs = (
        P(("cuts", "row"), "vec"),
        P("row", None),
        P(("cuts", "row"), None),
        P(("cuts", "row")),
        P("cuts"),
        P("cuts"),
        P("cuts"),
    )
    out_specs = P(("cuts", "row"), "vec")
    owners, shares = mesh.shape["row"], mesh.shape["vec"]
    few = owners == 4 and shares == 4 and DIAG == owners * shares * CYC
    body = local if few else local_many
    return jax.shard_map(body, mesh=mesh, in_specs=in_specs, out_specs=out_specs, check_vma=False)
```
